32 devices in a mesh: row: 8 (over y, x, core), col: 4 (over z).
Axes of the slice: x: 2, y: 2, z: 4, core: 2. Of those that a mesh axis runs over, the one named last changes fastest.
Arguments:
- batch: float32 [4096, 1024], P(('row', 'col')), may hold values from -5 to 5, as said below
- running: float32 [4096, 1000], P(('row', 'col')), may hold values from -6 to 6
- targets: float32 [4096, 1000], P(('row', 'col')), may hold values from -6 to 6
- centers: float32 [2048, 1024], P('row'), may hold values from -5 to 5, as said below
- weights: float32 [2048, 1000], P('row'), may hold values from -0.5 to 0.5
Outputs:
- gradient: float32 [2048, 1000], P('row')
- residual: float32 [4096, 1000], P(('row', 'col'))
The draws below stay inside these ranges and needn't reach their ends.
Inputs may be any that keep to these rules, and one draw needn't show every extreme that they name: Each row of batch is an independent vector of 1024 features times its own positive row scale. Each row of centers is an independent vector of 1024 features times its own positive row scale.
All inputs are finite; a program needn't handle non-finite values.
Results may differ from the reference program's by a relative error of at most 0.0001.
Values sent between devices are 32-bit elements; how exact they have to be, the bound alone decides.
No kernel may reach another device: no remote copies, remote signals or barrier semaphores. Data moves between devices by JAX's collectives and lax.ppermute only.
A program may use at most 64 MiB of HBM per device.

```python
import math
import jax
import jax.numpy as jnp
from jax import lax

F = 1024
OUT = 1000
B_DEV = 128
CENT = 2048
BATCH = 4096
DEVICES = 32


def scaled_rows(key, rows):
    key_scale, key_value = jax.random.split(jax.random.fold_in(key, 17))
    scales = jnp.exp(jax.random.uniform(key_scale, (rows, 1), jnp.float32, math.log(0.1), 0.0))
    values = jnp.clip(jax.random.normal(key_value, (rows, F), jnp.float32), -5.0, 5.0)
    return (scales * values).astype(jnp.float32)


def draw_batch(key, part):
    return scaled_rows(key, BATCH)


def draw_centers(key, part):
    return scaled_rows(key, CENT)


def block_scale(stream_key, extent, pieces, least, high):
    def one(dim, shards_of):
        draws = jax.random.uniform(jax.random.fold_in(jax.random.fold_in(stream_key, 6), dim), (shards_of,), jnp.float32, least / len(pieces), high / len(pieces))
        return jnp.repeat(jnp.exp(draws), extent[dim] // shards_of).reshape((-1,) + (1,) * (len(extent) - dim - 1))

    gain = one(*pieces[0])
    for cut in pieces[1:]:
        gain = gain * one(*cut)
    return gain


def centred(stream_key, dims, deviation, most, cuts=(), kind=jnp.bfloat16):
    drawn = deviation * jax.random.normal(stream_key, dims, jnp.float32)
    if cuts:
        drawn = drawn * block_scale(stream_key, dims, cuts, -0.22, 0.18)
    return jnp.clip(drawn, -most, most).astype(kind)


def setup_inputs(seed: int = 0) -> dict:
    arg_keys = jax.random.split(jax.random.key(seed), 6)
    return {
        "batch": draw_batch(jax.random.fold_in(arg_keys[5], 71), 0),
        "running": centred(arg_keys[1], (BATCH, OUT), 1.0, 6.0, ((0, 32),), jnp.float32),
        "targets": centred(arg_keys[2], (BATCH, OUT), 1.0, 6.0, ((0, 32),), jnp.float32),
        "centers": draw_centers(jax.random.fold_in(arg_keys[5], 71), 0),
        "weights": centred(arg_keys[4], (CENT, OUT), (CENT // 16) ** -0.5, 0.5, ((0, 8),), jnp.float32),
    }


def reference(batch, running, targets, centers, weights):
    length_scale = math.sqrt(F) / 4.0
    center_sq = lax.optimization_barrier(jnp.sum(centers * centers, axis=1))
    batch_blocks = batch.reshape(DEVICES, B_DEV, F)
    running_blocks = running.reshape(DEVICES, B_DEV, OUT)
    target_blocks = targets.reshape(DEVICES, B_DEV, OUT)

    def absorb_rows(accum, blocks):
        batch_rows, running_rows, target_rows = blocks
        row_sq = lax.optimization_barrier(jnp.sum(batch_rows * batch_rows, axis=1, keepdims=True))
        crossed = lax.dot_general(batch_rows, centers, (((1,), (1,)), ((), ())), precision=lax.Precision.HIGHEST, preferred_element_type=jnp.float32)
        dist_sq = row_sq + center_sq[None, :] - 2.0 * crossed
        kernel = jnp.exp(-jnp.sqrt(dist_sq + 1.0) / length_scale)
        predicted = running_rows + jnp.dot(kernel, weights, precision=lax.Precision.HIGHEST, preferred_element_type=jnp.float32)
        residual = predicted - target_rows
        accum = accum + lax.dot_general(kernel, residual, (((0,), (0,)), ((), ())), precision=lax.Precision.HIGHEST, preferred_element_type=jnp.float32)
        return (accum, residual)
    initial = jnp.zeros((CENT, OUT), jnp.float32)
    accum, residual = lax.scan(absorb_rows, initial, (batch_blocks, running_blocks, target_blocks))
    gradient = accum / jnp.sqrt(jnp.float32(BATCH))
    return (gradient, residual.reshape(BATCH, OUT))
```

```python
import math

import jax
import jax.numpy as jnp
from jax import lax
from jax.sharding import PartitionSpec as P

HIGHEST = lax.Precision.HIGHEST
HIGH = lax.Precision.HIGH
PIECES = 2


def dot(a, b, dims, precision):
    return lax.dot_general(
        a, b, (dims, ((), ())), precision=precision, preferred_element_type=jnp.float32
    )


def swap_row(value, owners, flip):
    return lax.ppermute(value, "row", [(i, i ^ flip) for i in range(owners)])


def sum_col(value, depth):
    if depth != 4:
        return lax.psum(value, "col")
    inner = value + lax.ppermute(value, "col", [(0, 1), (3, 2)])
    total = inner + lax.ppermute(inner, "col", [(1, 2), (2, 1)])
    back = lax.ppermute(total, "col", [(1, 0), (2, 3)])
    place = lax.axis_index("col")
    return jnp.where((place == 0) | (place == 3), back, total)


def cuts(size, pieces):
    step = -(-size // pieces // 8) * 8
    edges = list(range(0, size, step)) + [size]
    return list(zip(edges[:-1], edges[1:]))


def per_device(batch, running, targets, centers, weights):
    rows_here, feature_count = batch.shape
    owners = lax.axis_size("row")
    depth = lax.axis_size("col")
    chips = owners // 2
    length_scale = math.sqrt(feature_count) / 4.0
    factor = 1.0 / math.sqrt(rows_here * owners * depth)

    blocks = [batch] + [swap_row(batch, owners, 2 * j) for j in range(1, chips)]
    cent = jnp.concatenate([centers, swap_row(centers, owners, 1)], axis=0)
    weights_t = weights.T
    weight = jnp.concatenate([weights_t, swap_row(weights_t, owners, 1)], axis=1)
    cent_sq = jnp.sum(cent * cent, axis=1)

    kernels = []
    for block in blocks:
        crossed = dot(block, cent, ((1,), (1,)), HIGHEST)
        row_sq = jnp.sum(block * block, axis=1, keepdims=True)
        dist_sq = row_sq + cent_sq[None, :] - 2.0 * crossed
        kernels.append(jnp.exp(-jnp.sqrt(dist_sq + 1.0) / length_scale))

    running_t, targets_t = running.T, targets.T
    residuals, gradients = [], []
    for low, high in cuts(weights.shape[1], PIECES):
        piece = weight[low:high]
        predicted = running_t[low:high] + dot(piece, kernels[0], ((1,), (1,)), HIGH)
        for j in range(1, chips):
            share = dot(piece, kernels[j], ((1,), (1,)), HIGH)
            predicted = predicted + swap_row(share, owners, 2 * j)
        residual = predicted - targets_t[low:high]
        residuals.append(residual)
        gradient = dot(residual, kernels[0], ((1,), (0,)), HIGH)
        for j in range(1, chips):
            moved = swap_row(residual, owners, 2 * j)
            gradient = gradient + dot(moved, kernels[j], ((1,), (0,)), HIGH)
        half = centers.shape[0]
        owned = gradient[:, :half] + swap_row(gradient[:, half:], owners, 1)
        gradients.append(sum_col(owned * factor, depth))
    return (
        jnp.concatenate(gradients, axis=0).T,
        jnp.concatenate(residuals, axis=0).T,
    )


def solution(mesh):
    return jax.shard_map(
        per_device,
        mesh=mesh,
        in_specs=(
            P(("row", "col"), None),
            P(("row", "col"), None),
            P(("row", "col"), None),
            P("row", None),
            P("row", None),
        ),
        out_specs=(P("row", None), P(("row", "col"), None)),
        check_vma=False,
    )
```

```python
import math

import jax
import jax.numpy as jnp
from jax import lax
from jax.sharding import Mesh, PartitionSpec as P

HIGHEST = lax.Precision.HIGHEST
HIGH = lax.Precision.HIGH
PIECES = 2


def dot(a, b, dims, precision):
    return lax.dot_general(
        a, b, (dims, ((), ())), precision=precision, preferred_element_type=jnp.float32
    )


def swap_core(value):
    return lax.ppermute(value, "core", [(0, 1), (1, 0)])


def sum_col(value, depth):
    if depth != 4:
        return lax.psum(value, "col")
    inner = value + lax.ppermute(value, "col", [(0, 1), (3, 2)])
    total = inner + lax.ppermute(inner, "col", [(1, 2), (2, 1)])
    back = lax.ppermute(total, "col", [(1, 0), (2, 3)])
    place = lax.axis_index("col")
    return jnp.where((place == 0) | (place == 3), back, total)


def cuts(size, pieces):
    step = -(-size // pieces // 8) * 8
    edges = list(range(0, size, step)) + [size]
    return list(zip(edges[:-1], edges[1:]))


def per_device(batch, running, targets, centers, weights):
    rows_here, feature_count = batch.shape
    chips = lax.axis_size("chip")
    depth = lax.axis_size("col")
    length_scale = math.sqrt(feature_count) / 4.0
    factor = 1.0 / math.sqrt(rows_here * chips * 2 * depth)

    rows = lax.all_gather(batch, "chip", axis=0, tiled=True)
    cent = jnp.concatenate([centers, swap_core(centers)], axis=0)
    weights_t = weights.T
    weight = jnp.concatenate([weights_t, swap_core(weights_t)], axis=1)
    cent_sq = jnp.sum(cent * cent, axis=1)

    crossed = dot(rows, cent, ((1,), (1,)), HIGHEST)
    row_sq = jnp.sum(rows * rows, axis=1, keepdims=True)
    dist_sq = row_sq + cent_sq[None, :] - 2.0 * crossed
    kernel = jnp.exp(-jnp.sqrt(dist_sq + 1.0) / length_scale)

    running_t, targets_t = running.T, targets.T
    residuals, gradients = [], []
    for low, high in cuts(weights.shape[1], PIECES):
        shares = dot(weight[low:high], kernel, ((1,), (1,)), HIGH)
        shares = shares.reshape(high - low, chips, rows_here).transpose(1, 0, 2)
        predicted = running_t[low:high] + lax.psum_scatter(
            shares, "chip", scatter_dimension=0, tiled=False
        )
        residual = predicted - targets_t[low:high]
        residuals.append(residual)
        moved = lax.all_gather(residual, "chip", axis=0, tiled=False)
        moved = moved.transpose(1, 0, 2).reshape(high - low, chips * rows_here)
        gradient = dot(moved, kernel, ((1,), (0,)), HIGH)
        half = centers.shape[0]
        owned = gradient[:, :half] + swap_core(gradient[:, half:])
        gradients.append(sum_col(owned * factor, depth))
    return (
        jnp.concatenate(gradients, axis=0).T,
        jnp.concatenate(residuals, axis=0).T,
    )


def solution(mesh):
    owners, depth = mesh.shape["row"], mesh.shape["col"]
    split = Mesh(mesh.devices.reshape(owners // 2, 2, depth), ("chip", "core", "col"))
    everywhere = P(("chip", "core", "col"), None)
    owned = P(("chip", "core"), None)
    return jax.shard_map(
        per_device,
        mesh=split,
        in_specs=(everywhere, everywhere, everywhere, owned, owned),
        out_specs=(owned, everywhere),
        check_vma=False,
    )
```

```python
import math

import jax
import jax.numpy as jnp
from jax import lax
from jax.sharding import Mesh, PartitionSpec as P

HIGHEST = lax.Precision.HIGHEST
HIGH = lax.Precision.HIGH
ROUNDS = (400, 352, 248)


def dot(a, b, dims, precision):
    return lax.dot_general(
        a, b, (dims, ((), ())), precision=precision, preferred_element_type=jnp.float32
    )


def swap(value, axis, flip=1):
    size = lax.axis_size(axis)
    return lax.ppermute(value, axis, [(i, i ^ flip) for i in range(size)])


def after(value, *earlier):
    return lax.optimization_barrier((value,) + earlier)[0]


def sum_col(value):
    if lax.axis_size("col") != 4:
        return lax.psum(value, "col")
    inner = value + lax.ppermute(value, "col", [(0, 1), (3, 2)])
    total = inner + lax.ppermute(inner, "col", [(1, 2), (2, 1)])
    back = lax.ppermute(total, "col", [(1, 0), (2, 3)])
    place = lax.axis_index("col")
    return jnp.where((place == 0) | (place == 3), back, total)


def kernel_of(rows, cent, cent_sq):
    length_scale = math.sqrt(rows.shape[1]) / 4.0
    crossed = dot(rows, cent, ((1,), (1,)), HIGHEST)
    row_sq = jnp.sum(rows * rows, axis=1, keepdims=True)
    dist_sq = row_sq + cent_sq[None, :] - 2.0 * crossed
    return jnp.exp(-jnp.sqrt(dist_sq + 1.0) / length_scale)


def any_plane(batch, start_t, cent, cent_sq, weight):
    rows_here, chips = batch.shape[0], lax.axis_size("chip")
    rows = lax.all_gather(batch, "chip", axis=0, tiled=True)
    kernel = kernel_of(rows, cent, cent_sq)
    shares = dot(weight, kernel, ((1,), (1,)), HIGH)
    shares = shares.reshape(weight.shape[0], chips, rows_here).transpose(1, 0, 2)
    residual = start_t + lax.psum_scatter(shares, "chip", scatter_dimension=0, tiled=False)
    moved = lax.all_gather(residual, "chip", axis=0, tiled=False)
    moved = moved.transpose(1, 0, 2).reshape(weight.shape[0], chips * rows_here)
    gradient = dot(moved, kernel, ((1,), (0,)), HIGH)
    half = cent.shape[0] // 2
    owned = gradient[:, :half] + swap(gradient[:, half:], "core")
    return sum_col(owned), residual


def square(batch, start_t, cent, cent_sq, weight):
    rows, half, out = batch.shape[0], cent.shape[0] // 2, weight.shape[0]
    block_x = swap(batch, "chip", 1)
    block_y = swap(batch, "chip", 2)
    own = kernel_of(batch, cent, cent_sq)
    low = swap(after(block_x[: rows // 2], own), "chip", 2)
    high = swap(after(block_y[rows // 2 :], own), "chip", 1)
    side_x = kernel_of(block_x, cent, cent_sq)
    side_y = kernel_of(block_y, cent, cent_sq)
    far = kernel_of(jnp.concatenate([low, high], axis=0), cent, cent_sq)
    stay = (jnp.concatenate([own, side_y]), jnp.concatenate([own, side_x]))
    goes = (jnp.concatenate([side_x, far]), jnp.concatenate([side_y, far]))

    edges, at = [], 0
    for size in ROUNDS:
        size = min(size, out - at)
        middle = at + -(-size // 2 // 8) * 8
        edges.append(((at, middle), (middle, at + size)))
        at += size

    def shares(r):
        return [dot(weight[a:b], goes[i], ((1,), (1,)), HIGH) for i, (a, b) in enumerate(edges[r])]

    def begin(r):
        kept = []
        for i, (a, b) in enumerate(edges[r]):
            base = jnp.pad(start_t[a:b], ((0, 0), (0, rows)))
            kept.append(dot(weight[a:b], stay[i], ((1,), (1,)), HIGH) + base)
        return kept

    def turned(pair):
        return jnp.concatenate([pair[:, rows:], pair[:, :rows]], axis=1)

    axes = ((1, 2), (2, 1))
    gradients, residuals = [], []
    sent = shares(0)
    coming = [swap(sent[i], "chip", axes[i][0]) for i in (0, 1)]
    for r in range(len(edges)):
        partial = [k + c for k, c in zip(begin(r), coming)]
        full = [partial[i] + turned(swap(partial[i], "chip", axes[i][1])) for i in (0, 1)]
        if r + 1 < len(edges):
            sent = after(tuple(shares(r + 1)), *partial)
            coming = [swap(sent[i], "chip", axes[i][0]) for i in (0, 1)]
        residuals += [f[:, :rows] for f in full]
        if r:
            full = after(tuple(full), gone)
        other = [swap(full[i], "chip", axes[i][0]) for i in (0, 1)]
        if r:
            other = after(tuple(other), owned)
        gone, here = [
            jnp.concatenate(
                [
                    dot(full[i], stay[i][:, cols], ((1,), (0,)), HIGH)
                    + dot(other[i], goes[i][:, cols], ((1,), (0,)), HIGH)
                    for i in (0, 1)
                ]
            )
            for cols in (slice(half, None), slice(0, half))
        ]
        owned = here + swap(gone, "core")
        gradients.append(sum_col(owned))
    return jnp.concatenate(gradients), jnp.concatenate(residuals)


def per_device(batch, running, targets, centers, weights):
    chips, depth = lax.axis_size("chip"), lax.axis_size("col")
    factor = 1.0 / math.sqrt(batch.shape[0] * chips * 2 * depth)
    cent = jnp.concatenate([centers, swap(centers, "core")], axis=0)
    cent_sq = jnp.sum(cent * cent, axis=1)
    weights_t = weights.T
    weight = jnp.concatenate([weights_t, swap(weights_t, "core")], axis=1)
    plane = square if chips == 4 else any_plane
    gradient, residual = plane(batch, (running - targets).T, cent, cent_sq, weight)
    return (gradient * factor).T, residual.T


def solution(mesh):
    owners, depth = mesh.shape["row"], mesh.shape["col"]
    split = Mesh(mesh.devices.reshape(owners // 2, 2, depth), ("chip", "core", "col"))
    everywhere = P(("chip", "core", "col"), None)
    owned = P(("chip", "core"), None)
    return jax.shard_map(
        per_device,
        mesh=split,
        in_specs=(everywhere, everywhere, everywhere, owned, owned),
        out_specs=(owned, everywhere),
        check_vma=False,
    )
```

```python
import functools
import math

import jax
import jax.numpy as jnp
from jax import lax
from jax.experimental import pallas as pl
from jax.experimental.pallas import tpu as pltpu
from jax.sharding import Mesh, PartitionSpec as P

HIGHEST = lax.Precision.HIGHEST
HIGH = lax.Precision.HIGH
ROUNDS = (0.32, 0.32, 0.24)
BF16, F32 = jnp.bfloat16, jnp.float32
NT = (((1,), (1,)), ((), ()))
NN = (((1,), (0,)), ((), ()))


def swap(value, axis, flip=1):
    size = lax.axis_size(axis)
    return lax.ppermute(value, axis, [(i, i ^ flip) for i in range(size)])


class Line:
    def __init__(self):
        self.last = None

    def hold(self, args):
        if self.last is None:
            return args
        return lax.optimization_barrier((args, self.last))[0]

    def __call__(self, step, *args):
        out = step(*self.hold(args))
        self.last = jax.tree.leaves(out)[0]
        return out


def halves(value):
    high = value.astype(BF16)
    return high, (value - high.astype(F32)).astype(BF16)


def mul(a, b, dims):
    return lax.dot_general(a, b, dims, preferred_element_type=F32)


def mul3(a, b, dims):
    return mul(a[0], b[0], dims) + (mul(a[0], b[1], dims) + mul(a[1], b[0], dims))


def call(body, outs, args, flops=0, scratch=(), aliases=None):
    moved = sum(x.size * x.dtype.itemsize for x in (*args, *outs))
    vmem = pl.BlockSpec(memory_space=pltpu.VMEM)
    return pl.pallas_call(
        body,
        out_shape=outs,
        in_specs=[vmem] * len(args),
        out_specs=[vmem] * len(outs),
        scratch_shapes=list(scratch),
        input_output_aliases=aliases or {},
        cost_estimate=pl.CostEstimate(flops=flops, bytes_accessed=moved, transcendentals=0),
        compiler_params=pltpu.CompilerParams(vmem_limit_bytes=40 * 2**20),
    )(*args)


def shaped(shape, dtype=F32):
    return jax.ShapeDtypeStruct(shape, dtype)


def cent_body(mine_ref, theirs_ref, high_ref, low_ref, sq_ref):
    half = mine_ref.shape[0]
    for i, ref in enumerate((mine_ref, theirs_ref)):
        for at in range(0, half, 128):
            to = pl.ds(i * half + at, 128)
            value = ref[pl.ds(at, 128)]
            high_ref[to], low_ref[to] = halves(value)
            total = jnp.sum(value * value, axis=1, keepdims=True)
            sq_ref[:, to] = jnp.broadcast_to(total, (128, 128)).T[:8]


def split_cent(mine, theirs):
    half, width = mine.shape
    pair = [shaped((2 * half, width), BF16)] * 2
    return call(cent_body, pair + [shaped((8, 2 * half))], (mine, theirs))


def kernel_rows(high, low, row_sq, cent_refs, put):
    cent_high, cent_low, cent_sq = cent_refs
    scale = -4.0 / math.sqrt(cent_high.shape[1])
    for at in range(0, cent_high.shape[0], 256):
        to = pl.ds(at, 256)
        ch, cl = cent_high[to], cent_low[to]
        crossed = mul(high, ch, NT) + (mul(high, cl, NT) + mul(low, ch, NT) + mul(low, cl, NT))
        dist_sq = row_sq + cent_sq[0:1, to] - 2.0 * crossed
        put(to, halves(jnp.exp(jnp.sqrt(dist_sq + 1.0) * scale)))


def fill(refs, high_ref, low_ref, sq_ref):
    at = 0
    for ref in refs:
        to = pl.ds(at, ref.shape[0])
        value = ref[...]
        high_ref[to], low_ref[to] = halves(value)
        sq_ref[to] = jnp.broadcast_to(jnp.sum(value * value, axis=1, keepdims=True), (ref.shape[0], 128))
        at += ref.shape[0]


def near_body(x0, x1, own, y0, y1, c_high, c_low, c_sq, near_high, near_low, high, low, row_sq):
    fill((x0, x1, own, y0, y1), high, low, row_sq)

    def put(to, pair):
        near_high[:, to], near_low[:, to] = pair

    kernel_rows(high[...], low[...], row_sq[:, 0:1], (c_high, c_low, c_sq), put)


def near_kernels(x0, x1, own, y0, y1, cent):
    rows, width = own.shape
    total, wide = 3 * rows, cent[0].shape[0]
    return call(
        near_body,
        [shaped((total, wide), BF16)] * 2,
        (x0, x1, own, y0, y1, *cent),
        flops=8 * total * wide * width,
        scratch=[pltpu.VMEM((total, width), BF16)] * 2 + [pltpu.VMEM((total, 128), F32)],
    )


def share(w_refs, cols, k_refs, rows):
    half = w_refs[0].shape[1]
    total = None
    for i, ref in enumerate(w_refs):
        kept = pl.ds(i * half, half)
        part = mul3(halves(ref[cols]), (k_refs[0][rows, kept], k_refs[1][rows, kept]), NT)
        total = part if total is None else total + part
    return total


def stays(rows):
    return pl.ds(rows, 2 * rows), pl.ds(0, 2 * rows)


def goes(rows):
    return pl.ds(0, 2 * rows), pl.ds(rows, 2 * rows)


def keep_body(edges, rows, w0, w1, running, targets, near_high, near_low, *kept):
    for i, (a, b) in enumerate(edges):
        cols = pl.ds(a, b - a)
        value = share((w0, w1), cols, (near_high, near_low), stays(rows)[i % 2])
        own = slice(0, rows) if i % 2 == 0 else slice(rows, 2 * rows)
        other = slice(rows, 2 * rows) if i % 2 == 0 else slice(0, rows)
        kept[i][:, own] = value[:, own] + (running[cols] - targets[cols])
        kept[i][:, other] = value[:, other]


def keep_shares(edges, w0, w1, running, targets, near):
    rows = running.shape[1]
    outs = [shaped((b - a, 2 * rows)) for a, b in edges]
    flops = 12 * rows * near[0].shape[1] * w0.shape[0]
    return call(
        functools.partial(keep_body, edges, rows), outs, (w0, w1, running, targets, *near), flops
    )


def far_body(edges, low_rows, high_rows, c_high, c_low, c_sq, near_high, near_low, w0, w1, *rest):
    outs, (high, low, row_sq) = rest[:-3], rest[-3:]
    far_high, far_low, sent = outs[0], outs[1], outs[2:]
    rows = low.shape[0]
    fill((low_rows, high_rows), high, low, row_sq)
    for far, near in ((far_high, near_high), (far_low, near_low)):
        far[pl.ds(0, rows)] = near[pl.ds(0, rows)]
        far[pl.ds(2 * rows, rows)] = near[pl.ds(2 * rows, rows)]

    def put(to, pair):
        far_high[pl.ds(rows, rows), to], far_low[pl.ds(rows, rows), to] = pair

    kernel_rows(high[...], low[...], row_sq[:, 0:1], (c_high, c_low, c_sq), put)
    for i, (a, b) in enumerate(edges):
        sent[i][...] = share((w0, w1), pl.ds(a, b - a), (far_high, far_low), goes(rows)[i % 2])


def far_kernels(edges, low, high, cent, near, w0, w1):
    rows, width = 2 * low.shape[0], low.shape[1]
    wide = cent[0].shape[0]
    outs = [shaped(near[0].shape, BF16)] * 2 + [shaped((b - a, 2 * rows)) for a, b in edges]
    out = call(
        functools.partial(far_body, edges),
        outs,
        (low, high, *cent, *near, w0, w1),
        flops=8 * rows * wide * width,
        scratch=[pltpu.VMEM((rows, width), BF16)] * 2 + [pltpu.VMEM((rows, 128), F32)],
    )
    return out[:2], out[2:]


def send_body(edges, rows, w0, w1, far_high, far_low, *sent):
    for i, (a, b) in enumerate(edges):
        sent[i][...] = share((w0, w1), pl.ds(a, b - a), (far_high, far_low), goes(rows)[i % 2])


def send_shares(edges, w0, w1, far):
    rows = far[0].shape[0] // 3
    outs = [shaped((b - a, 2 * rows)) for a, b in edges]
    flops = sum(12 * rows * far[0].shape[1] * (b - a) for a, b in edges)
    return call(functools.partial(send_body, edges, rows), outs, (w0, w1, *far), flops)


def grad_body(factor, full_a, full_b, other_a, other_b, near_high, near_low, far_high, far_low, gone, here):
    rows, half = full_a.shape[1] // 2, gone.shape[1]
    at = 0
    for i, (full, other) in enumerate(((full_a, other_a), (full_b, other_b))):
        to = pl.ds(at, full.shape[0])
        at += full.shape[0]
        full_pair, other_pair = halves(full[...]), halves(other[...])
        stay, go = stays(rows)[i], goes(rows)[i]
        for out, cols in ((gone, pl.ds(half, half)), (here, pl.ds(0, half))):
            out[to] = factor * (
                mul3(full_pair, (near_high[stay, cols], near_low[stay, cols]), NN)
                + mul3(other_pair, (far_high[go, cols], far_low[go, cols]), NN)
            )


def grad_parts(factor, full, other, near, far):
    cols, half = full[0].shape[0] + full[1].shape[0], near[0].shape[1] // 2
    flops = 12 * cols * full[0].shape[1] * 2 * half
    outs = [shaped((cols, half))] * 2
    return call(functools.partial(grad_body, factor), outs, (*full, *other, *near, *far), flops)


def line_of_four(value, hop):
    pairs = ([(0, 1), (3, 2)], [(1, 2), (2, 1)], [(1, 0), (2, 3)])[hop]
    return lax.ppermute(value, "col", pairs)


def add(a, b):
    return a + b


def cut(out):
    edges, at = [], 0
    for part in ROUNDS + (1.0,):
        left = out - at
        both = left if part == 1.0 else min(left, round(out * part / 16) * 16)
        first = -(-both // 16) * 8
        edges += [(at, at + first), (at + first, at + both)]
        at += both
    return edges


def square(batch, running_t, targets_t, centers, weights_t, factor):
    rows, out = batch.shape[0], weights_t.shape[0]
    mid = rows // 2
    edges = cut(out)
    line = Line()
    x0 = swap(batch[:mid], "chip", 1)
    y1 = swap(batch[mid:], "chip", 2)
    x1 = swap(batch[mid:], "chip", 1)
    y0 = swap(batch[:mid], "chip", 2)
    cent_theirs = swap(centers, "core")
    cent = line(split_cent, centers, cent_theirs)
    w0 = weights_t
    w1 = swap(lax.optimization_barrier((weights_t, x0, y1, cent[0]))[0], "core")
    low = swap(x0, "chip", 2)
    high = swap(y1, "chip", 1)
    near = line(near_kernels, x0, x1, batch, y0, y1, cent)
    kept = line(lambda *a: keep_shares(edges, *a), w0, w1, running_t, targets_t, near)
    far, sent = line(lambda *a: far_kernels(edges[:4], *a), low, high, cent, near, w0, w1)

    axes = ((1, 2), (2, 1))

    def both(pair, step):
        return [swap(pair[i], "chip", axes[i][step]) for i in (0, 1)]

    def turned(a, b):
        return a + jnp.concatenate([b[:, rows:], b[:, :rows]], axis=1)

    rounds = len(edges) // 2
    coming, full, other, owned = [None] * rounds, [None] * rounds, [None] * rounds, [None] * rounds
    gone, here, inner, total, back = ([None] * rounds for _ in range(5))
    partial, crossing = [None] * rounds, [None] * rounds

    def do_partial(r):
        partial[r] = [line(add, kept[2 * r + i], coming[r][i]) for i in (0, 1)]
        crossing[r] = both(partial[r], 1)

    def do_full(r):
        full[r] = [line(turned, partial[r][i], crossing[r][i]) for i in (0, 1)]
        other[r] = both(full[r], 0)

    def do_grad(r):
        gone[r], here[r] = line(lambda *a: grad_parts(factor, *a), full[r], other[r], near, far)
        gone[r] = swap(gone[r], "core")

    def do_owned(r):
        owned[r] = line(add, here[r], gone[r])
        inner[r] = line_of_four(owned[r], 0)

    def do_inner(r):
        inner[r] = line(add, owned[r], inner[r])
        total[r] = line_of_four(inner[r], 1)

    def do_total(r):
        total[r] = line(add, inner[r], total[r])
        back[r] = line_of_four(total[r], 2)

    coming[0] = both(sent[0:2], 0)
    coming[1] = both(line.hold(tuple(sent[2:4])), 0)
    sent = list(sent) + list(line(lambda *a: send_shares(edges[4:], *a), w0, w1, far))
    do_partial(0)
    do_partial(1)
    do_full(0)
    coming[2] = both(line.hold(tuple(sent[4:6])), 0)
    do_full(1)
    do_grad(0)
    do_partial(2)
    coming[3] = both(line.hold(tuple(sent[6:8])), 0)
    do_owned(0)
    do_grad(1)
    do_full(2)
    do_owned(1)
    do_partial(3)
    do_inner(0)
    do_grad(2)
    do_full(3)
    do_owned(2)
    do_inner(1)
    do_total(0)
    do_grad(3)
    do_owned(3)
    do_inner(2)
    do_total(1)
    do_inner(3)
    do_total(2)
    do_total(3)

    place = lax.axis_index("col")
    ends = (place == 0) | (place == 3)
    gradient = jnp.concatenate([jnp.where(ends, b, t) for b, t in zip(back, total)])
    own = (slice(0, rows), slice(rows, None))
    residual = jnp.concatenate([f[i][:, own[i]] for f in full for i in (0, 1)])
    return gradient, residual


def any_plane(batch, running_t, targets_t, centers, weights_t, factor):
    def dot(a, b, dims, precision):
        return lax.dot_general(a, b, dims, precision=precision, preferred_element_type=F32)

    rows_here, chips = batch.shape[0], lax.axis_size("chip")
    half, out = centers.shape[0], weights_t.shape[0]
    cent = jnp.concatenate([centers, swap(centers, "core")], axis=0)
    weight = jnp.concatenate([weights_t, swap(weights_t, "core")], axis=1)
    rows = lax.all_gather(batch, "chip", axis=0, tiled=True)
    row_sq = jnp.sum(rows * rows, axis=1, keepdims=True)
    dist_sq = row_sq + jnp.sum(cent * cent, axis=1)[None, :] - 2.0 * dot(rows, cent, NT, HIGHEST)
    kernel = jnp.exp(-jnp.sqrt(dist_sq + 1.0) / (math.sqrt(rows.shape[1]) / 4.0))
    shares = dot(weight, kernel, NT, HIGH).reshape(out, chips, rows_here).transpose(1, 0, 2)
    residual = running_t - targets_t + lax.psum_scatter(shares, "chip", scatter_dimension=0, tiled=False)
    moved = lax.all_gather(residual, "chip", axis=0, tiled=False)
    moved = moved.transpose(1, 0, 2).reshape(out, chips * rows_here)
    gradient = dot(moved, kernel, NN, HIGH) * factor
    owned = gradient[:, :half] + swap(gradient[:, half:], "core")
    return lax.psum(owned, "col"), residual


def per_device(batch, running, targets, centers, weights):
    chips, depth = lax.axis_size("chip"), lax.axis_size("col")
    factor = 1.0 / math.sqrt(batch.shape[0] * chips * 2 * depth)
    plane = square if (chips, depth) == (4, 4) else any_plane
    gradient, residual = plane(batch, running.T, targets.T, centers, weights.T, factor)
    return gradient.T, residual.T


def solution(mesh):
    owners, depth = mesh.shape["row"], mesh.shape["col"]
    split = Mesh(mesh.devices.reshape(owners // 2, 2, depth), ("chip", "core", "col"))
    everywhere = P(("chip", "core", "col"), None)
    owned = P(("chip", "core"), None)
    return jax.shard_map(
        per_device,
        mesh=split,
        in_specs=(everywhere, everywhere, everywhere, owned, owned),
        out_specs=(owned, everywhere),
        check_vma=False,
    )
```

```python
import functools
import math

import jax
import jax.numpy as jnp
from jax import lax
from jax.experimental import pallas as pl
from jax.experimental.pallas import tpu as pltpu
from jax.sharding import Mesh, PartitionSpec as P

HIGHEST = lax.Precision.HIGHEST
HIGH = lax.Precision.HIGH
ROUNDS = (0.52,)
BF16, F32 = jnp.bfloat16, jnp.float32
NT = (((1,), (1,)), ((), ()))
NN = (((1,), (0,)), ((), ()))


def swap(value, axis, flip=1):
    size = lax.axis_size(axis)
    return lax.ppermute(value, axis, [(i, i ^ flip) for i in range(size)])


class Line:
    def __init__(self):
        self.last = None

    def hold(self, args):
        if self.last is None:
            return args
        return lax.optimization_barrier((args, self.last))[0]

    def __call__(self, step, *args):
        out = step(*self.hold(args))
        self.last = jax.tree.leaves(out)[0]
        return out


def halves(value):
    high = value.astype(BF16)
    return high, (value - high.astype(F32)).astype(BF16)


def mul(a, b, dims):
    return lax.dot_general(a, b, dims, preferred_element_type=F32)


def mul3(a, b, dims):
    return mul(a[0], b[0], dims) + (mul(a[0], b[1], dims) + mul(a[1], b[0], dims))


def call(body, outs, args, flops=0, scratch=(), aliases=None):
    vmem = pl.BlockSpec(memory_space=pltpu.VMEM)
    return pl.pallas_call(
        body,
        out_shape=outs,
        in_specs=[vmem] * len(args),
        out_specs=[vmem] * len(outs),
        scratch_shapes=list(scratch),
        input_output_aliases=aliases or {},
        cost_estimate=pl.CostEstimate(flops=flops // 2**20, bytes_accessed=0, transcendentals=0),
        compiler_params=pltpu.CompilerParams(vmem_limit_bytes=40 * 2**20),
    )(*args)


def shaped(shape, dtype=F32):
    return jax.ShapeDtypeStruct(shape, dtype)


def cent_body(mine_ref, theirs_ref, high_ref, low_ref, sq_ref):
    half = mine_ref.shape[0]
    for i, ref in enumerate((mine_ref, theirs_ref)):
        for at in range(0, half, 128):
            to = pl.ds(i * half + at, 128)
            value = ref[pl.ds(at, 128)]
            high_ref[to], low_ref[to] = halves(value)
            total = jnp.sum(value * value, axis=1, keepdims=True)
            sq_ref[:, to] = jnp.broadcast_to(total, (128, 128)).T[:8]


def split_cent(mine, theirs):
    half, width = mine.shape
    pair = [shaped((2 * half, width), BF16)] * 2
    return call(cent_body, pair + [shaped((8, 2 * half))], (mine, theirs))


def kernel_rows(high, low, row_sq, cent_refs, put):
    cent_high, cent_low, cent_sq = cent_refs
    scale = -4.0 / math.sqrt(cent_high.shape[1])
    for at in range(0, cent_high.shape[0], 256):
        to = pl.ds(at, 256)
        ch, cl = cent_high[to], cent_low[to]
        crossed = mul(high, ch, NT) + (mul(high, cl, NT) + mul(low, ch, NT) + mul(low, cl, NT))
        dist_sq = row_sq + cent_sq[0:1, to] - 2.0 * crossed
        put(to, halves(jnp.exp(jnp.sqrt(dist_sq + 1.0) * scale)))


def fill(refs, high_ref, low_ref, sq_ref):
    at = 0
    for ref in refs:
        to = pl.ds(at, ref.shape[0])
        value = ref[...]
        high_ref[to], low_ref[to] = halves(value)
        sq_ref[to] = jnp.broadcast_to(jnp.sum(value * value, axis=1, keepdims=True), (ref.shape[0], 128))
        at += ref.shape[0]


def own_body(own, c_high, c_low, c_sq, own_high, own_low, high, low, row_sq):
    fill((own,), high, low, row_sq)

    def put(to, pair):
        own_high[:, to], own_low[:, to] = pair

    kernel_rows(high[...], low[...], row_sq[:, 0:1], (c_high, c_low, c_sq), put)


def row_scratch(rows, width):
    return [pltpu.VMEM((rows, width), BF16)] * 2 + [pltpu.VMEM((rows, 128), F32)]


def own_kernels(own, cent):
    rows, width = own.shape
    wide = cent[0].shape[0]
    return call(
        own_body,
        [shaped((rows, wide), BF16)] * 2,
        (own, *cent),
        flops=8 * rows * wide * width,
        scratch=row_scratch(rows, width),
    )


def near_body(x, y, c_high, c_low, c_sq, own_high, own_low, near_high, near_low, high, low, row_sq):
    rows = x.shape[0]
    fill((x, y), high, low, row_sq)
    near_high[pl.ds(rows, rows)] = own_high[...]
    near_low[pl.ds(rows, rows)] = own_low[...]

    def put(to, pair):
        for ref, value in zip((near_high, near_low), pair):
            ref[pl.ds(0, rows), to] = value[:rows]
            ref[pl.ds(2 * rows, rows), to] = value[rows:]

    kernel_rows(high[...], low[...], row_sq[:, 0:1], (c_high, c_low, c_sq), put)


def near_kernels(x, y, cent, own):
    rows, width = x.shape
    wide = cent[0].shape[0]
    return call(
        near_body,
        [shaped((3 * rows, wide), BF16)] * 2,
        (x, y, *cent, *own),
        flops=16 * rows * wide * width,
        scratch=row_scratch(2 * rows, width),
    )


def share(w_refs, cols, k_refs, rows):
    half = w_refs[0].shape[1]
    total = None
    for i, ref in enumerate(w_refs):
        kept = pl.ds(i * half, half)
        part = mul3(halves(ref[cols]), (k_refs[0][rows, kept], k_refs[1][rows, kept]), NT)
        total = part if total is None else total + part
    return total


def stays(rows):
    return pl.ds(rows, 2 * rows), pl.ds(0, 2 * rows)


def goes(rows):
    return pl.ds(0, 2 * rows), pl.ds(rows, 2 * rows)


def keep_body(edges, rows, w0, w1, running, targets, near_high, near_low, *kept):
    for i, (a, b) in enumerate(edges):
        cols = pl.ds(a, b - a)
        value = share((w0, w1), cols, (near_high, near_low), stays(rows)[i % 2])
        own = slice(0, rows) if i % 2 == 0 else slice(rows, 2 * rows)
        other = slice(rows, 2 * rows) if i % 2 == 0 else slice(0, rows)
        kept[i][:, own] = value[:, own] + (running[cols] - targets[cols])
        kept[i][:, other] = value[:, other]


def keep_shares(edges, w0, w1, running, targets, near):
    rows = running.shape[1]
    outs = [shaped((b - a, 2 * rows)) for a, b in edges]
    flops = 12 * rows * near[0].shape[1] * w0.shape[0]
    return call(
        functools.partial(keep_body, edges, rows), outs, (w0, w1, running, targets, *near), flops
    )


def far_body(edges, low_rows, high_rows, c_high, c_low, c_sq, near_high, near_low, w0, w1, *rest):
    outs, (high, low, row_sq) = rest[:-3], rest[-3:]
    far_high, far_low, sent = outs[0], outs[1], outs[2:]
    rows = low.shape[0]
    fill((low_rows, high_rows), high, low, row_sq)
    for far, near in ((far_high, near_high), (far_low, near_low)):
        far[pl.ds(0, rows)] = near[pl.ds(0, rows)]
        far[pl.ds(2 * rows, rows)] = near[pl.ds(2 * rows, rows)]

    def put(to, pair):
        far_high[pl.ds(rows, rows), to], far_low[pl.ds(rows, rows), to] = pair

    kernel_rows(high[...], low[...], row_sq[:, 0:1], (c_high, c_low, c_sq), put)
    for i, (a, b) in enumerate(edges):
        sent[i][...] = share((w0, w1), pl.ds(a, b - a), (far_high, far_low), goes(rows)[i % 2])


def far_kernels(edges, low, high, cent, near, w0, w1):
    rows, width = 2 * low.shape[0], low.shape[1]
    wide = cent[0].shape[0]
    outs = [shaped(near[0].shape, BF16)] * 2 + [shaped((b - a, 2 * rows)) for a, b in edges]
    out = call(
        functools.partial(far_body, edges),
        outs,
        (low, high, *cent, *near, w0, w1),
        flops=8 * rows * wide * width,
        scratch=row_scratch(rows, width),
    )
    return out[:2], out[2:]


def send_body(edges, rows, w0, w1, far_high, far_low, *sent):
    for i, (a, b) in enumerate(edges):
        sent[i][...] = share((w0, w1), pl.ds(a, b - a), (far_high, far_low), goes(rows)[i % 2])


def send_shares(edges, w0, w1, far):
    rows = far[0].shape[0] // 3
    outs = [shaped((b - a, 2 * rows)) for a, b in edges]
    flops = sum(12 * rows * far[0].shape[1] * (b - a) for a, b in edges)
    return call(functools.partial(send_body, edges, rows), outs, (w0, w1, *far), flops)


def grad_body(factor, full_a, full_b, other_a, other_b, near_high, near_low, far_high, far_low, gone, here):
    rows, half = full_a.shape[1] // 2, gone.shape[1]
    at = 0
    for i, (full, other) in enumerate(((full_a, other_a), (full_b, other_b))):
        to = pl.ds(at, full.shape[0])
        at += full.shape[0]
        full_pair, other_pair = halves(full[...]), halves(other[...])
        stay, go = stays(rows)[i], goes(rows)[i]
        for out, cols in ((gone, pl.ds(half, half)), (here, pl.ds(0, half))):
            out[to] = factor * (
                mul3(full_pair, (near_high[stay, cols], near_low[stay, cols]), NN)
                + mul3(other_pair, (far_high[go, cols], far_low[go, cols]), NN)
            )


def grad_parts(factor, full, other, near, far):
    cols, half = full[0].shape[0] + full[1].shape[0], near[0].shape[1] // 2
    flops = 12 * cols * full[0].shape[1] * 2 * half
    outs = [shaped((cols, half))] * 2
    return call(functools.partial(grad_body, factor), outs, (*full, *other, *near, *far), flops)


def pass_line(value, pairs):
    return lax.ppermute(value, "col", pairs)


BESIDE = [(0, 1), (1, 0), (2, 3), (3, 2)]
ACROSS = [(0, 3), (3, 0), (1, 2), (2, 1)]


def add(a, b):
    return a + b


def cut(out):
    edges, at = [], 0
    for part in ROUNDS + (1.0,):
        left = out - at
        both = left if part == 1.0 else min(left, round(out * part / 16) * 16)
        first = -(-both // 16) * 8
        edges += [(at, at + first), (at + first, at + both)]
        at += both
    return edges


def square(batch, running_t, targets_t, centers, weights_t, factor):
    rows, out = batch.shape[0], weights_t.shape[0]
    mid, quarter = rows // 2, centers.shape[0] // 2
    edges = cut(out)
    rounds = len(edges) // 2
    line = Line()
    block_x = swap(batch, "chip", 1)
    block_y = swap(batch, "chip", 2)
    cent_theirs = swap(centers, "core")
    w0, w1 = weights_t, swap(weights_t, "core")
    cent = line(split_cent, centers, cent_theirs)
    own = line(own_kernels, batch, cent)
    low = swap(block_x[:mid], "chip", 2)
    high = swap(block_y[mid:], "chip", 1)
    near = line(near_kernels, block_x, block_y, cent, own)
    far, sent = line(lambda *a: far_kernels(edges[:4], *a), low, high, cent, near, w0, w1)

    axes = ((1, 2), (2, 1))
    place = lax.axis_index("col")
    ends = (place == 0) | (place == 3)

    def both(pair, step):
        return [swap(pair[i], "chip", axes[i][step]) for i in (0, 1)]

    def turned(a, b):
        return a + jnp.concatenate([b[:, rows:], b[:, :rows]], axis=1)

    coming, crossing, beside, across, back = ([None] * rounds for _ in range(5))
    partial, full, other, gone, here, mine, total = ([None] * rounds for _ in range(7))

    def do_partial(r):
        partial[r] = [line(add, kept[2 * r + i], coming[r][i]) for i in (0, 1)]
        crossing[r] = both(partial[r], 1)

    def do_full(r):
        full[r] = [line(turned, partial[r][i], crossing[r][i]) for i in (0, 1)]
        other[r] = both(full[r], 0)

    def do_grad(r):
        gone[r], here[r] = line(lambda *a: grad_parts(factor, *a), full[r], other[r], near, far)
        gone[r] = swap(gone[r], "core")

    def split(a, b):
        first, second = a[:, :quarter] + b[:, :quarter], a[:, quarter:] + b[:, quarter:]
        return jnp.where(ends, second, first), jnp.where(ends, first, second)

    def do_owned(r):
        sends, mine[r] = line(split, here[r], gone[r])
        beside[r] = pass_line(sends, BESIDE)

    def do_mine(r):
        mine[r] = line(add, mine[r], beside[r])
        across[r] = pass_line(mine[r], ACROSS)

    def do_total(r):
        total[r] = line(add, mine[r], across[r])
        back[r] = pass_line(total[r], BESIDE)

    coming[0] = both(sent[0:2], 0)
    coming[1] = both(line.hold(tuple(sent[2:4])), 0)
    kept = line(lambda *a: keep_shares(edges, *a), w0, w1, running_t, targets_t, near)
    if rounds == 3:
        sent = list(sent) + list(line(lambda *a: send_shares(edges[4:], *a), w0, w1, far))
    do_partial(0)
    do_partial(1)
    do_full(0)
    if rounds == 3:
        coming[2] = both(line.hold(tuple(sent[4:6])), 0)
    do_full(1)
    do_grad(0)
    do_owned(0)
    if rounds == 3:
        do_partial(2)
    do_grad(1)
    do_owned(1)
    if rounds == 3:
        do_full(2)
    do_mine(0)
    if rounds == 3:
        do_grad(2)
        do_owned(2)
    do_mine(1)
    do_total(0)
    if rounds == 3:
        do_mine(2)
    do_total(1)
    if rounds == 3:
        do_total(2)

    first = [jnp.where(ends, t, b) for t, b in zip(total, back)]
    second = [jnp.where(ends, b, t) for t, b in zip(total, back)]
    gradient = jnp.concatenate([jnp.concatenate(first), jnp.concatenate(second)], axis=1)
    mine_rows = (slice(0, rows), slice(rows, None))
    residual = jnp.concatenate([f[i][:, mine_rows[i]] for f in full for i in (0, 1)])
    return gradient, residual


def any_plane(batch, running_t, targets_t, centers, weights_t, factor):
    def dot(a, b, dims, precision):
        return lax.dot_general(a, b, dims, precision=precision, preferred_element_type=F32)

    rows_here, chips = batch.shape[0], lax.axis_size("chip")
    half, out = centers.shape[0], weights_t.shape[0]
    cent = jnp.concatenate([centers, swap(centers, "core")], axis=0)
    weight = jnp.concatenate([weights_t, swap(weights_t, "core")], axis=1)
    rows = lax.all_gather(batch, "chip", axis=0, tiled=True)
    row_sq = jnp.sum(rows * rows, axis=1, keepdims=True)
    dist_sq = row_sq + jnp.sum(cent * cent, axis=1)[None, :] - 2.0 * dot(rows, cent, NT, HIGHEST)
    kernel = jnp.exp(-jnp.sqrt(dist_sq + 1.0) / (math.sqrt(rows.shape[1]) / 4.0))
    shares = dot(weight, kernel, NT, HIGH).reshape(out, chips, rows_here).transpose(1, 0, 2)
    residual = running_t - targets_t + lax.psum_scatter(shares, "chip", scatter_dimension=0, tiled=False)
    moved = lax.all_gather(residual, "chip", axis=0, tiled=False)
    moved = moved.transpose(1, 0, 2).reshape(out, chips * rows_here)
    gradient = dot(moved, kernel, NN, HIGH) * factor
    owned = gradient[:, :half] + swap(gradient[:, half:], "core")
    return lax.psum(owned, "col"), residual


def per_device(batch, running, targets, centers, weights):
    chips, depth = lax.axis_size("chip"), lax.axis_size("col")
    factor = 1.0 / math.sqrt(batch.shape[0] * chips * 2 * depth)
    plane = square if (chips, depth) == (4, 4) else any_plane
    gradient, residual = plane(batch, running.T, targets.T, centers, weights.T, factor)
    return gradient.T, residual.T


def solution(mesh):
    owners, depth = mesh.shape["row"], mesh.shape["col"]
    split = Mesh(mesh.devices.reshape(owners // 2, 2, depth), ("chip", "core", "col"))
    everywhere = P(("chip", "core", "col"), None)
    owned = P(("chip", "core"), None)
    return jax.shard_map(
        per_device,
        mesh=split,
        in_specs=(everywhere, everywhere, everywhere, owned, owned),
        out_specs=(owned, everywhere),
        check_vma=False,
    )
```

```python
import functools
import math

import jax
import jax.numpy as jnp
from jax import lax
from jax.experimental import pallas as pl
from jax.experimental.pallas import tpu as pltpu
from jax.sharding import Mesh, PartitionSpec as P

HIGHEST = lax.Precision.HIGHEST
HIGH = lax.Precision.HIGH
ROUNDS = (0.48,)
BF16, F32 = jnp.bfloat16, jnp.float32
NT = (((1,), (1,)), ((), ()))
NN = (((1,), (0,)), ((), ()))


def swap(value, axis, flip=1):
    size = lax.axis_size(axis)
    return lax.ppermute(value, axis, [(i, i ^ flip) for i in range(size)])


class Line:
    def __init__(self):
        self.last = None

    def hold(self, args):
        if self.last is None:
            return args
        return lax.optimization_barrier((args, self.last))[0]

    def __call__(self, step, *args):
        out = step(*self.hold(args))
        self.last = jax.tree.leaves(out)[0]
        return out


def halves(value):
    high = value.astype(BF16)
    return high, (value - high.astype(F32)).astype(BF16)


def mul(a, b, dims):
    return lax.dot_general(a, b, dims, preferred_element_type=F32)


def mul3(a, b, dims):
    return mul(a[0], b[0], dims) + (mul(a[0], b[1], dims) + mul(a[1], b[0], dims))


def call(body, outs, args, flops=0, scratch=(), aliases=None):
    vmem = pl.BlockSpec(memory_space=pltpu.VMEM)
    return pl.pallas_call(
        body,
        out_shape=outs,
        in_specs=[vmem] * len(args),
        out_specs=[vmem] * len(outs),
        scratch_shapes=list(scratch),
        input_output_aliases=aliases or {},
        cost_estimate=pl.CostEstimate(flops=flops // 2**20, bytes_accessed=0, transcendentals=0),
        compiler_params=pltpu.CompilerParams(vmem_limit_bytes=40 * 2**20),
    )(*args)


def shaped(shape, dtype=F32):
    return jax.ShapeDtypeStruct(shape, dtype)


def cent_body(mine_ref, theirs_ref, high_ref, low_ref, sq_ref):
    half = mine_ref.shape[0]
    for i, ref in enumerate((mine_ref, theirs_ref)):
        for at in range(0, half, 128):
            to = pl.ds(i * half + at, 128)
            value = ref[pl.ds(at, 128)]
            high_ref[to], low_ref[to] = halves(value)
            total = jnp.sum(value * value, axis=1, keepdims=True)
            sq_ref[:, to] = jnp.broadcast_to(total, (128, 128)).T[:8]


def split_cent(mine, theirs):
    half, width = mine.shape
    pair = [shaped((2 * half, width), BF16)] * 2
    return call(cent_body, pair + [shaped((8, 2 * half))], (mine, theirs))


def kernel_rows(high, low, row_sq, cent_refs, put):
    cent_high, cent_low, cent_sq = cent_refs
    scale = -4.0 / math.sqrt(cent_high.shape[1])
    for at in range(0, cent_high.shape[0], 256):
        to = pl.ds(at, 256)
        ch, cl = cent_high[to], cent_low[to]
        crossed = mul(high, ch, NT) + (mul(high, cl, NT) + mul(low, ch, NT) + mul(low, cl, NT))
        dist_sq = row_sq + cent_sq[0:1, to] - 2.0 * crossed
        put(to, halves(jnp.exp(jnp.sqrt(dist_sq + 1.0) * scale)))


def fill(refs, high_ref, low_ref, sq_ref):
    at = 0
    for ref in refs:
        to = pl.ds(at, ref.shape[0])
        value = ref[...]
        high_ref[to], low_ref[to] = halves(value)
        sq_ref[to] = jnp.broadcast_to(jnp.sum(value * value, axis=1, keepdims=True), (ref.shape[0], 128))
        at += ref.shape[0]


def own_body(own, c_high, c_low, c_sq, own_high, own_low, high, low, row_sq):
    fill((own,), high, low, row_sq)

    def put(to, pair):
        own_high[:, to], own_low[:, to] = pair

    kernel_rows(high[...], low[...], row_sq[:, 0:1], (c_high, c_low, c_sq), put)


def row_scratch(rows, width):
    return [pltpu.VMEM((rows, width), BF16)] * 2 + [pltpu.VMEM((rows, 128), F32)]


def own_kernels(own, cent):
    rows, width = own.shape
    wide = cent[0].shape[0]
    return call(
        own_body,
        [shaped((rows, wide), BF16)] * 2,
        (own, *cent),
        flops=8 * rows * wide * width,
        scratch=row_scratch(rows, width),
    )


def near_body(x, y, c_high, c_low, c_sq, own_high, own_low, near_high, near_low, high, low, row_sq):
    rows = x.shape[0]
    fill((x, y), high, low, row_sq)
    near_high[pl.ds(rows, rows)] = own_high[...]
    near_low[pl.ds(rows, rows)] = own_low[...]

    def put(to, pair):
        for ref, value in zip((near_high, near_low), pair):
            ref[pl.ds(0, rows), to] = value[:rows]
            ref[pl.ds(2 * rows, rows), to] = value[rows:]

    kernel_rows(high[...], low[...], row_sq[:, 0:1], (c_high, c_low, c_sq), put)


def near_kernels(x, y, cent, own):
    rows, width = x.shape
    wide = cent[0].shape[0]
    return call(
        near_body,
        [shaped((3 * rows, wide), BF16)] * 2,
        (x, y, *cent, *own),
        flops=16 * rows * wide * width,
        scratch=row_scratch(2 * rows, width),
    )


def share(w_refs, cols, k_refs, rows):
    half = w_refs[0].shape[1]
    total = None
    for i, ref in enumerate(w_refs):
        kept = pl.ds(i * half, half)
        part = mul3(halves(ref[cols]), (k_refs[0][rows, kept], k_refs[1][rows, kept]), NT)
        total = part if total is None else total + part
    return total


def stays(rows):
    return pl.ds(rows, 2 * rows), pl.ds(0, 2 * rows)


def goes(rows):
    return pl.ds(0, 2 * rows), pl.ds(rows, 2 * rows)


def keep_body(edges, rows, w0, w1, running, targets, near_high, near_low, *kept):
    for i, (a, b) in enumerate(edges):
        cols = pl.ds(a, b - a)
        value = share((w0, w1), cols, (near_high, near_low), stays(rows)[i % 2])
        own = slice(0, rows) if i % 2 == 0 else slice(rows, 2 * rows)
        other = slice(rows, 2 * rows) if i % 2 == 0 else slice(0, rows)
        kept[i][:, own] = value[:, own] + (running[cols] - targets[cols])
        kept[i][:, other] = value[:, other]


def keep_shares(edges, w0, w1, running, targets, near):
    rows = running.shape[1]
    outs = [shaped((b - a, 2 * rows)) for a, b in edges]
    flops = 12 * rows * near[0].shape[1] * w0.shape[0]
    return call(
        functools.partial(keep_body, edges, rows), outs, (w0, w1, running, targets, *near), flops
    )


def far_body(edges, low_rows, high_rows, c_high, c_low, c_sq, near_high, near_low, w0, w1, *rest):
    outs, (high, low, row_sq) = rest[:-3], rest[-3:]
    far_high, far_low, sent = outs[0], outs[1], outs[2:]
    rows = low.shape[0]
    fill((low_rows, high_rows), high, low, row_sq)
    for far, near in ((far_high, near_high), (far_low, near_low)):
        far[pl.ds(0, rows)] = near[pl.ds(0, rows)]
        far[pl.ds(2 * rows, rows)] = near[pl.ds(2 * rows, rows)]

    def put(to, pair):
        far_high[pl.ds(rows, rows), to], far_low[pl.ds(rows, rows), to] = pair

    kernel_rows(high[...], low[...], row_sq[:, 0:1], (c_high, c_low, c_sq), put)
    for i, (a, b) in enumerate(edges):
        sent[i][...] = share((w0, w1), pl.ds(a, b - a), (far_high, far_low), goes(rows)[i % 2])


def far_kernels(edges, low, high, cent, near, w0, w1):
    rows, width = 2 * low.shape[0], low.shape[1]
    wide = cent[0].shape[0]
    outs = [shaped(near[0].shape, BF16)] * 2 + [shaped((b - a, 2 * rows)) for a, b in edges]
    out = call(
        functools.partial(far_body, edges),
        outs,
        (low, high, *cent, *near, w0, w1),
        flops=8 * rows * wide * width,
        scratch=row_scratch(rows, width),
    )
    return out[:2], out[2:]


def send_body(edges, rows, w0, w1, far_high, far_low, *sent):
    for i, (a, b) in enumerate(edges):
        sent[i][...] = share((w0, w1), pl.ds(a, b - a), (far_high, far_low), goes(rows)[i % 2])


def send_shares(edges, w0, w1, far):
    rows = far[0].shape[0] // 3
    outs = [shaped((b - a, 2 * rows)) for a, b in edges]
    flops = sum(12 * rows * far[0].shape[1] * (b - a) for a, b in edges)
    return call(functools.partial(send_body, edges, rows), outs, (w0, w1, *far), flops)


PARTS = 3


def part_rows(size):
    step = -(-size // PARTS // 8) * 8
    return [(at, min(size, at + step)) for at in range(0, size, step)]


def grad_body(factor, full_a, full_b, other_a, other_b, near_high, near_low, far_high, far_low, here, *gone):
    rows, half = full_a.shape[1] // 2, here.shape[1]
    at = 0
    for i, (full, other) in enumerate(((full_a, other_a), (full_b, other_b))):
        to = pl.ds(at, full.shape[0])
        at += full.shape[0]
        full_pair, other_pair = halves(full[...]), halves(other[...])
        stay, go = stays(rows)[i], goes(rows)[i]
        for away, cols in ((True, pl.ds(half, half)), (False, pl.ds(0, half))):
            value = factor * (
                mul3(full_pair, (near_high[stay, cols], near_low[stay, cols]), NN)
                + mul3(other_pair, (far_high[go, cols], far_low[go, cols]), NN)
            )
            if not away:
                here[to] = value
                continue
            start, end = at - full.shape[0], at
            for ref, (low, high) in zip(gone, part_rows(here.shape[0])):
                low_at, high_at = max(low, start), min(high, end)
                if low_at < high_at:
                    ref[pl.ds(low_at - low, high_at - low_at)] = value[low_at - start : high_at - start]


def grad_parts(factor, full, other, near, far):
    cols, half = full[0].shape[0] + full[1].shape[0], near[0].shape[1] // 2
    flops = 12 * cols * full[0].shape[1] * 2 * half
    outs = [shaped((cols, half))] + [shaped((b - a, half)) for a, b in part_rows(cols)]
    out = call(functools.partial(grad_body, factor), outs, (*full, *other, *near, *far), flops)
    return out[1:], out[0]


def pass_line(value, pairs):
    return lax.ppermute(value, "col", pairs)


BESIDE = [(0, 1), (1, 0), (2, 3), (3, 2)]
ACROSS = [(0, 3), (3, 0), (1, 2), (2, 1)]


def add_body(*refs):
    count = len(refs) // 3
    for i in range(count):
        refs[2 * count + i][...] = refs[i][...] + refs[count + i][...]


def add(many, more):
    return call(add_body, [shaped(a.shape) for a in many], (*many, *more))


def turn_body(*refs):
    for a, b, out in zip(refs[0:2], refs[2:4], refs[4:6]):
        rows = a.shape[1] // 2
        left, right = pl.ds(0, rows), pl.ds(rows, rows)
        out[:, left] = a[:, left] + b[:, right]
        out[:, right] = a[:, right] + b[:, left]


def turn(many, more):
    return call(turn_body, [shaped(a.shape) for a in many], (*many, *more))


def split_body(here, *refs):
    gone, sends, mine = refs[:-2], refs[-2], refs[-1]
    place = lax.axis_index("col")
    ends = (place == 0) | (place == 3)
    quarter = mine.shape[1]
    left, right = pl.ds(0, quarter), pl.ds(quarter, quarter)

    def put(kept, sent):
        for ref, (a, b) in zip(gone, part_rows(here.shape[0])):
            to = pl.ds(a, b - a)
            mine[to] = here[to, kept] + ref[:, kept]
            sends[to] = here[to, sent] + ref[:, sent]

    pl.when(ends)(lambda: put(left, right))
    pl.when(~ends)(lambda: put(right, left))


def split(here, gone):
    outs = [shaped((here.shape[0], here.shape[1] // 2))] * 2
    return call(split_body, outs, (here, *gone))


def cut(out):
    edges, at = [], 0
    for part in ROUNDS + (1.0,):
        left = out - at
        both = left if part == 1.0 else min(left, round(out * part / 16) * 16)
        first = -(-both // 16) * 8
        edges += [(at, at + first), (at + first, at + both)]
        at += both
    return edges


def square(batch, running_t, targets_t, centers, weights_t, factor):
    rows, out = batch.shape[0], weights_t.shape[0]
    mid = rows // 2
    edges = cut(out)
    rounds = len(edges) // 2
    line = Line()
    block_x = swap(batch, "chip", 1)
    block_y = swap(batch, "chip", 2)
    cent_theirs = swap(centers, "core")
    w0, w1 = weights_t, swap(weights_t, "core")
    cent = line(split_cent, centers, cent_theirs)
    own = line(own_kernels, batch, cent)
    low = swap(block_x[:mid], "chip", 2)
    high = swap(block_y[mid:], "chip", 1)
    near = line(near_kernels, block_x, block_y, cent, own)
    far, sent = line(lambda *a: far_kernels(edges[:4], *a), low, high, cent, near, w0, w1)

    axes = ((1, 2), (2, 1))
    place = lax.axis_index("col")
    ends = (place == 0) | (place == 3)

    def both(pair, step):
        return [swap(pair[i], "chip", axes[i][step]) for i in (0, 1)]

    coming, crossing, beside, across, back = ([None] * rounds for _ in range(5))
    partial, full, other, gone, here, mine, total = ([None] * rounds for _ in range(7))

    def do_partial(r):
        partial[r] = line(add, kept[2 * r : 2 * r + 2], coming[r])
        crossing[r] = both(partial[r], 1)

    def do_full(r):
        full[r] = line(turn, partial[r], crossing[r])
        other[r] = both(full[r], 0)

    def do_grad(r):
        gone[r], here[r] = line(lambda *a: grad_parts(factor, *a), full[r], other[r], near, far)
        gone[r] = [swap(part, "core") for part in gone[r]]

    def do_owned(r):
        sends, mine[r] = line(split, here[r], gone[r])
        beside[r] = pass_line(sends, BESIDE)

    def do_mine(r):
        (mine[r],) = line(add, [mine[r]], [beside[r]])
        across[r] = pass_line(mine[r], ACROSS)

    def do_total(r):
        (total[r],) = line(add, [mine[r]], [across[r]])
        back[r] = pass_line(total[r], BESIDE)

    coming[0] = both(sent[0:2], 0)
    coming[1] = both(line.hold(tuple(sent[2:4])), 0)
    kept = line(lambda *a: keep_shares(edges, *a), w0, w1, running_t, targets_t, near)
    do_partial(0)
    do_partial(1)
    do_full(0)
    do_full(1)
    do_grad(0)
    do_owned(0)
    do_grad(1)
    do_mine(0)
    do_owned(1)
    do_mine(1)
    do_total(0)
    do_total(1)

    first = [jnp.where(ends, t, b) for t, b in zip(total, back)]
    second = [jnp.where(ends, b, t) for t, b in zip(total, back)]
    gradient = jnp.concatenate([jnp.concatenate(first), jnp.concatenate(second)], axis=1)
    mine_rows = (slice(0, rows), slice(rows, None))
    residual = jnp.concatenate([f[i][:, mine_rows[i]] for f in full for i in (0, 1)])
    return gradient, residual


def any_plane(batch, running_t, targets_t, centers, weights_t, factor):
    def dot(a, b, dims, precision):
        return lax.dot_general(a, b, dims, precision=precision, preferred_element_type=F32)

    rows_here, chips = batch.shape[0], lax.axis_size("chip")
    half, out = centers.shape[0], weights_t.shape[0]
    cent = jnp.concatenate([centers, swap(centers, "core")], axis=0)
    weight = jnp.concatenate([weights_t, swap(weights_t, "core")], axis=1)
    rows = lax.all_gather(batch, "chip", axis=0, tiled=True)
    row_sq = jnp.sum(rows * rows, axis=1, keepdims=True)
    dist_sq = row_sq + jnp.sum(cent * cent, axis=1)[None, :] - 2.0 * dot(rows, cent, NT, HIGHEST)
    kernel = jnp.exp(-jnp.sqrt(dist_sq + 1.0) / (math.sqrt(rows.shape[1]) / 4.0))
    shares = dot(weight, kernel, NT, HIGH).reshape(out, chips, rows_here).transpose(1, 0, 2)
    residual = running_t - targets_t + lax.psum_scatter(shares, "chip", scatter_dimension=0, tiled=False)
    moved = lax.all_gather(residual, "chip", axis=0, tiled=False)
    moved = moved.transpose(1, 0, 2).reshape(out, chips * rows_here)
    gradient = dot(moved, kernel, NN, HIGH) * factor
    owned = gradient[:, :half] + swap(gradient[:, half:], "core")
    return lax.psum(owned, "col"), residual


def per_device(batch, running, targets, centers, weights):
    chips, depth = lax.axis_size("chip"), lax.axis_size("col")
    factor = 1.0 / math.sqrt(batch.shape[0] * chips * 2 * depth)
    plane = square if (chips, depth) == (4, 4) else any_plane
    gradient, residual = plane(batch, running.T, targets.T, centers, weights.T, factor)
    return gradient.T, residual.T


def solution(mesh):
    owners, depth = mesh.shape["row"], mesh.shape["col"]
    split = Mesh(mesh.devices.reshape(owners // 2, 2, depth), ("chip", "core", "col"))
    everywhere = P(("chip", "core", "col"), None)
    owned = P(("chip", "core"), None)
    return jax.shard_map(
        per_device,
        mesh=split,
        in_specs=(everywhere, everywhere, everywhere, owned, owned),
        out_specs=(owned, everywhere),
        check_vma=False,
    )
```

```python
import functools
import math

import jax
import jax.numpy as jnp
from jax import lax
from jax.experimental import pallas as pl
from jax.experimental.pallas import tpu as pltpu
from jax.sharding import Mesh, PartitionSpec as P

HIGHEST = lax.Precision.HIGHEST
HIGH = lax.Precision.HIGH
ROUNDS = (0.2,0.38,)
STEPS = "P0 P1 F0 P2 G0 F1 O0 F2 G1 M0 O1 G2 T0 M1 O2 T1 M2 T2".split()
BF16, F32 = jnp.bfloat16, jnp.float32
NT = (((1,), (1,)), ((), ()))
NN = (((1,), (0,)), ((), ()))


def swap(value, axis, flip=1):
    size = lax.axis_size(axis)
    return lax.ppermute(value, axis, [(i, i ^ flip) for i in range(size)])


class Line:
    def __init__(self):
        self.last = None

    def hold(self, args):
        if self.last is None:
            return args
        return lax.optimization_barrier((args, self.last))[0]

    def __call__(self, step, *args):
        out = step(*self.hold(args))
        self.last = jax.tree.leaves(out)[0]
        return out


def halves(value):
    high = value.astype(BF16)
    return high, (value - high.astype(F32)).astype(BF16)


def mul(a, b, dims):
    return lax.dot_general(a, b, dims, preferred_element_type=F32)


def mul3(a, b, dims):
    return mul(a[0], b[0], dims) + (mul(a[0], b[1], dims) + mul(a[1], b[0], dims))


def call(body, outs, args, scratch=()):
    vmem = pl.BlockSpec(memory_space=pltpu.VMEM)
    return pl.pallas_call(
        body,
        out_shape=outs,
        in_specs=[vmem] * len(args),
        out_specs=[vmem] * len(outs),
        scratch_shapes=list(scratch),
        cost_estimate=pl.CostEstimate(flops=0, bytes_accessed=0, transcendentals=0),
        compiler_params=pltpu.CompilerParams(vmem_limit_bytes=40 * 2**20),
    )(*args)


def shaped(shape, dtype=F32):
    return jax.ShapeDtypeStruct(shape, dtype)


def cent_body(mine_ref, theirs_ref, high_ref, low_ref, sq_ref):
    half = mine_ref.shape[0]
    for i, ref in enumerate((mine_ref, theirs_ref)):
        for at in range(0, half, 128):
            to = pl.ds(i * half + at, 128)
            value = ref[pl.ds(at, 128)]
            high_ref[to], low_ref[to] = halves(value)
            total = jnp.sum(value * value, axis=1, keepdims=True)
            sq_ref[:, to] = jnp.broadcast_to(total, (128, 128)).T[:8]


def split_cent(mine, theirs):
    half, width = mine.shape
    pair = [shaped((2 * half, width), BF16)] * 2
    return call(cent_body, pair + [shaped((8, 2 * half))], (mine, theirs))


def kernel_rows(high, low, row_sq, cent_refs, put):
    cent_high, cent_low, cent_sq = cent_refs
    scale = -4.0 / math.sqrt(cent_high.shape[1])
    for at in range(0, cent_high.shape[0], 256):
        to = pl.ds(at, 256)
        ch, cl = cent_high[to], cent_low[to]
        crossed = mul(high, ch, NT) + (mul(high, cl, NT) + mul(low, ch, NT) + mul(low, cl, NT))
        dist_sq = row_sq + cent_sq[0:1, to] - 2.0 * crossed
        put(to, halves(jnp.exp(jnp.sqrt(dist_sq + 1.0) * scale)))


def fill(refs, high_ref, low_ref, sq_ref):
    at = 0
    for ref in refs:
        to = pl.ds(at, ref.shape[0])
        value = ref[...]
        high_ref[to], low_ref[to] = halves(value)
        sq_ref[to] = jnp.broadcast_to(jnp.sum(value * value, axis=1, keepdims=True), (ref.shape[0], 128))
        at += ref.shape[0]


def own_body(own, c_high, c_low, c_sq, own_high, own_low, high, low, row_sq):
    fill((own,), high, low, row_sq)

    def put(to, pair):
        own_high[:, to], own_low[:, to] = pair

    kernel_rows(high[...], low[...], row_sq[:, 0:1], (c_high, c_low, c_sq), put)


def row_scratch(rows, width):
    return [pltpu.VMEM((rows, width), BF16)] * 2 + [pltpu.VMEM((rows, 128), F32)]


def own_kernels(own, cent):
    rows, width = own.shape
    wide = cent[0].shape[0]
    return call(
        own_body,
        [shaped((rows, wide), BF16)] * 2,
        (own, *cent),
        scratch=row_scratch(rows, width),
    )


def near_body(x, y, c_high, c_low, c_sq, own_high, own_low, near_high, near_low, high, low, row_sq):
    rows = x.shape[0]
    fill((x, y), high, low, row_sq)
    near_high[pl.ds(rows, rows)] = own_high[...]
    near_low[pl.ds(rows, rows)] = own_low[...]

    def put(to, pair):
        for ref, value in zip((near_high, near_low), pair):
            ref[pl.ds(0, rows), to] = value[:rows]
            ref[pl.ds(2 * rows, rows), to] = value[rows:]

    kernel_rows(high[...], low[...], row_sq[:, 0:1], (c_high, c_low, c_sq), put)


def near_kernels(x, y, cent, own):
    rows, width = x.shape
    wide = cent[0].shape[0]
    return call(
        near_body,
        [shaped((3 * rows, wide), BF16)] * 2,
        (x, y, *cent, *own),
        scratch=row_scratch(2 * rows, width),
    )


def share(w_refs, cols, k_refs, rows):
    half = w_refs[0].shape[1]
    total = None
    for i, ref in enumerate(w_refs):
        kept = pl.ds(i * half, half)
        part = mul3(halves(ref[cols]), (k_refs[0][rows, kept], k_refs[1][rows, kept]), NT)
        total = part if total is None else total + part
    return total


def stays(rows):
    return pl.ds(rows, 2 * rows), pl.ds(0, 2 * rows)


def goes(rows):
    return pl.ds(0, 2 * rows), pl.ds(rows, 2 * rows)


def keep_body(edges, rows, w0, w1, running, targets, near_high, near_low, *outs):
    kept, going = outs[: len(edges)], outs[len(edges) :]
    left, middle, right = pl.ds(0, rows), pl.ds(rows, rows), pl.ds(2 * rows, rows)
    for i, (a, b) in enumerate(edges):
        cols = pl.ds(a, b - a)
        value = share((w0, w1), cols, (near_high, near_low), pl.ds(0, 3 * rows))
        own = value[:, rows : 2 * rows] + (running[cols] - targets[cols])
        x, y = value[:, :rows], value[:, 2 * rows :]
        if i % 2 == 0:
            kept[i][:, left], kept[i][:, middle], going[i][...] = own, y, x
        else:
            kept[i][:, left], kept[i][:, middle], going[i][...] = x, own, y


def keep_shares(edges, w0, w1, running, targets, near):
    rows = running.shape[1]
    outs = [shaped((b - a, n * rows)) for n in (2, 1) for a, b in edges]
    out = call(
        functools.partial(keep_body, edges, rows), outs, (w0, w1, running, targets, *near)
    )
    return out[: len(edges)], out[len(edges) :]


def far_body(edges, low_rows, high_rows, c_high, c_low, c_sq, near_high, near_low, w0, w1, *rest):
    count = len(edges)
    going, outs, (high, low, row_sq) = rest[:count], rest[count:-3], rest[-3:]
    far_high, far_low, sent = outs[0], outs[1], outs[2:]
    rows = high.shape[0]
    left, middle, right = pl.ds(0, rows), pl.ds(rows, rows), pl.ds(2 * rows, rows)
    fill((low_rows, high_rows), high, low, row_sq)
    for far, near in ((far_high, near_high), (far_low, near_low)):
        far[left] = near[left]
        far[right] = near[right]

    def put(to, pair):
        far_high[middle, to], far_low[middle, to] = pair

    kernel_rows(high[...], low[...], row_sq[:, 0:1], (c_high, c_low, c_sq), put)
    for i, (a, b) in enumerate(edges):
        value = share((w0, w1), pl.ds(a, b - a), (far_high, far_low), middle)
        sent[i][:, left], sent[i][:, middle] = (
            (going[i][...], value) if i % 2 == 0 else (value, going[i][...])
        )


def far_kernels(edges, low, high, cent, near, w0, w1, going):
    rows, width = 2 * low.shape[0], low.shape[1]
    outs = [shaped(near[0].shape, BF16)] * 2 + [shaped((b - a, 2 * rows)) for a, b in edges]
    out = call(
        functools.partial(far_body, edges),
        outs,
        (low, high, *cent, *near, w0, w1, *going),
        scratch=row_scratch(rows, width),
    )
    return out[:2], out[2:]


PARTS = 3


def part_rows(size):
    step = -(-size // PARTS // 8) * 8
    return [(at, min(size, at + step)) for at in range(0, size, step)]


def grad_body(factor, full_a, full_b, other_a, other_b, near_high, near_low, far_high, far_low, here, *gone):
    rows, half = full_a.shape[1] // 2, here.shape[1]
    at = 0
    for i, (full, other) in enumerate(((full_a, other_a), (full_b, other_b))):
        to = pl.ds(at, full.shape[0])
        at += full.shape[0]
        full_pair, other_pair = halves(full[...]), halves(other[...])
        stay, go = stays(rows)[i], goes(rows)[i]
        for away, cols in ((True, pl.ds(half, half)), (False, pl.ds(0, half))):
            value = factor * (
                mul3(full_pair, (near_high[stay, cols], near_low[stay, cols]), NN)
                + mul3(other_pair, (far_high[go, cols], far_low[go, cols]), NN)
            )
            if not away:
                here[to] = value
                continue
            start, end = at - full.shape[0], at
            for ref, (low, high) in zip(gone, part_rows(here.shape[0])):
                low_at, high_at = max(low, start), min(high, end)
                if low_at < high_at:
                    ref[pl.ds(low_at - low, high_at - low_at)] = value[low_at - start : high_at - start]


def grad_parts(factor, full, other, near, far):
    cols, half = full[0].shape[0] + full[1].shape[0], near[0].shape[1] // 2
    outs = [shaped((cols, half))] + [shaped((b - a, half)) for a, b in part_rows(cols)]
    out = call(functools.partial(grad_body, factor), outs, (*full, *other, *near, *far))
    return out[1:], out[0]


def pass_line(value, pairs):
    return lax.ppermute(value, "col", pairs)


BESIDE = [(0, 1), (1, 0), (2, 3), (3, 2)]
ACROSS = [(0, 3), (3, 0), (1, 2), (2, 1)]


def add_body(*refs):
    count = len(refs) // 3
    for i in range(count):
        refs[2 * count + i][...] = refs[i][...] + refs[count + i][...]


def add(many, more):
    return call(add_body, [shaped(a.shape) for a in many], (*many, *more))


def turn_body(*refs):
    for a, b, out in zip(refs[0:2], refs[2:4], refs[4:6]):
        rows = a.shape[1] // 2
        left, right = pl.ds(0, rows), pl.ds(rows, rows)
        out[:, left] = a[:, left] + b[:, right]
        out[:, right] = a[:, right] + b[:, left]


def turn(many, more):
    return call(turn_body, [shaped(a.shape) for a in many], (*many, *more))


def split_body(here, *refs):
    gone, sends, mine = refs[:-2], refs[-2], refs[-1]
    place = lax.axis_index("col")
    ends = (place == 0) | (place == 3)
    quarter = mine.shape[1]
    left, right = pl.ds(0, quarter), pl.ds(quarter, quarter)

    def put(kept, sent):
        for ref, (a, b) in zip(gone, part_rows(here.shape[0])):
            to = pl.ds(a, b - a)
            mine[to] = here[to, kept] + ref[:, kept]
            sends[to] = here[to, sent] + ref[:, sent]

    pl.when(ends)(lambda: put(left, right))
    pl.when(~ends)(lambda: put(right, left))


def split(here, gone):
    outs = [shaped((here.shape[0], here.shape[1] // 2))] * 2
    return call(split_body, outs, (here, *gone))


def cut(out):
    edges, at = [], 0
    for part in ROUNDS + (1.0,):
        left = out - at
        both = left if part == 1.0 else min(left, round(out * part / 16) * 16)
        first = -(-both // 16) * 8
        edges += [(at, at + first), (at + first, at + both)]
        at += both
    return edges


def square(batch, running_t, targets_t, centers, weights_t, factor):
    rows, out = batch.shape[0], weights_t.shape[0]
    mid = rows // 2
    edges = cut(out)
    rounds = len(edges) // 2
    line = Line()
    block_x = swap(batch, "chip", 1)
    block_y = swap(batch, "chip", 2)
    cent_theirs = swap(centers, "core")
    w0, w1 = weights_t, swap(weights_t, "core")
    cent = line(split_cent, centers, cent_theirs)
    own = line(own_kernels, batch, cent)
    low = swap(block_x[:mid], "chip", 2)
    high = swap(block_y[mid:], "chip", 1)
    near = line(near_kernels, block_x, block_y, cent, own)
    kept, going = line(lambda *a: keep_shares(edges, *a), w0, w1, running_t, targets_t, near)
    far, sent = line(lambda *a: far_kernels(edges, *a), low, high, cent, near, w0, w1, going)

    axes = ((1, 2), (2, 1))
    place = lax.axis_index("col")
    ends = (place == 0) | (place == 3)

    def both(pair, step):
        return [swap(pair[i], "chip", axes[i][step]) for i in (0, 1)]

    coming, crossing, beside, across, back = ([None] * rounds for _ in range(5))
    partial, full, other, gone, here, mine, total = ([None] * rounds for _ in range(7))

    def do_partial(r):
        partial[r] = line(add, kept[2 * r : 2 * r + 2], coming[r])
        crossing[r] = both(partial[r], 1)

    def do_full(r):
        full[r] = line(turn, partial[r], crossing[r])
        other[r] = both(full[r], 0)

    def do_grad(r):
        gone[r], here[r] = line(lambda *a: grad_parts(factor, *a), full[r], other[r], near, far)
        gone[r] = [swap(part, "core") for part in gone[r]]

    def do_owned(r):
        sends, mine[r] = line(split, here[r], gone[r])
        beside[r] = pass_line(sends, BESIDE)

    def do_mine(r):
        (mine[r],) = line(add, [mine[r]], [beside[r]])
        across[r] = pass_line(mine[r], ACROSS)

    def do_total(r):
        (total[r],) = line(add, [mine[r]], [across[r]])
        back[r] = pass_line(total[r], BESIDE)

    for r in range(rounds):
        coming[r] = both(sent[2 * r : 2 * r + 2], 0)
    for step in STEPS:
        dict(P=do_partial, F=do_full, G=do_grad, O=do_owned, M=do_mine, T=do_total)[step[0]](int(step[1]))

    first = [jnp.where(ends, t, b) for t, b in zip(total, back)]
    second = [jnp.where(ends, b, t) for t, b in zip(total, back)]
    gradient = jnp.concatenate([jnp.concatenate(first), jnp.concatenate(second)], axis=1)
    mine_rows = (slice(0, rows), slice(rows, None))
    residual = jnp.concatenate([f[i][:, mine_rows[i]] for f in full for i in (0, 1)])
    return gradient, residual


def any_plane(batch, running_t, targets_t, centers, weights_t, factor):
    def dot(a, b, dims, precision):
        return lax.dot_general(a, b, dims, precision=precision, preferred_element_type=F32)

    rows_here, chips = batch.shape[0], lax.axis_size("chip")
    half, out = centers.shape[0], weights_t.shape[0]
    cent = jnp.concatenate([centers, swap(centers, "core")], axis=0)
    weight = jnp.concatenate([weights_t, swap(weights_t, "core")], axis=1)
    rows = lax.all_gather(batch, "chip", axis=0, tiled=True)
    row_sq = jnp.sum(rows * rows, axis=1, keepdims=True)
    dist_sq = row_sq + jnp.sum(cent * cent, axis=1)[None, :] - 2.0 * dot(rows, cent, NT, HIGHEST)
    kernel = jnp.exp(-jnp.sqrt(dist_sq + 1.0) / (math.sqrt(rows.shape[1]) / 4.0))
    shares = dot(weight, kernel, NT, HIGH).reshape(out, chips, rows_here).transpose(1, 0, 2)
    residual = running_t - targets_t + lax.psum_scatter(shares, "chip", scatter_dimension=0, tiled=False)
    moved = lax.all_gather(residual, "chip", axis=0, tiled=False)
    moved = moved.transpose(1, 0, 2).reshape(out, chips * rows_here)
    gradient = dot(moved, kernel, NN, HIGH) * factor
    owned = gradient[:, :half] + swap(gradient[:, half:], "core")
    return lax.psum(owned, "col"), residual


def per_device(batch, running, targets, centers, weights):
    chips, depth = lax.axis_size("chip"), lax.axis_size("col")
    factor = 1.0 / math.sqrt(batch.shape[0] * chips * 2 * depth)
    plane = square if (chips, depth) == (4, 4) else any_plane
    gradient, residual = plane(batch, running.T, targets.T, centers, weights.T, factor)
    return gradient.T, residual.T


def solution(mesh):
    owners, depth = mesh.shape["row"], mesh.shape["col"]
    split = Mesh(mesh.devices.reshape(owners // 2, 2, depth), ("chip", "core", "col"))
    everywhere = P(("chip", "core", "col"), None)
    owned = P(("chip", "core"), None)
    return jax.shard_map(
        per_device,
        mesh=split,
        in_specs=(everywhere, everywhere, everywhere, owned, owned),
        out_specs=(owned, everywhere),
        check_vma=False,
    )
```

```python
import functools
import math

import jax
import jax.numpy as jnp
from jax import lax
from jax.experimental import pallas as pl
from jax.experimental.pallas import tpu as pltpu
from jax.sharding import Mesh, PartitionSpec as P

HIGHEST = lax.Precision.HIGHEST
HIGH = lax.Precision.HIGH
ROUNDS = (0.48,)
STEPS = ("P0 P1 F0 F1", "G0 O0 G1 M0", "O1 M1 T0 T1")
BF16, F32 = jnp.bfloat16, jnp.float32
NT = (((1,), (1,)), ((), ()))
NN = (((1,), (0,)), ((), ()))


def swap(value, axis, flip=1):
    size = lax.axis_size(axis)
    return lax.ppermute(value, axis, [(i, i ^ flip) for i in range(size)])


class Line:
    def __init__(self):
        self.last = None

    def hold(self, args):
        if self.last is None:
            return args
        return lax.optimization_barrier((args, self.last))[0]

    def __call__(self, step, *args):
        out = step(*self.hold(args))
        self.last = jax.tree.leaves(out)[0]
        return out


def halves(value):
    high = value.astype(BF16)
    return high, (value - high.astype(F32)).astype(BF16)


def mul(a, b, dims):
    return lax.dot_general(a, b, dims, preferred_element_type=F32)


def mul3(a, b, dims):
    return mul(a[0], b[0], dims) + (mul(a[0], b[1], dims) + mul(a[1], b[0], dims))


def call(body, outs, args, scratch=()):
    vmem = pl.BlockSpec(memory_space=pltpu.VMEM)
    return pl.pallas_call(
        body,
        out_shape=outs,
        in_specs=[vmem] * len(args),
        out_specs=[vmem] * len(outs),
        scratch_shapes=list(scratch),
        cost_estimate=pl.CostEstimate(flops=0, bytes_accessed=0, transcendentals=0),
        compiler_params=pltpu.CompilerParams(vmem_limit_bytes=40 * 2**20),
    )(*args)


def shaped(shape, dtype=F32):
    return jax.ShapeDtypeStruct(shape, dtype)


def cent_body(mine_ref, theirs_ref, high_ref, low_ref, sq_ref):
    half = mine_ref.shape[0]
    for i, ref in enumerate((mine_ref, theirs_ref)):
        for at in range(0, half, 128):
            to = pl.ds(i * half + at, 128)
            value = ref[pl.ds(at, 128)]
            high_ref[to], low_ref[to] = halves(value)
            total = jnp.sum(value * value, axis=1, keepdims=True)
            sq_ref[:, to] = jnp.broadcast_to(total, (128, 128)).T[:8]


def split_cent(mine, theirs):
    half, width = mine.shape
    pair = [shaped((2 * half, width), BF16)] * 2
    return call(cent_body, pair + [shaped((8, 2 * half))], (mine, theirs))


def kernel_rows(high, low, row_sq, cent_refs, put):
    cent_high, cent_low, cent_sq = cent_refs
    scale = -4.0 / math.sqrt(cent_high.shape[1])
    for at in range(0, cent_high.shape[0], 256):
        to = pl.ds(at, 256)
        ch, cl = cent_high[to], cent_low[to]
        crossed = mul(high, ch, NT) + (mul(high, cl, NT) + mul(low, ch, NT) + mul(low, cl, NT))
        dist_sq = row_sq + cent_sq[0:1, to] - 2.0 * crossed
        put(to, halves(jnp.exp(jnp.sqrt(dist_sq + 1.0) * scale)))


def fill(refs, high_ref, low_ref, sq_ref):
    at = 0
    for ref in refs:
        to = pl.ds(at, ref.shape[0])
        value = ref[...]
        high_ref[to], low_ref[to] = halves(value)
        sq_ref[to] = jnp.broadcast_to(jnp.sum(value * value, axis=1, keepdims=True), (ref.shape[0], 128))
        at += ref.shape[0]


def own_body(own, c_high, c_low, c_sq, own_high, own_low, high, low, row_sq):
    fill((own,), high, low, row_sq)

    def put(to, pair):
        own_high[:, to], own_low[:, to] = pair

    kernel_rows(high[...], low[...], row_sq[:, 0:1], (c_high, c_low, c_sq), put)


def row_scratch(rows, width):
    return [pltpu.VMEM((rows, width), BF16)] * 2 + [pltpu.VMEM((rows, 128), F32)]


def own_kernels(own, cent):
    rows, width = own.shape
    wide = cent[0].shape[0]
    return call(
        own_body,
        [shaped((rows, wide), BF16)] * 2,
        (own, *cent),
        scratch=row_scratch(rows, width),
    )


def near_body(first, second, c_high, c_low, c_sq, own_high, own_low, *rest):
    stay_high, stay_low, first_high, first_low, high, low, row_sq = rest
    rows = first.shape[0]
    fill((first, second), high, low, row_sq)
    stay_high[pl.ds(0, rows)] = own_high[...]
    stay_low[pl.ds(0, rows)] = own_low[...]

    def put(to, pair):
        for stay, ref, value in zip((stay_high, stay_low), (first_high, first_low), pair):
            ref[:, to] = value[:rows]
            stay[pl.ds(rows, rows), to] = value[rows:]

    kernel_rows(high[...], low[...], row_sq[:, 0:1], (c_high, c_low, c_sq), put)


def near_kernels(first, second, cent, own):
    rows, width = first.shape
    wide = cent[0].shape[0]
    outs = [shaped((n * rows, wide), BF16) for n in (2, 2, 1, 1)]
    out = call(
        near_body, outs, (first, second, *cent, *own), scratch=row_scratch(2 * rows, width)
    )
    return out[:2], out[2:]


def share(w_refs, cols, k_refs):
    half = w_refs[0].shape[1]
    total = None
    for i, ref in enumerate(w_refs):
        kept = pl.ds(i * half, half)
        part = mul3(halves(ref[cols]), (k_refs[0][:, kept], k_refs[1][:, kept]), NT)
        total = part if total is None else total + part
    return total


def keep_body(edges, w0, w1, running, targets, stay_high, stay_low, *kept):
    rows = running.shape[1]
    left, right = pl.ds(0, rows), pl.ds(rows, rows)
    for ref, (a, b) in zip(kept, edges):
        cols = pl.ds(a, b - a)
        value = share((w0, w1), cols, (stay_high, stay_low))
        ref[:, left] = value[:, :rows] + (running[cols] - targets[cols])
        ref[:, right] = value[:, rows:]


def keep_shares(edges, w0, w1, running, targets, stay):
    outs = [shaped((b - a, 2 * running.shape[1])) for a, b in edges]
    return call(functools.partial(keep_body, edges), outs, (w0, w1, running, targets, *stay))


def far_body(edges, far, c_high, c_low, c_sq, first_high, first_low, w0, w1, *rest):
    go_high, go_low, *sent = rest[:-3]
    high, low, row_sq = rest[-3:]
    rows = far.shape[0]
    fill((far,), high, low, row_sq)
    go_high[pl.ds(0, rows)] = first_high[...]
    go_low[pl.ds(0, rows)] = first_low[...]

    def put(to, pair):
        go_high[pl.ds(rows, rows), to], go_low[pl.ds(rows, rows), to] = pair

    kernel_rows(high[...], low[...], row_sq[:, 0:1], (c_high, c_low, c_sq), put)
    for ref, (a, b) in zip(sent, edges):
        ref[...] = share((w0, w1), pl.ds(a, b - a), (go_high, go_low))


def far_kernels(edges, far, cent, first, w0, w1):
    rows, width = far.shape
    outs = [shaped((2 * rows, cent[0].shape[0]), BF16)] * 2
    outs += [shaped((b - a, 2 * rows)) for a, b in edges]
    out = call(
        functools.partial(far_body, edges),
        outs,
        (far, *cent, *first, w0, w1),
        scratch=row_scratch(rows, width),
    )
    return out[:2], out[2:]


def send_body(edges, w0, w1, go_high, go_low, *sent):
    for ref, (a, b) in zip(sent, edges):
        ref[...] = share((w0, w1), pl.ds(a, b - a), (go_high, go_low))


def send_shares(edges, w0, w1, go):
    outs = [shaped((b - a, go[0].shape[0])) for a, b in edges]
    return call(functools.partial(send_body, edges), outs, (w0, w1, *go))


PARTS = 3


def part_rows(size):
    step = -(-size // PARTS // 8) * 8
    return [(at, min(size, at + step)) for at in range(0, size, step)]


def grad_body(factor, full, other, stay_high, stay_low, go_high, go_low, here, *gone):
    half = here.shape[1]
    full_pair, other_pair = halves(full[...]), halves(other[...])

    def part(cols):
        return factor * (
            mul3(full_pair, (stay_high[:, cols], stay_low[:, cols]), NN)
            + mul3(other_pair, (go_high[:, cols], go_low[:, cols]), NN)
        )

    away = part(pl.ds(half, half))
    for ref, (a, b) in zip(gone, part_rows(here.shape[0])):
        ref[...] = away[a:b]
    here[...] = part(pl.ds(0, half))


def grad_parts(factor, full, other, stay, go):
    cols, half = full.shape[0], stay[0].shape[1] // 2
    outs = [shaped((cols, half))] + [shaped((b - a, half)) for a, b in part_rows(cols)]
    out = call(functools.partial(grad_body, factor), outs, (full, other, *stay, *go))
    return out[1:], out[0]


def pass_line(value, pairs):
    return lax.ppermute(value, "col", pairs)


BESIDE = [(0, 1), (1, 0), (2, 3), (3, 2)]
ACROSS = [(0, 3), (3, 0), (1, 2), (2, 1)]


def add_body(a, b, out):
    out[...] = a[...] + b[...]


def add(a, b):
    return call(add_body, [shaped(a.shape)], (a, b))[0]


def turn_body(a, b, out):
    rows = a.shape[1] // 2
    left, right = pl.ds(0, rows), pl.ds(rows, rows)
    out[:, left] = a[:, left] + b[:, right]
    out[:, right] = a[:, right] + b[:, left]


def turn(a, b):
    return call(turn_body, [shaped(a.shape)], (a, b))[0]


def split_body(here, *refs):
    gone, sends, mine = refs[:-2], refs[-2], refs[-1]
    place = lax.axis_index("col")
    ends = (place == 0) | (place == 3)
    quarter = mine.shape[1]
    left, right = pl.ds(0, quarter), pl.ds(quarter, quarter)

    def put(kept, sent):
        for ref, (a, b) in zip(gone, part_rows(here.shape[0])):
            to = pl.ds(a, b - a)
            mine[to] = here[to, kept] + ref[:, kept]
            sends[to] = here[to, sent] + ref[:, sent]

    pl.when(ends)(lambda: put(left, right))
    pl.when(~ends)(lambda: put(right, left))


def split(here, gone):
    outs = [shaped((here.shape[0], here.shape[1] // 2))] * 2
    return call(split_body, outs, (here, *gone))


def cut(out):
    edges, at = [], 0
    for part in ROUNDS + (1.0,):
        to = out if part == 1.0 else min(out, at + round(out * part / 8) * 8)
        edges.append((at, to))
        at = to
    return edges


def hop(value, second):
    pairs = []
    for chip in range(4):
        for core in range(2):
            flip = 1 if core == second else 2
            pairs.append((chip * 2 + core, (chip ^ flip) * 2 + core))
    return lax.ppermute(value, ("chip", "core"), pairs)


def square(batch, running_t, targets_t, centers, weights_t, factor):
    rows, out = batch.shape[0], weights_t.shape[0]
    edges = cut(out)
    rounds = len(edges)
    line = Line()
    first = hop(batch, 0)
    second = hop(batch, 1)
    cent_theirs = swap(centers, "core")
    w0, w1 = weights_t, swap(weights_t, "core")
    cent = line(split_cent, centers, cent_theirs)
    own = line(own_kernels, batch, cent)
    far = hop(first, 1)
    stay, go_first = line(near_kernels, first, second, cent, own)
    go, sent = line(lambda *a: far_kernels(edges[:1], *a), far, cent, go_first, w0, w1)

    coming, crossing, beside, across, back = ([None] * rounds for _ in range(5))
    partial, full, other, gone, here, mine, total = ([None] * rounds for _ in range(7))

    def do_partial(r):
        partial[r] = line(add, kept[r], coming[r])
        crossing[r] = hop(partial[r], 1)

    def do_full(r):
        full[r] = line(turn, partial[r], crossing[r])
        other[r] = hop(full[r], 0)

    def do_grad(r):
        gone[r], here[r] = line(lambda *a: grad_parts(factor, *a), full[r], other[r], stay, go)
        gone[r] = [swap(part, "core") for part in gone[r]]

    def do_owned(r):
        sends, mine[r] = line(split, here[r], gone[r])
        beside[r] = pass_line(sends, BESIDE)

    def do_mine(r):
        mine[r] = line(add, mine[r], beside[r])
        across[r] = pass_line(mine[r], ACROSS)

    def do_total(r):
        total[r] = line(add, mine[r], across[r])
        back[r] = pass_line(total[r], BESIDE)

    sent = list(sent) + list(line(lambda *a: send_shares(edges[1:], *a), w0, w1, go))
    coming = [hop(value, 0) for value in sent]
    kept = line(lambda *a: keep_shares(edges, *a), w0, w1, running_t, targets_t, stay)
    steps = dict(P=do_partial, F=do_full, G=do_grad, O=do_owned, M=do_mine, T=do_total)
    for step in " ".join(STEPS).split():
        steps[step[0]](int(step[1]))

    place = lax.axis_index("col")
    ends = (place == 0) | (place == 3)
    left = [jnp.where(ends, t, b) for t, b in zip(total, back)]
    right = [jnp.where(ends, b, t) for t, b in zip(total, back)]
    gradient = jnp.concatenate([jnp.concatenate(left), jnp.concatenate(right)], axis=1)
    residual = jnp.concatenate([f[:, :rows] for f in full])
    return gradient, residual


def any_plane(batch, running_t, targets_t, centers, weights_t, factor):
    def dot(a, b, dims, precision):
        return lax.dot_general(a, b, dims, precision=precision, preferred_element_type=F32)

    rows_here, chips = batch.shape[0], lax.axis_size("chip")
    half, out = centers.shape[0], weights_t.shape[0]
    cent = jnp.concatenate([centers, swap(centers, "core")], axis=0)
    weight = jnp.concatenate([weights_t, swap(weights_t, "core")], axis=1)
    rows = lax.all_gather(batch, "chip", axis=0, tiled=True)
    row_sq = jnp.sum(rows * rows, axis=1, keepdims=True)
    dist_sq = row_sq + jnp.sum(cent * cent, axis=1)[None, :] - 2.0 * dot(rows, cent, NT, HIGHEST)
    kernel = jnp.exp(-jnp.sqrt(dist_sq + 1.0) / (math.sqrt(rows.shape[1]) / 4.0))
    shares = dot(weight, kernel, NT, HIGH).reshape(out, chips, rows_here).transpose(1, 0, 2)
    residual = running_t - targets_t + lax.psum_scatter(shares, "chip", scatter_dimension=0, tiled=False)
    moved = lax.all_gather(residual, "chip", axis=0, tiled=False)
    moved = moved.transpose(1, 0, 2).reshape(out, chips * rows_here)
    gradient = dot(moved, kernel, NN, HIGH) * factor
    owned = gradient[:, :half] + swap(gradient[:, half:], "core")
    return lax.psum(owned, "col"), residual


def per_device(batch, running, targets, centers, weights):
    chips, depth = lax.axis_size("chip"), lax.axis_size("col")
    factor = 1.0 / math.sqrt(batch.shape[0] * chips * 2 * depth)
    plane = square if (chips, depth) == (4, 4) else any_plane
    gradient, residual = plane(batch, running.T, targets.T, centers, weights.T, factor)
    return gradient.T, residual.T


def solution(mesh):
    owners, depth = mesh.shape["row"], mesh.shape["col"]
    split = Mesh(mesh.devices.reshape(owners // 2, 2, depth), ("chip", "core", "col"))
    everywhere = P(("chip", "core", "col"), None)
    owned = P(("chip", "core"), None)
    return jax.shard_map(
        per_device,
        mesh=split,
        in_specs=(everywhere, everywhere, everywhere, owned, owned),
        out_specs=(owned, everywhere),
        check_vma=False,
    )
```

```python
import functools
import math

import jax
import jax.numpy as jnp
from jax import lax
from jax.experimental import pallas as pl
from jax.experimental.pallas import tpu as pltpu
from jax.sharding import Mesh, PartitionSpec as P

HIGHEST = lax.Precision.HIGHEST
HIGH = lax.Precision.HIGH
ROUNDS = (0.48,)
STEPS = ("P0 P1 F0 F1", "G0 O0 G1 O1", "M0 T0 M1 M2", "T1 T2")
LINE_PIECES = (1,2,)
BF16, F32 = jnp.bfloat16, jnp.float32
NT = (((1,), (1,)), ((), ()))
NN = (((1,), (0,)), ((), ()))


def swap(value, axis, flip=1):
    size = lax.axis_size(axis)
    return lax.ppermute(value, axis, [(i, i ^ flip) for i in range(size)])


class Line:
    def __init__(self):
        self.last = None

    def hold(self, args):
        if self.last is None:
            return args
        return lax.optimization_barrier((args, self.last))[0]

    def __call__(self, step, *args):
        out = step(*self.hold(args))
        self.last = jax.tree.leaves(out)[0]
        return out


def halves(value):
    high = value.astype(BF16)
    return high, (value - high.astype(F32)).astype(BF16)


def mul(a, b, dims):
    return lax.dot_general(a, b, dims, preferred_element_type=F32)


def mul3(a, b, dims):
    return mul(a[0], b[0], dims) + (mul(a[0], b[1], dims) + mul(a[1], b[0], dims))


def call(body, outs, args, scratch=()):
    vmem = pl.BlockSpec(memory_space=pltpu.VMEM)
    return pl.pallas_call(
        body,
        out_shape=outs,
        in_specs=[vmem] * len(args),
        out_specs=[vmem] * len(outs),
        scratch_shapes=list(scratch),
        cost_estimate=pl.CostEstimate(flops=0, bytes_accessed=0, transcendentals=0),
        compiler_params=pltpu.CompilerParams(vmem_limit_bytes=40 * 2**20),
    )(*args)


def shaped(shape, dtype=F32):
    return jax.ShapeDtypeStruct(shape, dtype)


def cent_body(mine_ref, theirs_ref, high_ref, low_ref, sq_ref):
    half = mine_ref.shape[0]
    for i, ref in enumerate((mine_ref, theirs_ref)):
        for at in range(0, half, 128):
            to = pl.ds(i * half + at, 128)
            value = ref[pl.ds(at, 128)]
            high_ref[to], low_ref[to] = halves(value)
            total = jnp.sum(value * value, axis=1, keepdims=True)
            sq_ref[:, to] = jnp.broadcast_to(total, (128, 128)).T[:8]


def split_cent(mine, theirs):
    half, width = mine.shape
    pair = [shaped((2 * half, width), BF16)] * 2
    return call(cent_body, pair + [shaped((8, 2 * half))], (mine, theirs))


def kernel_rows(high, low, row_sq, cent_refs, put):
    cent_high, cent_low, cent_sq = cent_refs
    scale = -4.0 / math.sqrt(cent_high.shape[1])
    for at in range(0, cent_high.shape[0], 256):
        to = pl.ds(at, 256)
        ch, cl = cent_high[to], cent_low[to]
        crossed = mul(high, ch, NT) + (mul(high, cl, NT) + mul(low, ch, NT) + mul(low, cl, NT))
        dist_sq = row_sq + cent_sq[0:1, to] - 2.0 * crossed
        put(to, halves(jnp.exp(jnp.sqrt(dist_sq + 1.0) * scale)))


def fill(refs, high_ref, low_ref, sq_ref):
    at = 0
    for ref in refs:
        to = pl.ds(at, ref.shape[0])
        value = ref[...]
        high_ref[to], low_ref[to] = halves(value)
        sq_ref[to] = jnp.broadcast_to(jnp.sum(value * value, axis=1, keepdims=True), (ref.shape[0], 128))
        at += ref.shape[0]


def own_body(own, c_high, c_low, c_sq, own_high, own_low, high, low, row_sq):
    fill((own,), high, low, row_sq)

    def put(to, pair):
        own_high[:, to], own_low[:, to] = pair

    kernel_rows(high[...], low[...], row_sq[:, 0:1], (c_high, c_low, c_sq), put)


def row_scratch(rows, width):
    return [pltpu.VMEM((rows, width), BF16)] * 2 + [pltpu.VMEM((rows, 128), F32)]


def own_kernels(own, cent):
    rows, width = own.shape
    wide = cent[0].shape[0]
    return call(
        own_body,
        [shaped((rows, wide), BF16)] * 2,
        (own, *cent),
        scratch=row_scratch(rows, width),
    )


def near_body(x, y, c_high, c_low, c_sq, own_high, own_low, near_high, near_low, high, low, row_sq):
    rows = x.shape[0]
    fill((x, y), high, low, row_sq)
    near_high[pl.ds(rows, rows)] = own_high[...]
    near_low[pl.ds(rows, rows)] = own_low[...]

    def put(to, pair):
        for ref, value in zip((near_high, near_low), pair):
            ref[pl.ds(0, rows), to] = value[:rows]
            ref[pl.ds(2 * rows, rows), to] = value[rows:]

    kernel_rows(high[...], low[...], row_sq[:, 0:1], (c_high, c_low, c_sq), put)


def near_kernels(x, y, cent, own):
    rows, width = x.shape
    wide = cent[0].shape[0]
    return call(
        near_body,
        [shaped((3 * rows, wide), BF16)] * 2,
        (x, y, *cent, *own),
        scratch=row_scratch(2 * rows, width),
    )


def share(w_refs, cols, k_refs, rows):
    half = w_refs[0].shape[1]
    total = None
    for i, ref in enumerate(w_refs):
        kept = pl.ds(i * half, half)
        part = mul3(halves(ref[cols]), (k_refs[0][rows, kept], k_refs[1][rows, kept]), NT)
        total = part if total is None else total + part
    return total


def stays(rows):
    return pl.ds(rows, 2 * rows), pl.ds(0, 2 * rows)


def goes(rows):
    return pl.ds(0, 2 * rows), pl.ds(rows, 2 * rows)


def keep_body(edges, rows, w0, w1, running, targets, near_high, near_low, *kept):
    for i, (a, b) in enumerate(edges):
        cols = pl.ds(a, b - a)
        value = share((w0, w1), cols, (near_high, near_low), stays(rows)[i % 2])
        own = slice(0, rows) if i % 2 == 0 else slice(rows, 2 * rows)
        other = slice(rows, 2 * rows) if i % 2 == 0 else slice(0, rows)
        kept[i][:, own] = value[:, own] + (running[cols] - targets[cols])
        kept[i][:, other] = value[:, other]


def keep_shares(edges, w0, w1, running, targets, near):
    rows = running.shape[1]
    outs = [shaped((b - a, 2 * rows)) for a, b in edges]
    return call(
        functools.partial(keep_body, edges, rows), outs, (w0, w1, running, targets, *near)
    )


def far_body(edges, block, c_high, c_low, c_sq, near_high, near_low, w0, w1, *rest):
    outs, (high, low, row_sq) = rest[:-3], rest[-3:]
    far_high, far_low, sent = outs[0], outs[1], outs[2:]
    rows = low.shape[0]
    fill((block,), high, low, row_sq)
    for far, near in ((far_high, near_high), (far_low, near_low)):
        far[pl.ds(0, rows)] = near[pl.ds(0, rows)]
        far[pl.ds(2 * rows, rows)] = near[pl.ds(2 * rows, rows)]

    def put(to, pair):
        far_high[pl.ds(rows, rows), to], far_low[pl.ds(rows, rows), to] = pair

    kernel_rows(high[...], low[...], row_sq[:, 0:1], (c_high, c_low, c_sq), put)
    for i, (a, b) in enumerate(edges):
        sent[i][...] = share((w0, w1), pl.ds(a, b - a), (far_high, far_low), goes(rows)[i % 2])


def far_kernels(edges, block, cent, near, w0, w1):
    rows, width = block.shape
    wide = cent[0].shape[0]
    outs = [shaped(near[0].shape, BF16)] * 2 + [shaped((b - a, 2 * rows)) for a, b in edges]
    out = call(
        functools.partial(far_body, edges),
        outs,
        (block, *cent, *near, w0, w1),
        scratch=row_scratch(rows, width),
    )
    return out[:2], out[2:]


def send_body(edges, rows, w0, w1, far_high, far_low, *sent):
    for i, (a, b) in enumerate(edges):
        sent[i][...] = share((w0, w1), pl.ds(a, b - a), (far_high, far_low), goes(rows)[i % 2])


def send_shares(edges, w0, w1, far):
    rows = far[0].shape[0] // 3
    outs = [shaped((b - a, 2 * rows)) for a, b in edges]
    return call(functools.partial(send_body, edges, rows), outs, (w0, w1, *far))


PARTS = 3


def blocks(size, count):
    step = -(-size // count // 8) * 8
    return [(at, min(size, at + step)) for at in range(0, size, step)]


def grad_body(factor, full_a, full_b, other_a, other_b, near_high, near_low, far_high, far_low, here, *gone):
    rows, half = full_a.shape[1] // 2, here.shape[1]
    at = 0
    for i, (full, other) in enumerate(((full_a, other_a), (full_b, other_b))):
        to = pl.ds(at, full.shape[0])
        at += full.shape[0]
        full_pair, other_pair = halves(full[...]), halves(other[...])
        stay, go = stays(rows)[i], goes(rows)[i]
        for away, cols in ((True, pl.ds(half, half)), (False, pl.ds(0, half))):
            value = factor * (
                mul3(full_pair, (near_high[stay, cols], near_low[stay, cols]), NN)
                + mul3(other_pair, (far_high[go, cols], far_low[go, cols]), NN)
            )
            if not away:
                here[to] = value
                continue
            start, end = at - full.shape[0], at
            for ref, (low, high) in zip(gone, blocks(here.shape[0], PARTS)):
                low_at, high_at = max(low, start), min(high, end)
                if low_at < high_at:
                    ref[pl.ds(low_at - low, high_at - low_at)] = value[low_at - start : high_at - start]


def grad_parts(factor, full, other, near, far):
    cols, half = full[0].shape[0] + full[1].shape[0], near[0].shape[1] // 2
    outs = [shaped((cols, half))] + [shaped((b - a, half)) for a, b in blocks(cols, PARTS)]
    out = call(functools.partial(grad_body, factor), outs, (*full, *other, *near, *far))
    return out[1:], out[0]


def pass_line(value, pairs):
    return lax.ppermute(value, "col", pairs)


BESIDE = [(0, 1), (1, 0), (2, 3), (3, 2)]
ACROSS = [(0, 3), (3, 0), (1, 2), (2, 1)]


def add_body(*refs):
    count = len(refs) // 3
    for i in range(count):
        refs[2 * count + i][...] = refs[i][...] + refs[count + i][...]


def add(many, more):
    return call(add_body, [shaped(a.shape) for a in many], (*many, *more))


def turn_body(*refs):
    for a, b, out in zip(refs[0:2], refs[2:4], refs[4:6]):
        rows = a.shape[1] // 2
        left, right = pl.ds(0, rows), pl.ds(rows, rows)
        out[:, left] = a[:, left] + b[:, right]
        out[:, right] = a[:, right] + b[:, left]


def turn(many, more):
    return call(turn_body, [shaped(a.shape) for a in many], (*many, *more))


def split_body(here, *refs):
    parts = blocks(here.shape[0], PARTS)
    gone, outs = refs[: len(parts)], refs[len(parts) :]
    count = len(outs) // 2
    pieces = blocks(here.shape[0], count)
    place = lax.axis_index("col")
    ends = (place == 0) | (place == 3)
    quarter = here.shape[1] // 2
    left, right = pl.ds(0, quarter), pl.ds(quarter, quarter)

    def put(kept, sent):
        for ref, (a, b) in zip(gone, parts):
            for i, (low, high) in enumerate(pieces):
                at, end = max(a, low), min(b, high)
                if at < end:
                    of, part, to = (pl.ds(at - n, end - at) for n in (0, a, low))
                    outs[i][to] = here[of, sent] + ref[part, sent]
                    outs[count + i][to] = here[of, kept] + ref[part, kept]

    pl.when(ends)(lambda: put(left, right))
    pl.when(~ends)(lambda: put(right, left))


def split(count, here, gone):
    rows, half = here.shape
    outs = [shaped((b - a, half // 2)) for a, b in blocks(rows, count)] * 2
    out = call(split_body, outs, (here, *gone))
    return out[: len(out) // 2], out[len(out) // 2 :]


def cut(out):
    edges, at = [], 0
    for part in ROUNDS + (1.0,):
        left = out - at
        both = left if part == 1.0 else min(left, round(out * part / 16) * 16)
        first = -(-both // 16) * 8
        edges += [(at, at + first), (at + first, at + both)]
        at += both
    return edges


def hop(value, second):
    pairs = []
    for chip in range(4):
        for core in range(2):
            flip = 1 if core == second else 2
            pairs.append((chip * 2 + core, (chip ^ flip) * 2 + core))
    return lax.ppermute(value, ("chip", "core"), pairs)


def square(batch, running_t, targets_t, centers, weights_t, factor):
    rows, out = batch.shape[0], weights_t.shape[0]
    edges = cut(out)
    rounds = len(edges) // 2
    line = Line()
    block_x = hop(batch, 0)
    block_y = hop(batch, 1)
    cent_theirs = swap(centers, "core")
    w0, w1 = weights_t, swap(weights_t, "core")
    cent = line(split_cent, centers, cent_theirs)
    own = line(own_kernels, batch, cent)
    block = hop(block_x, 1)
    near = line(near_kernels, block_x, block_y, cent, own)
    far, sent = line(lambda *a: far_kernels(edges[:2], *a), block, cent, near, w0, w1)

    place = lax.axis_index("col")
    ends = (place == 0) | (place == 3)

    def both(pair, step):
        return [hop(pair[i], (i + step) % 2) for i in (0, 1)]

    coming, crossing = [None] * rounds, [None] * rounds
    partial, full, other, gone, here = ([None] * rounds for _ in range(5))
    beside, mine, across, total, back = [], [], [], [], []

    def do_partial(r):
        partial[r] = line(add, kept[2 * r : 2 * r + 2], coming[r])
        crossing[r] = both(partial[r], 1)

    def do_full(r):
        full[r] = line(turn, partial[r], crossing[r])
        other[r] = both(full[r], 0)

    def do_grad(r):
        gone[r], here[r] = line(lambda *a: grad_parts(factor, *a), full[r], other[r], near, far)
        gone[r] = [swap(part, "core") for part in gone[r]]

    def do_owned(r):
        sends, keeps = line(lambda *a: split(LINE_PIECES[r], *a), here[r], gone[r])
        mine.extend(keeps)
        beside.extend(pass_line(value, BESIDE) for value in sends)

    def do_mine(i):
        (mine[i],) = line(add, [mine[i]], [beside[i]])
        across.append(pass_line(mine[i], ACROSS))

    def do_total(i):
        (value,) = line(add, [mine[i]], [across[i]])
        total.append(value)
        back.append(pass_line(value, BESIDE))

    sent = list(sent) + list(line(lambda *a: send_shares(edges[2:], *a), w0, w1, far))
    coming = [both(sent[2 * r : 2 * r + 2], 0) for r in range(rounds)]
    kept = line(lambda *a: keep_shares(edges, *a), w0, w1, running_t, targets_t, near)
    steps = dict(P=do_partial, F=do_full, G=do_grad, O=do_owned, M=do_mine, T=do_total)
    for step in " ".join(STEPS).split():
        steps[step[0]](int(step[1]))

    first = [jnp.where(ends, t, b) for t, b in zip(total, back)]
    second = [jnp.where(ends, b, t) for t, b in zip(total, back)]
    gradient = jnp.concatenate([jnp.concatenate(first), jnp.concatenate(second)], axis=1)
    mine_rows = (slice(0, rows), slice(rows, None))
    residual = jnp.concatenate([f[i][:, mine_rows[i]] for f in full for i in (0, 1)])
    return gradient, residual


def any_plane(batch, running_t, targets_t, centers, weights_t, factor):
    def dot(a, b, dims, precision):
        return lax.dot_general(a, b, dims, precision=precision, preferred_element_type=F32)

    rows_here, chips = batch.shape[0], lax.axis_size("chip")
    half, out = centers.shape[0], weights_t.shape[0]
    cent = jnp.concatenate([centers, swap(centers, "core")], axis=0)
    weight = jnp.concatenate([weights_t, swap(weights_t, "core")], axis=1)
    rows = lax.all_gather(batch, "chip", axis=0, tiled=True)
    row_sq = jnp.sum(rows * rows, axis=1, keepdims=True)
    dist_sq = row_sq + jnp.sum(cent * cent, axis=1)[None, :] - 2.0 * dot(rows, cent, NT, HIGHEST)
    kernel = jnp.exp(-jnp.sqrt(dist_sq + 1.0) / (math.sqrt(rows.shape[1]) / 4.0))
    shares = dot(weight, kernel, NT, HIGH).reshape(out, chips, rows_here).transpose(1, 0, 2)
    residual = running_t - targets_t + lax.psum_scatter(shares, "chip", scatter_dimension=0, tiled=False)
    moved = lax.all_gather(residual, "chip", axis=0, tiled=False)
    moved = moved.transpose(1, 0, 2).reshape(out, chips * rows_here)
    gradient = dot(moved, kernel, NN, HIGH) * factor
    owned = gradient[:, :half] + swap(gradient[:, half:], "core")
    return lax.psum(owned, "col"), residual


def per_device(batch, running, targets, centers, weights):
    chips, depth = lax.axis_size("chip"), lax.axis_size("col")
    factor = 1.0 / math.sqrt(batch.shape[0] * chips * 2 * depth)
    plane = square if (chips, depth) == (4, 4) else any_plane
    gradient, residual = plane(batch, running.T, targets.T, centers, weights.T, factor)
    return gradient.T, residual.T


def solution(mesh):
    owners, depth = mesh.shape["row"], mesh.shape["col"]
    split = Mesh(mesh.devices.reshape(owners // 2, 2, depth), ("chip", "core", "col"))
    everywhere = P(("chip", "core", "col"), None)
    owned = P(("chip", "core"), None)
    return jax.shard_map(
        per_device,
        mesh=split,
        in_specs=(everywhere, everywhere, everywhere, owned, owned),
        out_specs=(owned, everywhere),
        check_vma=False,
    )
```

```python
import functools
import math

import jax
import jax.numpy as jnp
from jax import lax
from jax.experimental import pallas as pl
from jax.experimental.pallas import tpu as pltpu
from jax.sharding import Mesh, PartitionSpec as P

HIGHEST = lax.Precision.HIGHEST
HIGH = lax.Precision.HIGH
ROUNDS = (0.36,)
STEPS = ("P0 F0 P1 G0", "O0 M0 F1 T0", "G1 O1 M1 M2", "T1 D0 T2 D1", "D2")
LINE_PIECES = (1,2,)
BF16, F32 = jnp.bfloat16, jnp.float32
NT = (((1,), (1,)), ((), ()))
NN = (((1,), (0,)), ((), ()))


def swap(value, axis, flip=1):
    size = lax.axis_size(axis)
    return lax.ppermute(value, axis, [(i, i ^ flip) for i in range(size)])


class Line:
    def __init__(self):
        self.last = None

    def hold(self, args):
        if self.last is None:
            return args
        return lax.optimization_barrier((args, self.last))[0]

    def __call__(self, step, *args):
        out = step(*self.hold(args))
        self.last = jax.tree.leaves(out)[0]
        return out


def halves(value):
    high = value.astype(BF16)
    return high, (value - high.astype(F32)).astype(BF16)


def mul(a, b, dims):
    return lax.dot_general(a, b, dims, preferred_element_type=F32)


def mul3(a, b, dims):
    return mul(a[0], b[0], dims) + (mul(a[0], b[1], dims) + mul(a[1], b[0], dims))


def call(body, outs, args, scratch=()):
    vmem = pl.BlockSpec(memory_space=pltpu.VMEM)
    return pl.pallas_call(
        body,
        out_shape=outs,
        in_specs=[vmem] * len(args),
        out_specs=[vmem] * len(outs),
        scratch_shapes=list(scratch),
        cost_estimate=pl.CostEstimate(flops=0, bytes_accessed=0, transcendentals=0),
        compiler_params=pltpu.CompilerParams(vmem_limit_bytes=40 * 2**20),
    )(*args)


def shaped(shape, dtype=F32):
    return jax.ShapeDtypeStruct(shape, dtype)


def cent_body(mine_ref, theirs_ref, high_ref, low_ref, sq_ref):
    half = mine_ref.shape[0]
    for i, ref in enumerate((mine_ref, theirs_ref)):
        for at in range(0, half, 128):
            to = pl.ds(i * half + at, 128)
            value = ref[pl.ds(at, 128)]
            high_ref[to], low_ref[to] = halves(value)
            total = jnp.sum(value * value, axis=1, keepdims=True)
            sq_ref[:, to] = jnp.broadcast_to(total, (128, 128)).T[:8]


def split_cent(mine, theirs):
    half, width = mine.shape
    pair = [shaped((2 * half, width), BF16)] * 2
    return call(cent_body, pair + [shaped((8, 2 * half))], (mine, theirs))


def kernel_rows(high, low, row_sq, cent_refs, put):
    cent_high, cent_low, cent_sq = cent_refs
    scale = -4.0 / math.sqrt(cent_high.shape[1])
    for at in range(0, cent_high.shape[0], 256):
        to = pl.ds(at, 256)
        ch, cl = cent_high[to], cent_low[to]
        crossed = mul(high, ch, NT) + (mul(high, cl, NT) + mul(low, ch, NT) + mul(low, cl, NT))
        dist_sq = row_sq + cent_sq[0:1, to] - 2.0 * crossed
        put(to, halves(jnp.exp(jnp.sqrt(dist_sq + 1.0) * scale)))


def fill(refs, high_ref, low_ref, sq_ref):
    at = 0
    for ref in refs:
        to = pl.ds(at, ref.shape[0])
        value = ref[...]
        high_ref[to], low_ref[to] = halves(value)
        sq_ref[to] = jnp.broadcast_to(jnp.sum(value * value, axis=1, keepdims=True), (ref.shape[0], 128))
        at += ref.shape[0]


def own_body(own, c_high, c_low, c_sq, own_high, own_low, high, low, row_sq):
    fill((own,), high, low, row_sq)

    def put(to, pair):
        own_high[:, to], own_low[:, to] = pair

    kernel_rows(high[...], low[...], row_sq[:, 0:1], (c_high, c_low, c_sq), put)


def row_scratch(rows, width):
    return [pltpu.VMEM((rows, width), BF16)] * 2 + [pltpu.VMEM((rows, 128), F32)]


def own_kernels(own, cent):
    rows, width = own.shape
    wide = cent[0].shape[0]
    return call(
        own_body,
        [shaped((rows, wide), BF16)] * 2,
        (own, *cent),
        scratch=row_scratch(rows, width),
    )


def near_body(x, y, c_high, c_low, c_sq, own_high, own_low, near_high, near_low, high, low, row_sq):
    rows = x.shape[0]
    fill((x, y), high, low, row_sq)
    near_high[pl.ds(rows, rows)] = own_high[...]
    near_low[pl.ds(rows, rows)] = own_low[...]

    def put(to, pair):
        for ref, value in zip((near_high, near_low), pair):
            ref[pl.ds(0, rows), to] = value[:rows]
            ref[pl.ds(2 * rows, rows), to] = value[rows:]

    kernel_rows(high[...], low[...], row_sq[:, 0:1], (c_high, c_low, c_sq), put)


def near_kernels(x, y, cent, own):
    rows, width = x.shape
    wide = cent[0].shape[0]
    return call(
        near_body,
        [shaped((3 * rows, wide), BF16)] * 2,
        (x, y, *cent, *own),
        scratch=row_scratch(2 * rows, width),
    )


def share(w_refs, cols, k_refs, rows):
    half = w_refs[0].shape[1]
    total = None
    for i, ref in enumerate(w_refs):
        kept = pl.ds(i * half, half)
        part = mul3(halves(ref[cols]), (k_refs[0][rows, kept], k_refs[1][rows, kept]), NT)
        total = part if total is None else total + part
    return total


def stays(rows):
    return pl.ds(rows, 2 * rows), pl.ds(0, 2 * rows)


def goes(rows):
    return pl.ds(0, 2 * rows), pl.ds(rows, 2 * rows)


def keep_body(edges, rows, w0, w1, running, targets, near_high, near_low, *kept):
    for i, (a, b) in enumerate(edges):
        cols = pl.ds(a, b - a)
        value = share((w0, w1), cols, (near_high, near_low), stays(rows)[i % 2])
        own = slice(0, rows) if i % 2 == 0 else slice(rows, 2 * rows)
        other = slice(rows, 2 * rows) if i % 2 == 0 else slice(0, rows)
        kept[i][:, own] = value[:, own] + (running[cols] - targets[cols])
        kept[i][:, other] = value[:, other]


def keep_shares(edges, w0, w1, running, targets, near):
    rows = running.shape[1]
    outs = [shaped((b - a, 2 * rows)) for a, b in edges]
    return call(
        functools.partial(keep_body, edges, rows), outs, (w0, w1, running, targets, *near)
    )


def far_body(edges, block, c_high, c_low, c_sq, near_high, near_low, w0, w1, *rest):
    outs, (high, low, row_sq) = rest[:-3], rest[-3:]
    far_high, far_low, sent = outs[0], outs[1], outs[2:]
    rows = low.shape[0]
    fill((block,), high, low, row_sq)
    for far, near in ((far_high, near_high), (far_low, near_low)):
        far[pl.ds(0, rows)] = near[pl.ds(0, rows)]
        far[pl.ds(2 * rows, rows)] = near[pl.ds(2 * rows, rows)]

    def put(to, pair):
        far_high[pl.ds(rows, rows), to], far_low[pl.ds(rows, rows), to] = pair

    kernel_rows(high[...], low[...], row_sq[:, 0:1], (c_high, c_low, c_sq), put)
    for i, (a, b) in enumerate(edges):
        sent[i][...] = share((w0, w1), pl.ds(a, b - a), (far_high, far_low), goes(rows)[i % 2])


def far_kernels(edges, block, cent, near, w0, w1):
    rows, width = block.shape
    wide = cent[0].shape[0]
    outs = [shaped(near[0].shape, BF16)] * 2 + [shaped((b - a, 2 * rows)) for a, b in edges]
    out = call(
        functools.partial(far_body, edges),
        outs,
        (block, *cent, *near, w0, w1),
        scratch=row_scratch(rows, width),
    )
    return out[:2], out[2:]


def send_body(edges, rows, w0, w1, far_high, far_low, *sent):
    for i, (a, b) in enumerate(edges):
        sent[i][...] = share((w0, w1), pl.ds(a, b - a), (far_high, far_low), goes(rows)[i % 2])


def send_shares(edges, w0, w1, far):
    rows = far[0].shape[0] // 3
    outs = [shaped((b - a, 2 * rows)) for a, b in edges]
    return call(functools.partial(send_body, edges, rows), outs, (w0, w1, *far))


PARTS = 3


def blocks(size, count):
    step = -(-size // count // 8) * 8
    return [(at, min(size, at + step)) for at in range(0, size, step)]


def grad_body(factor, full_a, full_b, other_a, other_b, near_high, near_low, far_high, far_low, here, *gone):
    rows, half = full_a.shape[1] // 2, here.shape[1]
    at = 0
    for i, (full, other) in enumerate(((full_a, other_a), (full_b, other_b))):
        to = pl.ds(at, full.shape[0])
        at += full.shape[0]
        full_pair, other_pair = halves(full[...]), halves(other[...])
        stay, go = stays(rows)[i], goes(rows)[i]
        for away, cols in ((True, pl.ds(half, half)), (False, pl.ds(0, half))):
            value = factor * (
                mul3(full_pair, (near_high[stay, cols], near_low[stay, cols]), NN)
                + mul3(other_pair, (far_high[go, cols], far_low[go, cols]), NN)
            )
            if not away:
                here[to] = value
                continue
            start, end = at - full.shape[0], at
            for ref, (low, high) in zip(gone, blocks(here.shape[0], PARTS)):
                low_at, high_at = max(low, start), min(high, end)
                if low_at < high_at:
                    ref[pl.ds(low_at - low, high_at - low_at)] = value[low_at - start : high_at - start]


def grad_parts(factor, full, other, near, far):
    cols, half = full[0].shape[0] + full[1].shape[0], near[0].shape[1] // 2
    outs = [shaped((cols, half))] + [shaped((b - a, half)) for a, b in blocks(cols, PARTS)]
    out = call(functools.partial(grad_body, factor), outs, (*full, *other, *near, *far))
    return out[1:], out[0]


def pass_line(value, pairs):
    return lax.ppermute(value, "col", pairs)


BESIDE = [(0, 1), (1, 0), (2, 3), (3, 2)]
ACROSS = [(0, 3), (3, 0), (1, 2), (2, 1)]


def add_body(*refs):
    count = len(refs) // 3
    for i in range(count):
        refs[2 * count + i][...] = refs[i][...] + refs[count + i][...]


def add(many, more):
    return call(add_body, [shaped(a.shape) for a in many], (*many, *more))


def turn_body(*refs):
    for a, b, out in zip(refs[0:2], refs[2:4], refs[4:6]):
        rows = a.shape[1] // 2
        left, right = pl.ds(0, rows), pl.ds(rows, rows)
        out[:, left] = a[:, left] + b[:, right]
        out[:, right] = a[:, right] + b[:, left]


def turn(many, more):
    return call(turn_body, [shaped(a.shape) for a in many], (*many, *more))


def split_body(here, *refs):
    parts = blocks(here.shape[0], PARTS)
    gone, outs = refs[: len(parts)], refs[len(parts) :]
    count = len(outs) // 2
    pieces = blocks(here.shape[0], count)
    place = lax.axis_index("col")
    ends = (place == 0) | (place == 3)
    quarter = here.shape[1] // 2
    left, right = pl.ds(0, quarter), pl.ds(quarter, quarter)

    def put(kept, sent):
        for ref, (a, b) in zip(gone, parts):
            for i, (low, high) in enumerate(pieces):
                at, end = max(a, low), min(b, high)
                if at < end:
                    of, part, to = (pl.ds(at - n, end - at) for n in (0, a, low))
                    outs[i][to] = here[of, sent] + ref[part, sent]
                    outs[count + i][to] = here[of, kept] + ref[part, kept]

    pl.when(ends)(lambda: put(left, right))
    pl.when(~ends)(lambda: put(right, left))


def split(count, here, gone):
    rows, half = here.shape
    outs = [shaped((b - a, half // 2)) for a, b in blocks(rows, count)] * 2
    out = call(split_body, outs, (here, *gone))
    return out[: len(out) // 2], out[len(out) // 2 :]


def join_body(a, b, out):
    place = lax.axis_index("col")
    ends = (place == 0) | (place == 3)
    quarter = a.shape[1]
    left, right = pl.ds(0, quarter), pl.ds(quarter, quarter)

    def put(mine, other):
        out[:, mine] = a[...]
        out[:, other] = b[...]

    pl.when(ends)(lambda: put(left, right))
    pl.when(~ends)(lambda: put(right, left))


def join(a, b):
    return call(join_body, [shaped((a.shape[0], 2 * a.shape[1]))], (a, b))[0]


def cut(out):
    edges, at = [], 0
    for part in ROUNDS + (1.0,):
        left = out - at
        both = left if part == 1.0 else min(left, round(out * part / 16) * 16)
        first = -(-both // 16) * 8
        edges += [(at, at + first), (at + first, at + both)]
        at += both
    return edges


def hop(value, second):
    pairs = []
    for chip in range(4):
        for core in range(2):
            flip = 1 if core == second else 2
            pairs.append((chip * 2 + core, (chip ^ flip) * 2 + core))
    return lax.ppermute(value, ("chip", "core"), pairs)


def square(batch, running_t, targets_t, centers, weights_t, factor):
    rows, out = batch.shape[0], weights_t.shape[0]
    edges = cut(out)
    rounds = len(edges) // 2
    line = Line()
    block_x = hop(batch, 0)
    block_y = hop(batch, 1)
    cent_theirs = swap(centers, "core")
    w0, w1 = weights_t, swap(weights_t, "core")
    cent = line(split_cent, centers, cent_theirs)
    own = line(own_kernels, batch, cent)
    block = hop(block_x, 1)
    near = line(near_kernels, block_x, block_y, cent, own)
    far, sent = line(lambda *a: far_kernels(edges[:2], *a), block, cent, near, w0, w1)

    def both(pair, step):
        return [hop(pair[i], (i + step) % 2) for i in (0, 1)]

    coming, crossing = [None] * rounds, [None] * rounds
    partial, full, other, gone, here = ([None] * rounds for _ in range(5))
    beside, mine, across, total, back, whole = [], [], [], [], [], []

    def do_partial(r):
        partial[r] = line(add, kept[2 * r : 2 * r + 2], coming[r])
        crossing[r] = both(partial[r], 1)

    def do_full(r):
        full[r] = line(turn, partial[r], crossing[r])
        other[r] = both(full[r], 0)

    def do_grad(r):
        gone[r], here[r] = line(lambda *a: grad_parts(factor, *a), full[r], other[r], near, far)
        gone[r] = [swap(part, "core") for part in gone[r]]

    def do_owned(r):
        sends, keeps = line(lambda *a: split(LINE_PIECES[r], *a), here[r], gone[r])
        mine.extend(keeps)
        beside.extend(pass_line(value, BESIDE) for value in sends)

    def do_mine(i):
        (mine[i],) = line(add, [mine[i]], [beside[i]])
        across.append(pass_line(mine[i], ACROSS))

    def do_total(i):
        (value,) = line(add, [mine[i]], [across[i]])
        total.append(value)
        back.append(pass_line(value, BESIDE))

    def do_whole(i):
        whole.append(line(join, total[i], back[i]))

    sent = list(sent) + list(line(lambda *a: send_shares(edges[2:], *a), w0, w1, far))
    coming = [both(sent[2 * r : 2 * r + 2], 0) for r in range(rounds)]
    kept = line(lambda *a: keep_shares(edges, *a), w0, w1, running_t, targets_t, near)
    steps = dict(P=do_partial, F=do_full, G=do_grad, O=do_owned, M=do_mine, T=do_total, D=do_whole)
    for step in " ".join(STEPS).split():
        steps[step[0]](int(step[1]))

    gradient = jnp.concatenate(whole)
    mine_rows = (slice(0, rows), slice(rows, None))
    residual = jnp.concatenate([f[i][:, mine_rows[i]] for f in full for i in (0, 1)])
    return gradient, residual


def any_plane(batch, running_t, targets_t, centers, weights_t, factor):
    def dot(a, b, dims, precision):
        return lax.dot_general(a, b, dims, precision=precision, preferred_element_type=F32)

    rows_here, chips = batch.shape[0], lax.axis_size("chip")
    half, out = centers.shape[0], weights_t.shape[0]
    cent = jnp.concatenate([centers, swap(centers, "core")], axis=0)
    weight = jnp.concatenate([weights_t, swap(weights_t, "core")], axis=1)
    rows = lax.all_gather(batch, "chip", axis=0, tiled=True)
    row_sq = jnp.sum(rows * rows, axis=1, keepdims=True)
    dist_sq = row_sq + jnp.sum(cent * cent, axis=1)[None, :] - 2.0 * dot(rows, cent, NT, HIGHEST)
    kernel = jnp.exp(-jnp.sqrt(dist_sq + 1.0) / (math.sqrt(rows.shape[1]) / 4.0))
    shares = dot(weight, kernel, NT, HIGH).reshape(out, chips, rows_here).transpose(1, 0, 2)
    residual = running_t - targets_t + lax.psum_scatter(shares, "chip", scatter_dimension=0, tiled=False)
    moved = lax.all_gather(residual, "chip", axis=0, tiled=False)
    moved = moved.transpose(1, 0, 2).reshape(out, chips * rows_here)
    gradient = dot(moved, kernel, NN, HIGH) * factor
    owned = gradient[:, :half] + swap(gradient[:, half:], "core")
    return lax.psum(owned, "col"), residual


def per_device(batch, running, targets, centers, weights):
    chips, depth = lax.axis_size("chip"), lax.axis_size("col")
    factor = 1.0 / math.sqrt(batch.shape[0] * chips * 2 * depth)
    plane = square if (chips, depth) == (4, 4) else any_plane
    gradient, residual = plane(batch, running.T, targets.T, centers, weights.T, factor)
    return gradient.T, residual.T


def solution(mesh):
    owners, depth = mesh.shape["row"], mesh.shape["col"]
    split = Mesh(mesh.devices.reshape(owners // 2, 2, depth), ("chip", "core", "col"))
    everywhere = P(("chip", "core", "col"), None)
    owned = P(("chip", "core"), None)
    return jax.shard_map(
        per_device,
        mesh=split,
        in_specs=(everywhere, everywhere, everywhere, owned, owned),
        out_specs=(owned, everywhere),
        check_vma=False,
    )
```

```python
import functools
import math

import jax
import jax.numpy as jnp
from jax import lax
from jax.experimental import pallas as pl
from jax.experimental.pallas import tpu as pltpu
from jax.sharding import Mesh, PartitionSpec as P

HIGHEST = lax.Precision.HIGHEST
HIGH = lax.Precision.HIGH
ROUNDS = (0.48,)
STEPS = ("P0 P1 F0 F1", "G0 O0 G1 O1", "M0 T0 M1 M2", "T1 D0 T2 D1", "D2")
LINE_PIECES = (1,2,)
BF16, F32 = jnp.bfloat16, jnp.float32
NT = (((1,), (1,)), ((), ()))
NN = (((1,), (0,)), ((), ()))


def swap(value, axis, flip=1):
    size = lax.axis_size(axis)
    return lax.ppermute(value, axis, [(i, i ^ flip) for i in range(size)])


class Line:
    def __init__(self):
        self.last = None

    def hold(self, args):
        if self.last is None:
            return args
        return lax.optimization_barrier((args, self.last))[0]

    def __call__(self, step, *args):
        out = step(*self.hold(args))
        self.last = jax.tree.leaves(out)[0]
        return out


def halves(value):
    high = value.astype(BF16)
    return high, (value - high.astype(F32)).astype(BF16)


def mul(a, b, dims):
    return lax.dot_general(a, b, dims, preferred_element_type=F32)


def mul3(a, b, dims):
    return mul(a[0], b[0], dims) + (mul(a[0], b[1], dims) + mul(a[1], b[0], dims))


def call(body, outs, args, scratch=()):
    vmem = pl.BlockSpec(memory_space=pltpu.VMEM)
    return pl.pallas_call(
        body,
        out_shape=outs,
        in_specs=[vmem] * len(args),
        out_specs=[vmem] * len(outs),
        scratch_shapes=list(scratch),
        cost_estimate=pl.CostEstimate(flops=0, bytes_accessed=0, transcendentals=0),
        compiler_params=pltpu.CompilerParams(vmem_limit_bytes=40 * 2**20),
    )(*args)


def shaped(shape, dtype=F32):
    return jax.ShapeDtypeStruct(shape, dtype)


def cent_body(mine_ref, theirs_ref, high_ref, low_ref, sq_ref):
    half = mine_ref.shape[0]
    for i, ref in enumerate((mine_ref, theirs_ref)):
        for at in range(0, half, 128):
            to = pl.ds(i * half + at, 128)
            value = ref[pl.ds(at, 128)]
            high_ref[to], low_ref[to] = halves(value)
            total = jnp.sum(value * value, axis=1, keepdims=True)
            sq_ref[:, to] = jnp.broadcast_to(total, (128, 128)).T[:8]


def split_cent(mine, theirs):
    half, width = mine.shape
    pair = [shaped((2 * half, width), BF16)] * 2
    return call(cent_body, pair + [shaped((8, 2 * half))], (mine, theirs))


def kernel_rows(high, low, row_sq, cent_refs, put):
    cent_high, cent_low, cent_sq = cent_refs
    scale = -4.0 / math.sqrt(cent_high.shape[1])
    for at in range(0, cent_high.shape[0], 256):
        to = pl.ds(at, 256)
        ch, cl = cent_high[to], cent_low[to]
        crossed = mul(high, ch, NT) + (mul(high, cl, NT) + mul(low, ch, NT) + mul(low, cl, NT))
        dist_sq = row_sq + cent_sq[0:1, to] - 2.0 * crossed
        put(to, halves(jnp.exp(jnp.sqrt(dist_sq + 1.0) * scale)))


def fill(refs, high_ref, low_ref, sq_ref):
    at = 0
    for ref in refs:
        to = pl.ds(at, ref.shape[0])
        value = ref[...]
        high_ref[to], low_ref[to] = halves(value)
        sq_ref[to] = jnp.broadcast_to(jnp.sum(value * value, axis=1, keepdims=True), (ref.shape[0], 128))
        at += ref.shape[0]


def own_body(own, c_high, c_low, c_sq, own_high, own_low, high, low, row_sq):
    fill((own,), high, low, row_sq)

    def put(to, pair):
        own_high[:, to], own_low[:, to] = pair

    kernel_rows(high[...], low[...], row_sq[:, 0:1], (c_high, c_low, c_sq), put)


def row_scratch(rows, width):
    return [pltpu.VMEM((rows, width), BF16)] * 2 + [pltpu.VMEM((rows, 128), F32)]


def own_kernels(own, cent):
    rows, width = own.shape
    wide = cent[0].shape[0]
    return call(
        own_body,
        [shaped((rows, wide), BF16)] * 2,
        (own, *cent),
        scratch=row_scratch(rows, width),
    )


def share(w_refs, cols, k_refs, rows):
    half = w_refs[0].shape[1]
    total = None
    for i, ref in enumerate(w_refs):
        kept = pl.ds(i * half, half)
        part = mul3(halves(ref[cols]), (k_refs[0][rows, kept], k_refs[1][rows, kept]), NT)
        total = part if total is None else total + part
    return total


def stays(rows):
    return pl.ds(rows, 2 * rows), pl.ds(0, 2 * rows)


def goes(rows):
    return pl.ds(0, 2 * rows), pl.ds(rows, 2 * rows)


def keep_body(edges, rows, w0, w1, running, targets, near_high, near_low, *kept):
    for i, (a, b) in enumerate(edges):
        cols = pl.ds(a, b - a)
        value = share((w0, w1), cols, (near_high, near_low), stays(rows)[i % 2])
        own = slice(0, rows) if i % 2 == 0 else slice(rows, 2 * rows)
        other = slice(rows, 2 * rows) if i % 2 == 0 else slice(0, rows)
        kept[i][:, own] = value[:, own] + (running[cols] - targets[cols])
        kept[i][:, other] = value[:, other]


def keep_shares(edges, w0, w1, running, targets, near):
    rows = running.shape[1]
    outs = [shaped((b - a, 2 * rows)) for a, b in edges]
    return call(
        functools.partial(keep_body, edges, rows), outs, (w0, w1, running, targets, *near)
    )


def far_body(edges, block_y, block_far, c_high, c_low, c_sq, *rest):
    pairs, (w0, w1), rest = rest[:4], rest[4:6], rest[6:]
    near_high, near_low, far_high, far_low, *sent = rest[:-3]
    high, low, row_sq = rest[-3:]
    rows = block_y.shape[0]
    left, middle, right = pl.ds(0, rows), pl.ds(rows, rows), pl.ds(2 * rows, rows)
    fill((block_y, block_far), high, low, row_sq)
    for near, far, own, x in zip((near_high, near_low), (far_high, far_low), pairs[:2], pairs[2:]):
        near[left] = x[...]
        near[middle] = own[...]
        far[left] = x[...]

    def put(to, pair):
        for near, far, value in zip((near_high, near_low), (far_high, far_low), pair):
            near[right, to] = value[:rows]
            far[right, to] = value[:rows]
            far[middle, to] = value[rows:]

    kernel_rows(high[...], low[...], row_sq[:, 0:1], (c_high, c_low, c_sq), put)
    for i, (a, b) in enumerate(edges):
        sent[i][...] = share((w0, w1), pl.ds(a, b - a), (far_high, far_low), goes(rows)[i % 2])


def far_kernels(edges, block_y, block_far, cent, own, x, w0, w1):
    rows, width = block_y.shape
    outs = [shaped((3 * rows, cent[0].shape[0]), BF16)] * 4
    outs += [shaped((b - a, 2 * rows)) for a, b in edges]
    out = call(
        functools.partial(far_body, edges),
        outs,
        (block_y, block_far, *cent, *own, *x, w0, w1),
        scratch=row_scratch(2 * rows, width),
    )
    return out[:2], out[2:4], out[4:]


def send_body(edges, rows, w0, w1, far_high, far_low, *sent):
    for i, (a, b) in enumerate(edges):
        sent[i][...] = share((w0, w1), pl.ds(a, b - a), (far_high, far_low), goes(rows)[i % 2])


def send_shares(edges, w0, w1, far):
    rows = far[0].shape[0] // 3
    outs = [shaped((b - a, 2 * rows)) for a, b in edges]
    return call(functools.partial(send_body, edges, rows), outs, (w0, w1, *far))


PARTS = 3


def blocks(size, count):
    step = -(-size // count // 8) * 8
    return [(at, min(size, at + step)) for at in range(0, size, step)]


def grad_body(factor, full_a, full_b, other_a, other_b, near_high, near_low, far_high, far_low, here, *gone):
    rows, half = full_a.shape[1] // 2, here.shape[1]
    at = 0
    for i, (full, other) in enumerate(((full_a, other_a), (full_b, other_b))):
        to = pl.ds(at, full.shape[0])
        at += full.shape[0]
        full_pair, other_pair = halves(full[...]), halves(other[...])
        stay, go = stays(rows)[i], goes(rows)[i]
        for away, cols in ((True, pl.ds(half, half)), (False, pl.ds(0, half))):
            value = factor * (
                mul3(full_pair, (near_high[stay, cols], near_low[stay, cols]), NN)
                + mul3(other_pair, (far_high[go, cols], far_low[go, cols]), NN)
            )
            if not away:
                here[to] = value
                continue
            start, end = at - full.shape[0], at
            for ref, (low, high) in zip(gone, blocks(here.shape[0], PARTS)):
                low_at, high_at = max(low, start), min(high, end)
                if low_at < high_at:
                    ref[pl.ds(low_at - low, high_at - low_at)] = value[low_at - start : high_at - start]


def grad_parts(factor, full, other, near, far):
    cols, half = full[0].shape[0] + full[1].shape[0], near[0].shape[1] // 2
    outs = [shaped((cols, half))] + [shaped((b - a, half)) for a, b in blocks(cols, PARTS)]
    out = call(functools.partial(grad_body, factor), outs, (*full, *other, *near, *far))
    return out[1:], out[0]


def pass_line(value, pairs):
    return lax.ppermute(value, "col", pairs)


BESIDE = [(0, 1), (1, 0), (2, 3), (3, 2)]
ACROSS = [(0, 3), (3, 0), (1, 2), (2, 1)]


def add_body(*refs):
    count = len(refs) // 3
    for i in range(count):
        refs[2 * count + i][...] = refs[i][...] + refs[count + i][...]


def add(many, more):
    return call(add_body, [shaped(a.shape) for a in many], (*many, *more))


def turn_body(*refs):
    for a, b, out in zip(refs[0:2], refs[2:4], refs[4:6]):
        rows = a.shape[1] // 2
        left, right = pl.ds(0, rows), pl.ds(rows, rows)
        out[:, left] = a[:, left] + b[:, right]
        out[:, right] = a[:, right] + b[:, left]


def turn(many, more):
    return call(turn_body, [shaped(a.shape) for a in many], (*many, *more))


def split_body(here, *refs):
    parts = blocks(here.shape[0], PARTS)
    gone, outs = refs[: len(parts)], refs[len(parts) :]
    count = len(outs) // 2
    pieces = blocks(here.shape[0], count)
    place = lax.axis_index("col")
    ends = (place == 0) | (place == 3)
    quarter = here.shape[1] // 2
    left, right = pl.ds(0, quarter), pl.ds(quarter, quarter)

    def put(kept, sent):
        for ref, (a, b) in zip(gone, parts):
            for i, (low, high) in enumerate(pieces):
                at, end = max(a, low), min(b, high)
                if at < end:
                    of, part, to = (pl.ds(at - n, end - at) for n in (0, a, low))
                    outs[i][to] = here[of, sent] + ref[part, sent]
                    outs[count + i][to] = here[of, kept] + ref[part, kept]

    pl.when(ends)(lambda: put(left, right))
    pl.when(~ends)(lambda: put(right, left))


def split(count, here, gone):
    rows, half = here.shape
    outs = [shaped((b - a, half // 2)) for a, b in blocks(rows, count)] * 2
    out = call(split_body, outs, (here, *gone))
    return out[: len(out) // 2], out[len(out) // 2 :]


def join_body(a, b, out):
    place = lax.axis_index("col")
    ends = (place == 0) | (place == 3)
    quarter = a.shape[1]
    left, right = pl.ds(0, quarter), pl.ds(quarter, quarter)

    def put(mine, other):
        out[:, mine] = a[...]
        out[:, other] = b[...]

    pl.when(ends)(lambda: put(left, right))
    pl.when(~ends)(lambda: put(right, left))


def join(a, b):
    return call(join_body, [shaped((a.shape[0], 2 * a.shape[1]))], (a, b))[0]


def cut(out):
    edges, at = [], 0
    for part in ROUNDS + (1.0,):
        left = out - at
        both = left if part == 1.0 else min(left, round(out * part / 16) * 16)
        first = -(-both // 16) * 8
        edges += [(at, at + first), (at + first, at + both)]
        at += both
    return edges


def hop(value, second):
    pairs = []
    for chip in range(4):
        for core in range(2):
            flip = 1 if core == second else 2
            pairs.append((chip * 2 + core, (chip ^ flip) * 2 + core))
    return lax.ppermute(value, ("chip", "core"), pairs)


def square(batch, running_t, targets_t, centers, weights_t, factor):
    rows, out = batch.shape[0], weights_t.shape[0]
    edges = cut(out)
    rounds = len(edges) // 2
    line = Line()
    block_x = hop(batch, 0)
    cent_theirs = swap(centers, "core")
    w0, w1 = weights_t, swap(weights_t, "core")
    cent = line(split_cent, centers, cent_theirs)
    own = line(own_kernels, batch, cent)
    block_far = hop(block_x, 1)
    block_y = hop(lax.optimization_barrier((batch, block_x))[0], 1)
    x = line(own_kernels, block_x, cent)
    near, far, sent = line(
        lambda *a: far_kernels(edges[:2], *a), block_y, block_far, cent, own, x, w0, w1
    )

    def both(pair, step):
        return [hop(pair[i], (i + step) % 2) for i in (0, 1)]

    coming, crossing = [None] * rounds, [None] * rounds
    partial, full, other, gone, here = ([None] * rounds for _ in range(5))
    beside, mine, across, total, back, whole = [], [], [], [], [], []

    def do_partial(r):
        partial[r] = line(add, kept[2 * r : 2 * r + 2], coming[r])
        crossing[r] = both(partial[r], 1)

    def do_full(r):
        full[r] = line(turn, partial[r], crossing[r])
        other[r] = both(full[r], 0)

    def do_grad(r):
        gone[r], here[r] = line(lambda *a: grad_parts(factor, *a), full[r], other[r], near, far)
        gone[r] = [swap(part, "core") for part in gone[r]]

    def do_owned(r):
        sends, keeps = line(lambda *a: split(LINE_PIECES[r], *a), here[r], gone[r])
        mine.extend(keeps)
        beside.extend(pass_line(value, BESIDE) for value in sends)

    def do_mine(i):
        (mine[i],) = line(add, [mine[i]], [beside[i]])
        across.append(pass_line(mine[i], ACROSS))

    def do_total(i):
        (value,) = line(add, [mine[i]], [across[i]])
        total.append(value)
        back.append(pass_line(value, BESIDE))

    def do_whole(i):
        whole.append(line(join, total[i], back[i]))

    sent = list(sent) + list(line(lambda *a: send_shares(edges[2:], *a), w0, w1, far))
    coming = [both(sent[2 * r : 2 * r + 2], 0) for r in range(rounds)]
    kept = line(lambda *a: keep_shares(edges, *a), w0, w1, running_t, targets_t, near)
    steps = dict(P=do_partial, F=do_full, G=do_grad, O=do_owned, M=do_mine, T=do_total, D=do_whole)
    for step in " ".join(STEPS).split():
        steps[step[0]](int(step[1]))

    gradient = jnp.concatenate(whole)
    mine_rows = (slice(0, rows), slice(rows, None))
    residual = jnp.concatenate([f[i][:, mine_rows[i]] for f in full for i in (0, 1)])
    return gradient, residual


def any_plane(batch, running_t, targets_t, centers, weights_t, factor):
    def dot(a, b, dims, precision):
        return lax.dot_general(a, b, dims, precision=precision, preferred_element_type=F32)

    rows_here, chips = batch.shape[0], lax.axis_size("chip")
    half, out = centers.shape[0], weights_t.shape[0]
    cent = jnp.concatenate([centers, swap(centers, "core")], axis=0)
    weight = jnp.concatenate([weights_t, swap(weights_t, "core")], axis=1)
    rows = lax.all_gather(batch, "chip", axis=0, tiled=True)
    row_sq = jnp.sum(rows * rows, axis=1, keepdims=True)
    dist_sq = row_sq + jnp.sum(cent * cent, axis=1)[None, :] - 2.0 * dot(rows, cent, NT, HIGHEST)
    kernel = jnp.exp(-jnp.sqrt(dist_sq + 1.0) / (math.sqrt(rows.shape[1]) / 4.0))
    shares = dot(weight, kernel, NT, HIGH).reshape(out, chips, rows_here).transpose(1, 0, 2)
    residual = running_t - targets_t + lax.psum_scatter(shares, "chip", scatter_dimension=0, tiled=False)
    moved = lax.all_gather(residual, "chip", axis=0, tiled=False)
    moved = moved.transpose(1, 0, 2).reshape(out, chips * rows_here)
    gradient = dot(moved, kernel, NN, HIGH) * factor
    owned = gradient[:, :half] + swap(gradient[:, half:], "core")
    return lax.psum(owned, "col"), residual


def per_device(batch, running, targets, centers, weights):
    chips, depth = lax.axis_size("chip"), lax.axis_size("col")
    factor = 1.0 / math.sqrt(batch.shape[0] * chips * 2 * depth)
    plane = square if (chips, depth) == (4, 4) else any_plane
    gradient, residual = plane(batch, running.T, targets.T, centers, weights.T, factor)
    return gradient.T, residual.T


def solution(mesh):
    owners, depth = mesh.shape["row"], mesh.shape["col"]
    split = Mesh(mesh.devices.reshape(owners // 2, 2, depth), ("chip", "core", "col"))
    everywhere = P(("chip", "core", "col"), None)
    owned = P(("chip", "core"), None)
    return jax.shard_map(
        per_device,
        mesh=split,
        in_specs=(everywhere, everywhere, everywhere, owned, owned),
        out_specs=(owned, everywhere),
        check_vma=False,
    )
```

```python
import functools
import math

import jax
import jax.numpy as jnp
from jax import lax
from jax.experimental import pallas as pl
from jax.experimental.pallas import tpu as pltpu
from jax.sharding import Mesh, PartitionSpec as P

HIGHEST = lax.Precision.HIGHEST
HIGH = lax.Precision.HIGH
ROUNDS = (0.32,0.336,)
STEPS = ("P0 P1 F0 P2", "F1 G0 O0 F2", "G1 M0 O1 G2", "T0 M1 O2 T1", "M2 D0 T2 D1", "D2")
LINE_PIECES = (1,1,1,)
BF16, F32 = jnp.bfloat16, jnp.float32
NT = (((1,), (1,)), ((), ()))
NN = (((1,), (0,)), ((), ()))


def swap(value, axis, flip=1):
    size = lax.axis_size(axis)
    return lax.ppermute(value, axis, [(i, i ^ flip) for i in range(size)])


class Line:
    def __init__(self):
        self.last = None

    def hold(self, args):
        if self.last is None:
            return args
        return lax.optimization_barrier((args, self.last))[0]

    def __call__(self, step, *args):
        out = step(*self.hold(args))
        self.last = jax.tree.leaves(out)[0]
        return out


def halves(value):
    high = value.astype(BF16)
    return high, (value - high.astype(F32)).astype(BF16)


def mul(a, b, dims):
    return lax.dot_general(a, b, dims, preferred_element_type=F32)


def mul3(a, b, dims):
    return mul(a[0], b[0], dims) + (mul(a[0], b[1], dims) + mul(a[1], b[0], dims))


def call(body, outs, args, scratch=()):
    vmem = pl.BlockSpec(memory_space=pltpu.VMEM)
    return pl.pallas_call(
        body,
        out_shape=outs,
        in_specs=[vmem] * len(args),
        out_specs=[vmem] * len(outs),
        scratch_shapes=list(scratch),
        cost_estimate=pl.CostEstimate(flops=0, bytes_accessed=0, transcendentals=0),
        compiler_params=pltpu.CompilerParams(vmem_limit_bytes=40 * 2**20),
    )(*args)


def shaped(shape, dtype=F32):
    return jax.ShapeDtypeStruct(shape, dtype)


def cent_body(mine_ref, theirs_ref, high_ref, low_ref, sq_ref):
    half = mine_ref.shape[0]
    for i, ref in enumerate((mine_ref, theirs_ref)):
        for at in range(0, half, 128):
            to = pl.ds(i * half + at, 128)
            value = ref[pl.ds(at, 128)]
            high_ref[to], low_ref[to] = halves(value)
            total = jnp.sum(value * value, axis=1, keepdims=True)
            sq_ref[:, to] = jnp.broadcast_to(total, (128, 128)).T[:8]


def split_cent(mine, theirs):
    half, width = mine.shape
    pair = [shaped((2 * half, width), BF16)] * 2
    return call(cent_body, pair + [shaped((8, 2 * half))], (mine, theirs))


def kernel_rows(high, low, row_sq, cent_refs, put):
    cent_high, cent_low, cent_sq = cent_refs
    scale = -4.0 / math.sqrt(cent_high.shape[1])
    for at in range(0, cent_high.shape[0], 256):
        to = pl.ds(at, 256)
        ch, cl = cent_high[to], cent_low[to]
        crossed = mul(high, ch, NT) + (mul(high, cl, NT) + mul(low, ch, NT) + mul(low, cl, NT))
        dist_sq = row_sq + cent_sq[0:1, to] - 2.0 * crossed
        put(to, halves(jnp.exp(jnp.sqrt(dist_sq + 1.0) * scale)))


def fill(refs, high_ref, low_ref, sq_ref):
    at = 0
    for ref in refs:
        to = pl.ds(at, ref.shape[0])
        value = ref[...]
        high_ref[to], low_ref[to] = halves(value)
        sq_ref[to] = jnp.broadcast_to(jnp.sum(value * value, axis=1, keepdims=True), (ref.shape[0], 128))
        at += ref.shape[0]


def own_body(own, c_high, c_low, c_sq, own_high, own_low, high, low, row_sq):
    fill((own,), high, low, row_sq)

    def put(to, pair):
        own_high[:, to], own_low[:, to] = pair

    kernel_rows(high[...], low[...], row_sq[:, 0:1], (c_high, c_low, c_sq), put)


def row_scratch(rows, width):
    return [pltpu.VMEM((rows, width), BF16)] * 2 + [pltpu.VMEM((rows, 128), F32)]


def own_kernels(own, cent):
    rows, width = own.shape
    wide = cent[0].shape[0]
    return call(
        own_body,
        [shaped((rows, wide), BF16)] * 2,
        (own, *cent),
        scratch=row_scratch(rows, width),
    )


def near_body(x, y, c_high, c_low, c_sq, own_high, own_low, near_high, near_low, high, low, row_sq):
    rows = x.shape[0]
    fill((x, y), high, low, row_sq)
    near_high[pl.ds(rows, rows)] = own_high[...]
    near_low[pl.ds(rows, rows)] = own_low[...]

    def put(to, pair):
        for ref, value in zip((near_high, near_low), pair):
            ref[pl.ds(0, rows), to] = value[:rows]
            ref[pl.ds(2 * rows, rows), to] = value[rows:]

    kernel_rows(high[...], low[...], row_sq[:, 0:1], (c_high, c_low, c_sq), put)


def near_kernels(x, y, cent, own):
    rows, width = x.shape
    wide = cent[0].shape[0]
    return call(
        near_body,
        [shaped((3 * rows, wide), BF16)] * 2,
        (x, y, *cent, *own),
        scratch=row_scratch(2 * rows, width),
    )


def share(w_refs, cols, k_refs, rows):
    half = w_refs[0].shape[1]
    total = None
    for i, ref in enumerate(w_refs):
        kept = pl.ds(i * half, half)
        part = mul3(halves(ref[cols]), (k_refs[0][rows, kept], k_refs[1][rows, kept]), NT)
        total = part if total is None else total + part
    return total


def stays(rows):
    return pl.ds(rows, 2 * rows), pl.ds(0, 2 * rows)


def goes(rows):
    return pl.ds(0, 2 * rows), pl.ds(rows, 2 * rows)


def keep_body(edges, rows, w0, w1, running, targets, near_high, near_low, *kept):
    for i, (a, b) in enumerate(edges):
        cols = pl.ds(a, b - a)
        value = share((w0, w1), cols, (near_high, near_low), stays(rows)[i % 2])
        own = slice(0, rows) if i % 2 == 0 else slice(rows, 2 * rows)
        other = slice(rows, 2 * rows) if i % 2 == 0 else slice(0, rows)
        kept[i][:, own] = value[:, own] + (running[cols] - targets[cols])
        kept[i][:, other] = value[:, other]


def keep_shares(edges, w0, w1, running, targets, near):
    rows = running.shape[1]
    outs = [shaped((b - a, 2 * rows)) for a, b in edges]
    return call(
        functools.partial(keep_body, edges, rows), outs, (w0, w1, running, targets, *near)
    )


def far_body(edges, block, c_high, c_low, c_sq, near_high, near_low, w0, w1, *rest):
    outs, (high, low, row_sq) = rest[:-3], rest[-3:]
    far_high, far_low, sent = outs[0], outs[1], outs[2:]
    rows = low.shape[0]
    fill((block,), high, low, row_sq)
    for far, near in ((far_high, near_high), (far_low, near_low)):
        far[pl.ds(0, rows)] = near[pl.ds(0, rows)]
        far[pl.ds(2 * rows, rows)] = near[pl.ds(2 * rows, rows)]

    def put(to, pair):
        far_high[pl.ds(rows, rows), to], far_low[pl.ds(rows, rows), to] = pair

    kernel_rows(high[...], low[...], row_sq[:, 0:1], (c_high, c_low, c_sq), put)
    for i, (a, b) in enumerate(edges):
        sent[i][...] = share((w0, w1), pl.ds(a, b - a), (far_high, far_low), goes(rows)[i % 2])


def far_kernels(edges, block, cent, near, w0, w1):
    rows, width = block.shape
    wide = cent[0].shape[0]
    outs = [shaped(near[0].shape, BF16)] * 2 + [shaped((b - a, 2 * rows)) for a, b in edges]
    out = call(
        functools.partial(far_body, edges),
        outs,
        (block, *cent, *near, w0, w1),
        scratch=row_scratch(rows, width),
    )
    return out[:2], out[2:]


def send_body(edges, rows, w0, w1, far_high, far_low, *sent):
    for i, (a, b) in enumerate(edges):
        sent[i][...] = share((w0, w1), pl.ds(a, b - a), (far_high, far_low), goes(rows)[i % 2])


def send_shares(edges, w0, w1, far):
    rows = far[0].shape[0] // 3
    outs = [shaped((b - a, 2 * rows)) for a, b in edges]
    return call(functools.partial(send_body, edges, rows), outs, (w0, w1, *far))


PARTS = 1


def blocks(size, count):
    step = -(-size // count // 8) * 8
    return [(at, min(size, at + step)) for at in range(0, size, step)]


def grad_body(factor, full_a, full_b, other_a, other_b, near_high, near_low, far_high, far_low, here, *gone):
    rows, half = full_a.shape[1] // 2, here.shape[1]
    at = 0
    for i, (full, other) in enumerate(((full_a, other_a), (full_b, other_b))):
        to = pl.ds(at, full.shape[0])
        at += full.shape[0]
        full_pair, other_pair = halves(full[...]), halves(other[...])
        stay, go = stays(rows)[i], goes(rows)[i]
        for away, cols in ((True, pl.ds(half, half)), (False, pl.ds(0, half))):
            value = factor * (
                mul3(full_pair, (near_high[stay, cols], near_low[stay, cols]), NN)
                + mul3(other_pair, (far_high[go, cols], far_low[go, cols]), NN)
            )
            if not away:
                here[to] = value
                continue
            start, end = at - full.shape[0], at
            for ref, (low, high) in zip(gone, blocks(here.shape[0], PARTS)):
                low_at, high_at = max(low, start), min(high, end)
                if low_at < high_at:
                    ref[pl.ds(low_at - low, high_at - low_at)] = value[low_at - start : high_at - start]


def grad_parts(factor, full, other, near, far):
    cols, half = full[0].shape[0] + full[1].shape[0], near[0].shape[1] // 2
    outs = [shaped((cols, half))] + [shaped((b - a, half)) for a, b in blocks(cols, PARTS)]
    out = call(functools.partial(grad_body, factor), outs, (*full, *other, *near, *far))
    return out[1:], out[0]


def pass_line(value, pairs):
    return lax.ppermute(value, "col", pairs)


BESIDE = [(0, 1), (1, 0), (2, 3), (3, 2)]
ACROSS = [(0, 3), (3, 0), (1, 2), (2, 1)]


def add_body(*refs):
    count = len(refs) // 3
    for i in range(count):
        refs[2 * count + i][...] = refs[i][...] + refs[count + i][...]


def add(many, more):
    return call(add_body, [shaped(a.shape) for a in many], (*many, *more))


def turn_body(*refs):
    for a, b, out in zip(refs[0:2], refs[2:4], refs[4:6]):
        rows = a.shape[1] // 2
        left, right = pl.ds(0, rows), pl.ds(rows, rows)
        out[:, left] = a[:, left] + b[:, right]
        out[:, right] = a[:, right] + b[:, left]


def turn(many, more):
    return call(turn_body, [shaped(a.shape) for a in many], (*many, *more))


def split_body(here, *refs):
    parts = blocks(here.shape[0], PARTS)
    gone, outs = refs[: len(parts)], refs[len(parts) :]
    count = len(outs) // 2
    pieces = blocks(here.shape[0], count)
    place = lax.axis_index("col")
    ends = (place == 0) | (place == 3)
    quarter = here.shape[1] // 2
    left, right = pl.ds(0, quarter), pl.ds(quarter, quarter)

    def put(kept, sent):
        for ref, (a, b) in zip(gone, parts):
            for i, (low, high) in enumerate(pieces):
                at, end = max(a, low), min(b, high)
                if at < end:
                    of, part, to = (pl.ds(at - n, end - at) for n in (0, a, low))
                    outs[i][to] = here[of, sent] + ref[part, sent]
                    outs[count + i][to] = here[of, kept] + ref[part, kept]

    pl.when(ends)(lambda: put(left, right))
    pl.when(~ends)(lambda: put(right, left))


def split(count, here, gone):
    rows, half = here.shape
    outs = [shaped((b - a, half // 2)) for a, b in blocks(rows, count)] * 2
    out = call(split_body, outs, (here, *gone))
    return out[: len(out) // 2], out[len(out) // 2 :]


def join_body(a, b, out):
    place = lax.axis_index("col")
    ends = (place == 0) | (place == 3)
    quarter = a.shape[1]
    left, right = pl.ds(0, quarter), pl.ds(quarter, quarter)

    def put(mine, other):
        out[:, mine] = a[...]
        out[:, other] = b[...]

    pl.when(ends)(lambda: put(left, right))
    pl.when(~ends)(lambda: put(right, left))


def join(a, b):
    return call(join_body, [shaped((a.shape[0], 2 * a.shape[1]))], (a, b))[0]


def cut(out):
    edges, at = [], 0
    for part in ROUNDS + (1.0,):
        left = out - at
        both = left if part == 1.0 else min(left, round(out * part / 16) * 16)
        first = -(-both // 16) * 8
        edges += [(at, at + first), (at + first, at + both)]
        at += both
    return edges


def hop(value, second):
    pairs = []
    for chip in range(4):
        for core in range(2):
            flip = 1 if core == second else 2
            pairs.append((chip * 2 + core, (chip ^ flip) * 2 + core))
    return lax.ppermute(value, ("chip", "core"), pairs)


def square(batch, running_t, targets_t, centers, weights_t, factor):
    rows, out = batch.shape[0], weights_t.shape[0]
    edges = cut(out)
    rounds = len(edges) // 2
    line = Line()
    block_x = hop(batch, 0)
    block_y = hop(batch, 1)
    cent_theirs = swap(centers, "core")
    w0, w1 = weights_t, swap(weights_t, "core")
    cent = line(split_cent, centers, cent_theirs)
    own = line(own_kernels, batch, cent)
    block = hop(block_x, 1)
    near = line(near_kernels, block_x, block_y, cent, own)
    far, sent = line(lambda *a: far_kernels(edges[:2], *a), block, cent, near, w0, w1)

    def both(pair, step):
        return [hop(pair[i], (i + step) % 2) for i in (0, 1)]

    coming, crossing = [None] * rounds, [None] * rounds
    partial, full, other, gone, here = ([None] * rounds for _ in range(5))
    beside, mine, across, total, back, whole = [], [], [], [], [], []

    def do_partial(r):
        partial[r] = line(add, kept[2 * r : 2 * r + 2], coming[r])
        crossing[r] = both(partial[r], 1)

    def do_full(r):
        full[r] = line(turn, partial[r], crossing[r])
        other[r] = both(full[r], 0)

    def do_grad(r):
        gone[r], here[r] = line(lambda *a: grad_parts(factor, *a), full[r], other[r], near, far)
        gone[r] = [swap(part, "core") for part in gone[r]]

    def do_owned(r):
        sends, keeps = line(lambda *a: split(LINE_PIECES[r], *a), here[r], gone[r])
        mine.extend(keeps)
        beside.extend(pass_line(value, BESIDE) for value in sends)

    def do_mine(i):
        (mine[i],) = line(add, [mine[i]], [beside[i]])
        across.append(pass_line(mine[i], ACROSS))

    def do_total(i):
        (value,) = line(add, [mine[i]], [across[i]])
        total.append(value)
        back.append(pass_line(value, BESIDE))

    def do_whole(i):
        whole.append(line(join, total[i], back[i]))

    sent = list(sent) + list(line(lambda *a: send_shares(edges[2:], *a), w0, w1, far))
    coming = [both(sent[2 * r : 2 * r + 2], 0) for r in range(rounds)]
    kept = line(lambda *a: keep_shares(edges, *a), w0, w1, running_t, targets_t, near)
    steps = dict(P=do_partial, F=do_full, G=do_grad, O=do_owned, M=do_mine, T=do_total, D=do_whole)
    for step in " ".join(STEPS).split():
        steps[step[0]](int(step[1]))

    gradient = jnp.concatenate(whole)
    mine_rows = (slice(0, rows), slice(rows, None))
    residual = jnp.concatenate([f[i][:, mine_rows[i]] for f in full for i in (0, 1)])
    return gradient, residual


def any_plane(batch, running_t, targets_t, centers, weights_t, factor):
    def dot(a, b, dims, precision):
        return lax.dot_general(a, b, dims, precision=precision, preferred_element_type=F32)

    rows_here, chips = batch.shape[0], lax.axis_size("chip")
    half, out = centers.shape[0], weights_t.shape[0]
    cent = jnp.concatenate([centers, swap(centers, "core")], axis=0)
    weight = jnp.concatenate([weights_t, swap(weights_t, "core")], axis=1)
    rows = lax.all_gather(batch, "chip", axis=0, tiled=True)
    row_sq = jnp.sum(rows * rows, axis=1, keepdims=True)
    dist_sq = row_sq + jnp.sum(cent * cent, axis=1)[None, :] - 2.0 * dot(rows, cent, NT, HIGHEST)
    kernel = jnp.exp(-jnp.sqrt(dist_sq + 1.0) / (math.sqrt(rows.shape[1]) / 4.0))
    shares = dot(weight, kernel, NT, HIGH).reshape(out, chips, rows_here).transpose(1, 0, 2)
    residual = running_t - targets_t + lax.psum_scatter(shares, "chip", scatter_dimension=0, tiled=False)
    moved = lax.all_gather(residual, "chip", axis=0, tiled=False)
    moved = moved.transpose(1, 0, 2).reshape(out, chips * rows_here)
    gradient = dot(moved, kernel, NN, HIGH) * factor
    owned = gradient[:, :half] + swap(gradient[:, half:], "core")
    return lax.psum(owned, "col"), residual


def per_device(batch, running, targets, centers, weights):
    chips, depth = lax.axis_size("chip"), lax.axis_size("col")
    factor = 1.0 / math.sqrt(batch.shape[0] * chips * 2 * depth)
    plane = square if (chips, depth) == (4, 4) else any_plane
    gradient, residual = plane(batch, running.T, targets.T, centers, weights.T, factor)
    return gradient.T, residual.T


def solution(mesh):
    owners, depth = mesh.shape["row"], mesh.shape["col"]
    split = Mesh(mesh.devices.reshape(owners // 2, 2, depth), ("chip", "core", "col"))
    everywhere = P(("chip", "core", "col"), None)
    owned = P(("chip", "core"), None)
    return jax.shard_map(
        per_device,
        mesh=split,
        in_specs=(everywhere, everywhere, everywhere, owned, owned),
        out_specs=(owned, everywhere),
        check_vma=False,
    )
```

```python
import functools
import math

import jax
import jax.numpy as jnp
from jax import lax
from jax.experimental import pallas as pl
from jax.experimental.pallas import tpu as pltpu
from jax.sharding import Mesh, PartitionSpec as P

HIGHEST = lax.Precision.HIGHEST
HIGH = lax.Precision.HIGH
ROUNDS = (0.48,)
STEPS = ("P0 P1 F0 F1", "G0 O0 G1 O1", "M0 M1 T0 D0", "T1 D1")
LINE_PIECES = (1,1,)
BF16, F32 = jnp.bfloat16, jnp.float32
NT = (((1,), (1,)), ((), ()))
NN = (((1,), (0,)), ((), ()))


def swap(value, axis, flip=1):
    size = lax.axis_size(axis)
    return lax.ppermute(value, axis, [(i, i ^ flip) for i in range(size)])


class Line:
    def __init__(self):
        self.last = None

    def hold(self, args):
        if self.last is None:
            return args
        return lax.optimization_barrier((args, self.last))[0]

    def __call__(self, step, *args):
        out = step(*self.hold(args))
        self.last = jax.tree.leaves(out)[0]
        return out


def halves(value):
    high = value.astype(BF16)
    return high, (value - high.astype(F32)).astype(BF16)


def mul(a, b, dims):
    return lax.dot_general(a, b, dims, preferred_element_type=F32)


def mul3(a, b, dims):
    return mul(a[0], b[0], dims) + (mul(a[0], b[1], dims) + mul(a[1], b[0], dims))


def call(body, outs, args, scratch=()):
    vmem = pl.BlockSpec(memory_space=pltpu.VMEM)
    return pl.pallas_call(
        body,
        out_shape=outs,
        in_specs=[vmem] * len(args),
        out_specs=[vmem] * len(outs),
        scratch_shapes=list(scratch),
        cost_estimate=pl.CostEstimate(flops=0, bytes_accessed=0, transcendentals=0),
        compiler_params=pltpu.CompilerParams(vmem_limit_bytes=40 * 2**20),
    )(*args)


def shaped(shape, dtype=F32):
    return jax.ShapeDtypeStruct(shape, dtype)


def cent_body(mine_ref, theirs_ref, high_ref, low_ref, sq_ref):
    half = mine_ref.shape[0]
    for i, ref in enumerate((mine_ref, theirs_ref)):
        for at in range(0, half, 128):
            to = pl.ds(i * half + at, 128)
            value = ref[pl.ds(at, 128)]
            high_ref[to], low_ref[to] = halves(value)
            total = jnp.sum(value * value, axis=1, keepdims=True)
            sq_ref[:, to] = jnp.broadcast_to(total, (128, 128)).T[:8]


def split_cent(mine, theirs):
    half, width = mine.shape
    pair = [shaped((2 * half, width), BF16)] * 2
    return call(cent_body, pair + [shaped((8, 2 * half))], (mine, theirs))


def kernel_rows(high, low, row_sq, cent_refs, put):
    cent_high, cent_low, cent_sq = cent_refs
    scale = -4.0 / math.sqrt(cent_high.shape[1])
    for at in range(0, cent_high.shape[0], 256):
        to = pl.ds(at, 256)
        ch, cl = cent_high[to], cent_low[to]
        crossed = mul(high, ch, NT) + (mul(high, cl, NT) + mul(low, ch, NT) + mul(low, cl, NT))
        dist_sq = row_sq + cent_sq[0:1, to] - 2.0 * crossed
        put(to, halves(jnp.exp(jnp.sqrt(dist_sq + 1.0) * scale)))


def fill(refs, high_ref, low_ref, sq_ref):
    at = 0
    for ref in refs:
        to = pl.ds(at, ref.shape[0])
        value = ref[...]
        high_ref[to], low_ref[to] = halves(value)
        sq_ref[to] = jnp.broadcast_to(jnp.sum(value * value, axis=1, keepdims=True), (ref.shape[0], 128))
        at += ref.shape[0]


def own_body(own, c_high, c_low, c_sq, own_high, own_low, high, low, row_sq):
    fill((own,), high, low, row_sq)

    def put(to, pair):
        own_high[:, to], own_low[:, to] = pair

    kernel_rows(high[...], low[...], row_sq[:, 0:1], (c_high, c_low, c_sq), put)


def row_scratch(rows, width):
    return [pltpu.VMEM((rows, width), BF16)] * 2 + [pltpu.VMEM((rows, 128), F32)]


def own_kernels(own, cent):
    rows, width = own.shape
    wide = cent[0].shape[0]
    return call(
        own_body,
        [shaped((rows, wide), BF16)] * 2,
        (own, *cent),
        scratch=row_scratch(rows, width),
    )


def near_body(x, y, c_high, c_low, c_sq, own_high, own_low, near_high, near_low, high, low, row_sq):
    rows = x.shape[0]
    fill((x, y), high, low, row_sq)
    near_high[pl.ds(rows, rows)] = own_high[...]
    near_low[pl.ds(rows, rows)] = own_low[...]

    def put(to, pair):
        for ref, value in zip((near_high, near_low), pair):
            ref[pl.ds(0, rows), to] = value[:rows]
            ref[pl.ds(2 * rows, rows), to] = value[rows:]

    kernel_rows(high[...], low[...], row_sq[:, 0:1], (c_high, c_low, c_sq), put)


def near_kernels(x, y, cent, own):
    rows, width = x.shape
    wide = cent[0].shape[0]
    return call(
        near_body,
        [shaped((3 * rows, wide), BF16)] * 2,
        (x, y, *cent, *own),
        scratch=row_scratch(2 * rows, width),
    )


def share(w_refs, cols, k_refs, rows):
    half = w_refs[0].shape[1]
    total = None
    for i, ref in enumerate(w_refs):
        kept = pl.ds(i * half, half)
        part = mul3(halves(ref[cols]), (k_refs[0][rows, kept], k_refs[1][rows, kept]), NT)
        total = part if total is None else total + part
    return total


def stays(rows):
    return pl.ds(rows, 2 * rows), pl.ds(0, 2 * rows)


def goes(rows):
    return pl.ds(0, 2 * rows), pl.ds(rows, 2 * rows)


def keep_body(edges, rows, w0, w1, running, targets, near_high, near_low, *kept):
    for i, (a, b) in enumerate(edges):
        cols = pl.ds(a, b - a)
        value = share((w0, w1), cols, (near_high, near_low), stays(rows)[i % 2])
        own = slice(0, rows) if i % 2 == 0 else slice(rows, 2 * rows)
        other = slice(rows, 2 * rows) if i % 2 == 0 else slice(0, rows)
        kept[i][:, own] = value[:, own] + (running[cols] - targets[cols])
        kept[i][:, other] = value[:, other]


def keep_shares(edges, w0, w1, running, targets, near):
    rows = running.shape[1]
    outs = [shaped((b - a, 2 * rows)) for a, b in edges]
    return call(
        functools.partial(keep_body, edges, rows), outs, (w0, w1, running, targets, *near)
    )


def far_body(edges, block, c_high, c_low, c_sq, near_high, near_low, w0, w1, *rest):
    outs, (high, low, row_sq) = rest[:-3], rest[-3:]
    far_high, far_low, sent = outs[0], outs[1], outs[2:]
    rows = low.shape[0]
    fill((block,), high, low, row_sq)
    for far, near in ((far_high, near_high), (far_low, near_low)):
        far[pl.ds(0, rows)] = near[pl.ds(0, rows)]
        far[pl.ds(2 * rows, rows)] = near[pl.ds(2 * rows, rows)]

    def put(to, pair):
        far_high[pl.ds(rows, rows), to], far_low[pl.ds(rows, rows), to] = pair

    kernel_rows(high[...], low[...], row_sq[:, 0:1], (c_high, c_low, c_sq), put)
    for i, (a, b) in enumerate(edges):
        sent[i][...] = share((w0, w1), pl.ds(a, b - a), (far_high, far_low), goes(rows)[i % 2])


def far_kernels(edges, block, cent, near, w0, w1):
    rows, width = block.shape
    wide = cent[0].shape[0]
    outs = [shaped(near[0].shape, BF16)] * 2 + [shaped((b - a, 2 * rows)) for a, b in edges]
    out = call(
        functools.partial(far_body, edges),
        outs,
        (block, *cent, *near, w0, w1),
        scratch=row_scratch(rows, width),
    )
    return out[:2], out[2:]


def send_body(edges, rows, w0, w1, far_high, far_low, *sent):
    for i, (a, b) in enumerate(edges):
        sent[i][...] = share((w0, w1), pl.ds(a, b - a), (far_high, far_low), goes(rows)[i % 2])


def send_shares(edges, w0, w1, far):
    rows = far[0].shape[0] // 3
    outs = [shaped((b - a, 2 * rows)) for a, b in edges]
    return call(functools.partial(send_body, edges, rows), outs, (w0, w1, *far))


PARTS = 3


def blocks(size, count):
    step = -(-size // count // 8) * 8
    return [(at, min(size, at + step)) for at in range(0, size, step)]


def grad_body(factor, full_a, full_b, other_a, other_b, near_high, near_low, far_high, far_low, here, *gone):
    rows, half = full_a.shape[1] // 2, here.shape[1]
    at = 0
    for i, (full, other) in enumerate(((full_a, other_a), (full_b, other_b))):
        to = pl.ds(at, full.shape[0])
        at += full.shape[0]
        full_pair, other_pair = halves(full[...]), halves(other[...])
        stay, go = stays(rows)[i], goes(rows)[i]
        for away, cols in ((True, pl.ds(half, half)), (False, pl.ds(0, half))):
            value = factor * (
                mul3(full_pair, (near_high[stay, cols], near_low[stay, cols]), NN)
                + mul3(other_pair, (far_high[go, cols], far_low[go, cols]), NN)
            )
            if not away:
                here[to] = value
                continue
            start, end = at - full.shape[0], at
            for ref, (low, high) in zip(gone, blocks(here.shape[0], PARTS)):
                low_at, high_at = max(low, start), min(high, end)
                if low_at < high_at:
                    ref[pl.ds(low_at - low, high_at - low_at)] = value[low_at - start : high_at - start]


def grad_parts(factor, full, other, near, far):
    cols, half = full[0].shape[0] + full[1].shape[0], near[0].shape[1] // 2
    outs = [shaped((cols, half))] + [shaped((b - a, half)) for a, b in blocks(cols, PARTS)]
    out = call(functools.partial(grad_body, factor), outs, (*full, *other, *near, *far))
    return out[1:], out[0]


def pass_line(value, pairs):
    return lax.ppermute(value, "col", pairs)


BESIDE = [(0, 1), (1, 0), (2, 3), (3, 2)]
ACROSS = [(0, 3), (3, 0), (1, 2), (2, 1)]


def add_body(*refs):
    count = len(refs) // 3
    for i in range(count):
        refs[2 * count + i][...] = refs[i][...] + refs[count + i][...]


def add(many, more):
    return call(add_body, [shaped(a.shape) for a in many], (*many, *more))


def turn_body(*refs):
    for a, b, out in zip(refs[0:2], refs[2:4], refs[4:6]):
        rows = a.shape[1] // 2
        left, right = pl.ds(0, rows), pl.ds(rows, rows)
        out[:, left] = a[:, left] + b[:, right]
        out[:, right] = a[:, right] + b[:, left]


def turn(many, more):
    return call(turn_body, [shaped(a.shape) for a in many], (*many, *more))


def split_body(here, *refs):
    parts = blocks(here.shape[0], PARTS)
    gone, outs = refs[: len(parts)], refs[len(parts) :]
    count = len(outs) // 2
    pieces = blocks(here.shape[0], count)
    place = lax.axis_index("col")
    ends = (place == 0) | (place == 3)
    quarter = here.shape[1] // 2
    left, right = pl.ds(0, quarter), pl.ds(quarter, quarter)

    def put(kept, sent):
        for ref, (a, b) in zip(gone, parts):
            for i, (low, high) in enumerate(pieces):
                at, end = max(a, low), min(b, high)
                if at < end:
                    of, part, to = (pl.ds(at - n, end - at) for n in (0, a, low))
                    outs[i][to] = here[of, sent] + ref[part, sent]
                    outs[count + i][to] = here[of, kept] + ref[part, kept]

    pl.when(ends)(lambda: put(left, right))
    pl.when(~ends)(lambda: put(right, left))


def split(count, here, gone):
    rows, half = here.shape
    outs = [shaped((b - a, half // 2)) for a, b in blocks(rows, count)] * 2
    out = call(split_body, outs, (here, *gone))
    return out[: len(out) // 2], out[len(out) // 2 :]


def join_body(a, b, out):
    place = lax.axis_index("col")
    ends = (place == 0) | (place == 3)
    quarter = a.shape[1]
    left, right = pl.ds(0, quarter), pl.ds(quarter, quarter)

    def put(mine, other):
        out[:, mine] = a[...]
        out[:, other] = b[...]

    pl.when(ends)(lambda: put(left, right))
    pl.when(~ends)(lambda: put(right, left))


def join(a, b):
    return call(join_body, [shaped((a.shape[0], 2 * a.shape[1]))], (a, b))[0]


def cut(out):
    edges, at = [], 0
    for part in ROUNDS + (1.0,):
        left = out - at
        both = left if part == 1.0 else min(left, round(out * part / 16) * 16)
        first = -(-both // 16) * 8
        edges += [(at, at + first), (at + first, at + both)]
        at += both
    return edges


def hop(value, second):
    pairs = []
    for chip in range(4):
        for core in range(2):
            flip = 1 if core == second else 2
            pairs.append((chip * 2 + core, (chip ^ flip) * 2 + core))
    return lax.ppermute(value, ("chip", "core"), pairs)


def square(batch, running_t, targets_t, centers, weights_t, factor):
    rows, out = batch.shape[0], weights_t.shape[0]
    edges = cut(out)
    rounds = len(edges) // 2
    line = Line()
    block_x = hop(batch, 0)
    block_y = hop(batch, 1)
    cent_theirs = swap(centers, "core")
    w0, w1 = weights_t, swap(weights_t, "core")
    cent = line(split_cent, centers, cent_theirs)
    own = line(own_kernels, batch, cent)
    block = hop(block_x, 1)
    near = line(near_kernels, block_x, block_y, cent, own)
    far, sent = line(lambda *a: far_kernels(edges[:2], *a), block, cent, near, w0, w1)

    def both(pair, step):
        return [hop(pair[i], (i + step) % 2) for i in (0, 1)]

    coming, crossing = [None] * rounds, [None] * rounds
    partial, full, other, gone, here = ([None] * rounds for _ in range(5))
    beside, mine, across, total, back, whole = [], [], [], [], [], []

    def do_partial(r):
        partial[r] = line(add, kept[2 * r : 2 * r + 2], coming[r])
        crossing[r] = both(partial[r], 1)

    def do_full(r):
        full[r] = line(turn, partial[r], crossing[r])
        other[r] = both(full[r], 0)

    def do_grad(r):
        gone[r], here[r] = line(lambda *a: grad_parts(factor, *a), full[r], other[r], near, far)
        gone[r] = [swap(part, "core") for part in gone[r]]

    def do_owned(r):
        sends, keeps = line(lambda *a: split(LINE_PIECES[r], *a), here[r], gone[r])
        mine.extend(keeps)
        beside.extend(pass_line(value, BESIDE) for value in sends)

    def do_mine(i):
        (mine[i],) = line(add, [mine[i]], [beside[i]])
        across.append(pass_line(mine[i], ACROSS))

    def do_total(i):
        (value,) = line(add, [mine[i]], [across[i]])
        total.append(value)
        back.append(pass_line(value, BESIDE))

    def do_whole(i):
        whole.append(line(join, total[i], back[i]))

    sent = list(sent) + list(line(lambda *a: send_shares(edges[2:], *a), w0, w1, far))
    coming = [both(sent[2 * r : 2 * r + 2], 0) for r in range(rounds)]
    kept = line(lambda *a: keep_shares(edges, *a), w0, w1, running_t, targets_t, near)
    steps = dict(P=do_partial, F=do_full, G=do_grad, O=do_owned, M=do_mine, T=do_total, D=do_whole)
    for step in " ".join(STEPS).split():
        steps[step[0]](int(step[1]))

    gradient = jnp.concatenate(whole)
    mine_rows = (slice(0, rows), slice(rows, None))
    residual = jnp.concatenate([f[i][:, mine_rows[i]] for f in full for i in (0, 1)])
    return gradient, residual


def any_plane(batch, running_t, targets_t, centers, weights_t, factor):
    def dot(a, b, dims, precision):
        return lax.dot_general(a, b, dims, precision=precision, preferred_element_type=F32)

    rows_here, chips = batch.shape[0], lax.axis_size("chip")
    half, out = centers.shape[0], weights_t.shape[0]
    cent = jnp.concatenate([centers, swap(centers, "core")], axis=0)
    weight = jnp.concatenate([weights_t, swap(weights_t, "core")], axis=1)
    rows = lax.all_gather(batch, "chip", axis=0, tiled=True)
    row_sq = jnp.sum(rows * rows, axis=1, keepdims=True)
    dist_sq = row_sq + jnp.sum(cent * cent, axis=1)[None, :] - 2.0 * dot(rows, cent, NT, HIGHEST)
    kernel = jnp.exp(-jnp.sqrt(dist_sq + 1.0) / (math.sqrt(rows.shape[1]) / 4.0))
    shares = dot(weight, kernel, NT, HIGH).reshape(out, chips, rows_here).transpose(1, 0, 2)
    residual = running_t - targets_t + lax.psum_scatter(shares, "chip", scatter_dimension=0, tiled=False)
    moved = lax.all_gather(residual, "chip", axis=0, tiled=False)
    moved = moved.transpose(1, 0, 2).reshape(out, chips * rows_here)
    gradient = dot(moved, kernel, NN, HIGH) * factor
    owned = gradient[:, :half] + swap(gradient[:, half:], "core")
    return lax.psum(owned, "col"), residual


def per_device(batch, running, targets, centers, weights):
    chips, depth = lax.axis_size("chip"), lax.axis_size("col")
    factor = 1.0 / math.sqrt(batch.shape[0] * chips * 2 * depth)
    plane = square if (chips, depth) == (4, 4) else any_plane
    gradient, residual = plane(batch, running.T, targets.T, centers, weights.T, factor)
    return gradient.T, residual.T


def solution(mesh):
    owners, depth = mesh.shape["row"], mesh.shape["col"]
    split = Mesh(mesh.devices.reshape(owners // 2, 2, depth), ("chip", "core", "col"))
    everywhere = P(("chip", "core", "col"), None)
    owned = P(("chip", "core"), None)
    return jax.shard_map(
        per_device,
        mesh=split,
        in_specs=(everywhere, everywhere, everywhere, owned, owned),
        out_specs=(owned, everywhere),
        check_vma=False,
    )
```

```python
import functools
import math

import jax
import jax.numpy as jnp
from jax import lax
from jax.experimental import pallas as pl
from jax.experimental.pallas import tpu as pltpu
from jax.sharding import Mesh, PartitionSpec as P

HIGHEST = lax.Precision.HIGHEST
HIGH = lax.Precision.HIGH
ROUNDS = (0.48,)
STEPS = ("P0 P1 F0 F1", "G0 O0 G1 O1", "M0 M1 T0 D0", "T1 D1")
LINE_PIECES = (1,1,)
BF16, F32 = jnp.bfloat16, jnp.float32
NT = (((1,), (1,)), ((), ()))
NN = (((1,), (0,)), ((), ()))


def swap(value, axis, flip=1):
    size = lax.axis_size(axis)
    return lax.ppermute(value, axis, [(i, i ^ flip) for i in range(size)])


class Line:
    def __init__(self):
        self.last = None

    def hold(self, args):
        if self.last is None:
            return args
        return lax.optimization_barrier((args, self.last))[0]

    def __call__(self, step, *args):
        out = step(*self.hold(args))
        self.last = jax.tree.leaves(out)[0]
        return out


def halves(value):
    high = value.astype(BF16)
    return high, (value - high.astype(F32)).astype(BF16)


def mul(a, b, dims):
    return lax.dot_general(a, b, dims, preferred_element_type=F32)


def mul3(a, b, dims):
    return mul(a[0], b[0], dims) + (mul(a[0], b[1], dims) + mul(a[1], b[0], dims))


def call(body, outs, args, scratch=()):
    vmem = pl.BlockSpec(memory_space=pltpu.VMEM)
    return pl.pallas_call(
        body,
        out_shape=outs,
        in_specs=[vmem] * len(args),
        out_specs=[vmem] * len(outs),
        scratch_shapes=list(scratch),
        cost_estimate=pl.CostEstimate(flops=0, bytes_accessed=0, transcendentals=0),
        compiler_params=pltpu.CompilerParams(vmem_limit_bytes=40 * 2**20),
    )(*args)


def shaped(shape, dtype=F32):
    return jax.ShapeDtypeStruct(shape, dtype)


def cent_body(mine_ref, theirs_ref, high_ref, low_ref, sq_ref):
    half = mine_ref.shape[0]
    for i, ref in enumerate((mine_ref, theirs_ref)):
        for at in range(0, half, 128):
            to = pl.ds(i * half + at, 128)
            value = ref[pl.ds(at, 128)]
            high_ref[to], low_ref[to] = halves(value)
            total = jnp.sum(value * value, axis=1, keepdims=True)
            sq_ref[:, to] = jnp.broadcast_to(total, (128, 128)).T[:8]


def split_cent(mine, theirs):
    half, width = mine.shape
    pair = [shaped((2 * half, width), BF16)] * 2
    return call(cent_body, pair + [shaped((8, 2 * half))], (mine, theirs))


def kernel_rows(high, low, row_sq, cent_refs, put):
    cent_high, cent_low, cent_sq = cent_refs
    scale = -4.0 / math.sqrt(cent_high.shape[1])
    for at in range(0, cent_high.shape[0], 256):
        to = pl.ds(at, 256)
        ch, cl = cent_high[to], cent_low[to]
        crossed = mul(high, ch, NT) + (mul(high, cl, NT) + mul(low, ch, NT) + mul(low, cl, NT))
        dist_sq = row_sq + cent_sq[0:1, to] - 2.0 * crossed
        put(to, halves(jnp.exp(jnp.sqrt(dist_sq + 1.0) * scale)))


def fill(refs, high_ref, low_ref, sq_ref):
    at = 0
    for ref in refs:
        to = pl.ds(at, ref.shape[0])
        value = ref[...]
        high_ref[to], low_ref[to] = halves(value)
        sq_ref[to] = jnp.broadcast_to(jnp.sum(value * value, axis=1, keepdims=True), (ref.shape[0], 128))
        at += ref.shape[0]


def own_body(own, c_high, c_low, c_sq, own_high, own_low, high, low, row_sq):
    fill((own,), high, low, row_sq)

    def put(to, pair):
        own_high[:, to], own_low[:, to] = pair

    kernel_rows(high[...], low[...], row_sq[:, 0:1], (c_high, c_low, c_sq), put)


def row_scratch(rows, width):
    return [pltpu.VMEM((rows, width), BF16)] * 2 + [pltpu.VMEM((rows, 128), F32)]


def own_kernels(own, cent):
    rows, width = own.shape
    wide = cent[0].shape[0]
    return call(
        own_body,
        [shaped((rows, wide), BF16)] * 2,
        (own, *cent),
        scratch=row_scratch(rows, width),
    )


def near_body(x, y, c_high, c_low, c_sq, own_high, own_low, near_high, near_low, high, low, row_sq):
    rows = x.shape[0]
    fill((x, y), high, low, row_sq)
    near_high[pl.ds(rows, rows)] = own_high[...]
    near_low[pl.ds(rows, rows)] = own_low[...]

    def put(to, pair):
        for ref, value in zip((near_high, near_low), pair):
            ref[pl.ds(0, rows), to] = value[:rows]
            ref[pl.ds(2 * rows, rows), to] = value[rows:]

    kernel_rows(high[...], low[...], row_sq[:, 0:1], (c_high, c_low, c_sq), put)


def near_kernels(x, y, cent, own):
    rows, width = x.shape
    wide = cent[0].shape[0]
    return call(
        near_body,
        [shaped((3 * rows, wide), BF16)] * 2,
        (x, y, *cent, *own),
        scratch=row_scratch(2 * rows, width),
    )


def share(w_refs, cols, k_refs, rows):
    half = w_refs[0].shape[1]
    total = None
    for i, ref in enumerate(w_refs):
        kept = pl.ds(i * half, half)
        part = mul3(halves(ref[cols]), (k_refs[0][rows, kept], k_refs[1][rows, kept]), NT)
        total = part if total is None else total + part
    return total


def stays(rows):
    return pl.ds(rows, 2 * rows), pl.ds(0, 2 * rows)


def goes(rows):
    return pl.ds(0, 2 * rows), pl.ds(rows, 2 * rows)


def keep_body(edges, rows, w0, w1, running, targets, near_high, near_low, *kept):
    for i, (a, b) in enumerate(edges):
        cols = pl.ds(a, b - a)
        value = share((w0, w1), cols, (near_high, near_low), stays(rows)[i % 2])
        own = slice(0, rows) if i % 2 == 0 else slice(rows, 2 * rows)
        other = slice(rows, 2 * rows) if i % 2 == 0 else slice(0, rows)
        kept[i][:, own] = value[:, own] + (running[cols] - targets[cols])
        kept[i][:, other] = value[:, other]


def keep_shares(edges, w0, w1, running, targets, near):
    rows = running.shape[1]
    outs = [shaped((b - a, 2 * rows)) for a, b in edges]
    return call(
        functools.partial(keep_body, edges, rows), outs, (w0, w1, running, targets, *near)
    )


def far_body(edges, block, c_high, c_low, c_sq, near_high, near_low, w0, w1, *rest):
    outs, (high, low, row_sq) = rest[:-3], rest[-3:]
    far_high, far_low, sent = outs[0], outs[1], outs[2:]
    rows = low.shape[0]
    fill((block,), high, low, row_sq)
    for far, near in ((far_high, near_high), (far_low, near_low)):
        far[pl.ds(0, rows)] = near[pl.ds(0, rows)]
        far[pl.ds(2 * rows, rows)] = near[pl.ds(2 * rows, rows)]

    def put(to, pair):
        far_high[pl.ds(rows, rows), to], far_low[pl.ds(rows, rows), to] = pair

    kernel_rows(high[...], low[...], row_sq[:, 0:1], (c_high, c_low, c_sq), put)
    for i, (a, b) in enumerate(edges):
        sent[i][...] = share((w0, w1), pl.ds(a, b - a), (far_high, far_low), goes(rows)[i % 2])


def far_kernels(edges, block, cent, near, w0, w1):
    rows, width = block.shape
    wide = cent[0].shape[0]
    outs = [shaped(near[0].shape, BF16)] * 2 + [shaped((b - a, 2 * rows)) for a, b in edges]
    out = call(
        functools.partial(far_body, edges),
        outs,
        (block, *cent, *near, w0, w1),
        scratch=row_scratch(rows, width),
    )
    return out[:2], out[2:]


def send_body(edges, rows, w0, w1, far_high, far_low, *sent):
    for i, (a, b) in enumerate(edges):
        sent[i][...] = share((w0, w1), pl.ds(a, b - a), (far_high, far_low), goes(rows)[i % 2])


def send_shares(edges, w0, w1, far):
    rows = far[0].shape[0] // 3
    outs = [shaped((b - a, 2 * rows)) for a, b in edges]
    return call(functools.partial(send_body, edges, rows), outs, (w0, w1, *far))


PARTS = 3


def blocks(size, count):
    step = -(-size // count // 8) * 8
    return [(at, min(size, at + step)) for at in range(0, size, step)]


def grad_body(factor, away, full_a, full_b, other_a, other_b, near_high, near_low, far_high, far_low, *outs):
    rows, half = full_a.shape[1] // 2, outs[0].shape[1]
    cols = pl.ds(half if away else 0, half)
    parts = blocks(full_a.shape[0] + full_b.shape[0], len(outs))
    start = 0
    for i, (full, other) in enumerate(((full_a, other_a), (full_b, other_b))):
        end = start + full.shape[0]
        stay, go = stays(rows)[i], goes(rows)[i]
        value = factor * (
            mul3(halves(full[...]), (near_high[stay, cols], near_low[stay, cols]), NN)
            + mul3(halves(other[...]), (far_high[go, cols], far_low[go, cols]), NN)
        )
        for ref, (low, high) in zip(outs, parts):
            at, to = max(low, start), min(high, end)
            if at < to:
                ref[pl.ds(at - low, to - at)] = value[at - start : to - start]
        start = end


def grad_parts(factor, away, full, other, near, far):
    cols, half = full[0].shape[0] + full[1].shape[0], near[0].shape[1] // 2
    outs = [shaped((b - a, half)) for a, b in blocks(cols, PARTS if away else 1)]
    return call(functools.partial(grad_body, factor, away), outs, (*full, *other, *near, *far))


def pass_line(value, pairs):
    return lax.ppermute(value, "col", pairs)


BESIDE = [(0, 1), (1, 0), (2, 3), (3, 2)]
ACROSS = [(0, 3), (3, 0), (1, 2), (2, 1)]


def add_body(*refs):
    count = len(refs) // 3
    for i in range(count):
        refs[2 * count + i][...] = refs[i][...] + refs[count + i][...]


def add(many, more):
    return call(add_body, [shaped(a.shape) for a in many], (*many, *more))


def turn_body(*refs):
    for a, b, out in zip(refs[0:2], refs[2:4], refs[4:6]):
        rows = a.shape[1] // 2
        left, right = pl.ds(0, rows), pl.ds(rows, rows)
        out[:, left] = a[:, left] + b[:, right]
        out[:, right] = a[:, right] + b[:, left]


def turn(many, more):
    return call(turn_body, [shaped(a.shape) for a in many], (*many, *more))


def split_body(here, *refs):
    parts = blocks(here.shape[0], PARTS)
    gone, outs = refs[: len(parts)], refs[len(parts) :]
    count = len(outs) // 2
    pieces = blocks(here.shape[0], count)
    place = lax.axis_index("col")
    ends = (place == 0) | (place == 3)
    quarter = here.shape[1] // 2
    left, right = pl.ds(0, quarter), pl.ds(quarter, quarter)

    def put(kept, sent):
        for ref, (a, b) in zip(gone, parts):
            for i, (low, high) in enumerate(pieces):
                at, end = max(a, low), min(b, high)
                if at < end:
                    of, part, to = (pl.ds(at - n, end - at) for n in (0, a, low))
                    outs[i][to] = here[of, sent] + ref[part, sent]
                    outs[count + i][to] = here[of, kept] + ref[part, kept]

    pl.when(ends)(lambda: put(left, right))
    pl.when(~ends)(lambda: put(right, left))


def split(count, here, gone):
    rows, half = here.shape
    outs = [shaped((b - a, half // 2)) for a, b in blocks(rows, count)] * 2
    out = call(split_body, outs, (here, *gone))
    return out[: len(out) // 2], out[len(out) // 2 :]


def join_body(a, b, out):
    place = lax.axis_index("col")
    ends = (place == 0) | (place == 3)
    quarter = a.shape[1]
    left, right = pl.ds(0, quarter), pl.ds(quarter, quarter)

    def put(mine, other):
        out[:, mine] = a[...]
        out[:, other] = b[...]

    pl.when(ends)(lambda: put(left, right))
    pl.when(~ends)(lambda: put(right, left))


def join(a, b):
    return call(join_body, [shaped((a.shape[0], 2 * a.shape[1]))], (a, b))[0]


def cut(out):
    edges, at = [], 0
    for part in ROUNDS + (1.0,):
        left = out - at
        both = left if part == 1.0 else min(left, round(out * part / 16) * 16)
        first = -(-both // 16) * 8
        edges += [(at, at + first), (at + first, at + both)]
        at += both
    return edges


def hop(value, second):
    pairs = []
    for chip in range(4):
        for core in range(2):
            flip = 1 if core == second else 2
            pairs.append((chip * 2 + core, (chip ^ flip) * 2 + core))
    return lax.ppermute(value, ("chip", "core"), pairs)


def square(batch, running_t, targets_t, centers, weights_t, factor):
    rows, out = batch.shape[0], weights_t.shape[0]
    edges = cut(out)
    rounds = len(edges) // 2
    line = Line()
    block_x = hop(batch, 0)
    block_y = hop(batch, 1)
    cent_theirs = swap(centers, "core")
    w0, w1 = weights_t, swap(weights_t, "core")
    cent = line(split_cent, centers, cent_theirs)
    own = line(own_kernels, batch, cent)
    block = hop(block_x, 1)
    near = line(near_kernels, block_x, block_y, cent, own)
    far, sent = line(lambda *a: far_kernels(edges[:2], *a), block, cent, near, w0, w1)

    def both(pair, step):
        return [hop(pair[i], (i + step) % 2) for i in (0, 1)]

    coming, crossing = [None] * rounds, [None] * rounds
    partial, full, other, gone, here = ([None] * rounds for _ in range(5))
    beside, mine, across, total, back, whole = [], [], [], [], [], []

    def do_partial(r):
        partial[r] = line(add, kept[2 * r : 2 * r + 2], coming[r])
        crossing[r] = both(partial[r], 1)

    def do_full(r):
        full[r] = line(turn, partial[r], crossing[r])
        other[r] = both(full[r], 0)

    def do_grad(r):
        gone[r] = line(lambda *a: grad_parts(factor, True, *a), full[r], other[r], near, far)
        gone[r] = [swap(part, "core") for part in gone[r]]
        (here[r],) = line(lambda *a: grad_parts(factor, False, *a), full[r], other[r], near, far)

    def do_owned(r):
        sends, keeps = line(lambda *a: split(LINE_PIECES[r], *a), here[r], gone[r])
        mine.extend(keeps)
        beside.extend(pass_line(value, BESIDE) for value in sends)

    def do_mine(i):
        (mine[i],) = line(add, [mine[i]], [beside[i]])
        across.append(pass_line(mine[i], ACROSS))

    def do_total(i):
        (value,) = line(add, [mine[i]], [across[i]])
        total.append(value)
        back.append(pass_line(value, BESIDE))

    def do_whole(i):
        whole.append(line(join, total[i], back[i]))

    sent = list(sent) + list(line(lambda *a: send_shares(edges[2:], *a), w0, w1, far))
    coming = [both(sent[2 * r : 2 * r + 2], 0) for r in range(rounds)]
    kept = line(lambda *a: keep_shares(edges, *a), w0, w1, running_t, targets_t, near)
    steps = dict(P=do_partial, F=do_full, G=do_grad, O=do_owned, M=do_mine, T=do_total, D=do_whole)
    for step in " ".join(STEPS).split():
        steps[step[0]](int(step[1]))

    gradient = jnp.concatenate(whole)
    mine_rows = (slice(0, rows), slice(rows, None))
    residual = jnp.concatenate([f[i][:, mine_rows[i]] for f in full for i in (0, 1)])
    return gradient, residual


def any_plane(batch, running_t, targets_t, centers, weights_t, factor):
    def dot(a, b, dims, precision):
        return lax.dot_general(a, b, dims, precision=precision, preferred_element_type=F32)

    rows_here, chips = batch.shape[0], lax.axis_size("chip")
    half, out = centers.shape[0], weights_t.shape[0]
    cent = jnp.concatenate([centers, swap(centers, "core")], axis=0)
    weight = jnp.concatenate([weights_t, swap(weights_t, "core")], axis=1)
    rows = lax.all_gather(batch, "chip", axis=0, tiled=True)
    row_sq = jnp.sum(rows * rows, axis=1, keepdims=True)
    dist_sq = row_sq + jnp.sum(cent * cent, axis=1)[None, :] - 2.0 * dot(rows, cent, NT, HIGHEST)
    kernel = jnp.exp(-jnp.sqrt(dist_sq + 1.0) / (math.sqrt(rows.shape[1]) / 4.0))
    shares = dot(weight, kernel, NT, HIGH).reshape(out, chips, rows_here).transpose(1, 0, 2)
    residual = running_t - targets_t + lax.psum_scatter(shares, "chip", scatter_dimension=0, tiled=False)
    moved = lax.all_gather(residual, "chip", axis=0, tiled=False)
    moved = moved.transpose(1, 0, 2).reshape(out, chips * rows_here)
    gradient = dot(moved, kernel, NN, HIGH) * factor
    owned = gradient[:, :half] + swap(gradient[:, half:], "core")
    return lax.psum(owned, "col"), residual


def per_device(batch, running, targets, centers, weights):
    chips, depth = lax.axis_size("chip"), lax.axis_size("col")
    factor = 1.0 / math.sqrt(batch.shape[0] * chips * 2 * depth)
    plane = square if (chips, depth) == (4, 4) else any_plane
    gradient, residual = plane(batch, running.T, targets.T, centers, weights.T, factor)
    return gradient.T, residual.T


def solution(mesh):
    owners, depth = mesh.shape["row"], mesh.shape["col"]
    split = Mesh(mesh.devices.reshape(owners // 2, 2, depth), ("chip", "core", "col"))
    everywhere = P(("chip", "core", "col"), None)
    owned = P(("chip", "core"), None)
    return jax.shard_map(
        per_device,
        mesh=split,
        in_specs=(everywhere, everywhere, everywhere, owned, owned),
        out_specs=(owned, everywhere),
        check_vma=False,
    )
```
